128 devices in a mesh: seq: 8 (over x, core), head: 16 (over z, y).
Axes of the slice: x: 4, y: 4, z: 4, core: 2. Of those that a mesh axis runs over, the one named last changes fastest.
Arguments:
- hidden: bfloat16 [4096, 3584], P('seq', 'head'), may hold values from -6 to 6
- embedding: bfloat16 [4096, 3584], P('seq', 'head'), may hold values from -6 to 6
- input_gain: float32 [3584], replicated, may hold values from 0.1 to 1.9
- w_input: bfloat16 [3584, 8192], P(None, 'head'), may hold values from -0.09375 to 0.09375
- w_groups: bfloat16 [3584, 256], replicated, may hold values from -0.09375 to 0.09375
- w_step: bfloat16 [3584, 64], P(None, 'head'), may hold values from -0.09375 to 0.09375
- step_bias: float32 [64], P('head'), may hold values from -1 to 1
- decay_rate: float32 [64], P('head'), may hold values from 0.000390625 to 0.0390625
- skip_gain: float32 [64], P('head'), may hold values from -16 to 16
- conv_weight: float32 [4, 4096], P(None, 'head'), may hold values from -3 to 3
- mix_gain: float32 [4096], P('head'), may hold values from 0.1 to 1.9
- w_output: bfloat16 [4096, 3584], P('head'), may hold values from -0.09375 to 0.09375
- state_store: float32 [16, 64, 4096], P('seq', 'head'), may hold values from -6 to 6
- conv_store: bfloat16 [16, 3, 4096], P('seq', None, 'head'), may hold values from -6 to 6
- state_slot: int32 [8], replicated, may hold values from 0 to 15, as said below
- prefix_len: int32 [8], replicated, may hold values from 1 to 8192, as said below
- block_table: int32 [8, 64], replicated, may hold values from 0 to 159, as said below
- shared_gain: float32 [7168], replicated, may hold values from 0.1 to 1.9
- w_attend: bfloat16 [7168, 10752], P(None, 'head'), may hold values from -0.06496264 to 0.06496264
- cache_pool: bfloat16 [160, 2, 128, 3584], P('seq', None, None, 'head'), may hold values from -8 to 8
- w_merge: bfloat16 [3584, 3584], P('head'), may hold values from -0.09375 to 0.09375
Outputs:
- layer_output: float32 [4096, 3584], P('seq', 'head')
- final_state: float32 [8, 64, 4096], P('seq', 'head')
The draws below stay inside these ranges and needn't reach their ends.
Inputs may be any that keep to these rules, and one draw needn't show every extreme that they name: `prefix_len`: one request has a prefix of exactly 8192 tokens; every other has at most 1664. block_table[r, j] is the first index of cache_pool holding prefix positions j * 128 to (j + 1) * 128 - 1 of request r; it is read only where j * 128 < prefix_len[r], and such entries are distinct over all requests. `state_slot`: different requests have different rows.
All inputs are finite; a program needn't handle non-finite values.
Results may differ from the reference program's by a relative error of at most 0.014.
Values may be sent and summed in bfloat16 or wider, within the bound.
A program may use at most 192 MiB of HBM per device.

```python
import math
import jax
import jax.numpy as jnp
from jax import lax

D = 3584
MH = 64
P_SIZE = 64
NS = 64
G = 2
CONV = 4
AH = 16
HD = 224
STRETCH = 512
BLOCK = 128
MAXB = 64
SLOTS = 2
REQS = 8
TOKENS = 4096
TOTALB = 160
OTHERB = 13
STATE_SLOTS = 16


def prefix_lengths(key):
    key_long, key_rest = jax.random.split(jax.random.fold_in(key, 11))
    longest = jax.random.randint(key_long, (), 0, REQS)
    others = jax.random.randint(key_rest, (REQS,), 1, OTHERB * BLOCK + 1)
    return jnp.where(jnp.arange(REQS) == longest, MAXB * BLOCK, others).astype(jnp.int32)


def draw_prefix_len(key, part):
    return prefix_lengths(key)


def draw_block_table(key, part):
    lengths = prefix_lengths(key)
    key = jax.random.fold_in(key, 3)
    counts = (lengths + BLOCK - 1) // BLOCK
    starts = jnp.cumsum(counts) - counts
    shuffled = jax.random.permutation(key, TOTALB)
    places = (starts[:, None] + jnp.arange(MAXB)[None, :]) % TOTALB
    return shuffled[places].astype(jnp.int32)


def draw_state_slot(key, part):
    key = jax.random.fold_in(key, 5)
    key_order, key_bits = jax.random.split(key)
    order = jax.random.permutation(key_order, REQS)
    offsets = jax.random.randint(key_bits, (REQS,), 0, SLOTS)
    offsets = jnp.where(order == 0, 0, jnp.where(order == REQS - 1, SLOTS - 1, offsets))
    return (order * SLOTS + offsets).astype(jnp.int32)


def draw_skip_gain(key, part):
    key = jax.random.fold_in(key, 17)
    key_size, key_sign = jax.random.split(key)
    signs = jnp.where(jax.random.bernoulli(key_sign, 0.5, (MH,)), 1.0, -1.0)
    magnitude = jnp.exp(jax.random.uniform(key_size, (MH,), jnp.float32, math.log(0.5), math.log(16.0)))
    return (signs * magnitude).astype(jnp.float32)


def draw_w_attend(key, part):
    key = jax.random.fold_in(key, 13)
    key_main = jax.random.fold_in(key, 0)
    fan_scale = (2 * D) ** (-0.5)
    entries = jnp.clip(jax.random.normal(key_main, (2 * D, AH, 3, HD), jnp.float32), -5.5, 5.5) * fan_scale
    return entries.reshape(2 * D, AH * 3 * HD).astype(jnp.bfloat16)


def draw_cache_pool(key, part):
    key = jax.random.fold_in(key, 7)
    key_main = jax.random.fold_in(key, 0)
    entries = jnp.clip(jax.random.normal(key_main, (TOTALB, 2, BLOCK, AH, HD), jnp.float32), -4.0, 4.0)
    return entries.reshape(TOTALB, 2, BLOCK, AH * HD).astype(jnp.bfloat16)


def level_of(rng, dims, shards, least, largest):
    level, own = 1.0, jax.random.fold_in(rng, 6)
    for position, shards_of in shards:
        draws = jnp.exp(jax.random.uniform(jax.random.fold_in(own, position), (shards_of,), jnp.float32, least / len(shards), largest / len(shards)))
        level = level * jnp.repeat(draws, dims[position] // shards_of).reshape([-1 if axis == position else 1 for axis in range(len(dims))])
    return level


def gaussian(rng, extent, scale, limit, cuts=(), dtype=jnp.bfloat16):
    gain = level_of(rng, extent, cuts, -0.22, 0.18) if cuts else 1.0
    array = jax.random.normal(rng, extent, jnp.float32) * scale * gain
    return jnp.minimum(jnp.maximum(array, -limit), limit).astype(dtype)


def setup_inputs(seed: int = 0) -> dict:
    splits = jax.random.split(jax.random.key(seed), 22)
    hidden = gaussian(splits[0], (TOKENS, D), 1.0, 6.0, ((0, 8), (1, 16)))
    embedding = gaussian(splits[1], (TOKENS, D), 1.0, 6.0, ((0, 8), (1, 16)))
    input_gain = jnp.clip(1.0 + 0.18 * jax.random.normal(splits[2], (D,), jnp.float32), 0.1, 1.9)
    w_input = gaussian(splits[3], (D, MH * 2 * P_SIZE), D ** -0.5, 0.09375, ((1, 16),))
    w_groups = gaussian(splits[4], (D, 2 * G * NS), D ** -0.5, 0.09375)
    w_step = gaussian(splits[5], (D, MH), D ** -0.5, 0.09375, ((1, 16),))
    step_bias = jnp.clip(jax.random.uniform(splits[6], (MH,), jnp.float32, -1.0, 1.0) * level_of(splits[6], (MH,), ((0, 16),), -0.4, 0.0), -1.0, 1.0)
    decay_rate = jnp.clip(jnp.exp(math.log(0.0390625) - 4.6051702 * jax.random.uniform(splits[7], (MH,), jnp.float32) ** level_of(splits[7], (MH,), ((0, 16),), -0.2, 0.2)), 0.000390625, 0.0390625)
    skip_gain = draw_skip_gain(jax.random.fold_in(splits[21], 71), 0)
    conv_weight = gaussian(splits[9], (CONV, MH * P_SIZE), CONV ** -0.5, 3.0, ((1, 16),), jnp.float32)
    mix_gain = jnp.clip(1.0 + 0.18 * jax.random.normal(splits[10], (MH * P_SIZE,), jnp.float32), 0.1, 1.9)
    w_output = gaussian(splits[11], (MH * P_SIZE, D), (MH * P_SIZE) ** -0.5, 0.09375, ((0, 16),))
    state_store = gaussian(splits[12], (STATE_SLOTS, MH, P_SIZE * NS), 1.0, 6.0, ((0, 8), (1, 16)), jnp.float32)
    conv_store = gaussian(splits[13], (STATE_SLOTS, CONV - 1, MH * P_SIZE), 1.0, 6.0, ((0, 8), (2, 16)))
    state_slot = draw_state_slot(jax.random.fold_in(splits[21], 71), 0)
    prefix_len = draw_prefix_len(jax.random.fold_in(splits[21], 71), 0)
    block_table = draw_block_table(jax.random.fold_in(splits[21], 71), 0)
    shared_gain = jnp.clip(1.0 + 0.18 * jax.random.normal(splits[17], (2 * D,), jnp.float32), 0.1, 1.9)
    w_attend = draw_w_attend(jax.random.fold_in(splits[21], 71), 0)
    cache_pool = draw_cache_pool(jax.random.fold_in(splits[21], 71), 0)
    w_merge = gaussian(splits[20], (AH * HD, D), (AH * HD) ** -0.5, 0.09375, ((0, 16),))
    return dict(hidden=hidden, embedding=embedding, input_gain=input_gain, w_input=w_input, w_groups=w_groups, w_step=w_step, step_bias=step_bias, decay_rate=decay_rate, skip_gain=skip_gain, conv_weight=conv_weight, mix_gain=mix_gain, w_output=w_output, state_store=state_store, conv_store=conv_store, state_slot=state_slot, prefix_len=prefix_len, block_table=block_table, shared_gain=shared_gain, w_attend=w_attend, cache_pool=cache_pool, w_merge=w_merge)


epsilon = 1e-05
masked = -1e+30
highest = lax.Precision.HIGHEST

def norm_rows(matrix, norm_gain):
    matrix = matrix.astype(jnp.float32)
    return matrix * lax.rsqrt(lax.optimization_barrier(jnp.mean(matrix * matrix, axis=-1, keepdims=True)) + epsilon) * norm_gain

def state_block(activated, step_sizes, cumulative, b_proj, c_proj, init_state, skip_gain):
    length = activated.shape[0]
    positions = jnp.arange(length)
    causal = (positions[:, None] >= positions[None, :])[None]
    cums_heads = cumulative.T
    gaps = cums_heads[:, :, None] - cums_heads[:, None, :]
    decays = jnp.where(causal, jnp.exp(jnp.where(causal, gaps, 0.0)), 0.0)
    product = jnp.einsum('tn,sn->ts', c_proj, b_proj, precision=highest)
    weighted = decays * product[None] * step_sizes.T[:, None, :]
    within = jnp.einsum('hts,shp->thp', weighted, activated, precision=highest)
    carried = jnp.einsum('tn,hpn->thp', c_proj, init_state, precision=highest) * jnp.exp(cumulative)[:, :, None]
    output = within + carried + skip_gain[None, :, None] * activated
    to_end = jnp.exp(cumulative[-1][None, :] - cumulative) * step_sizes
    final_state = jnp.exp(cumulative[-1])[:, None, None] * init_state + jnp.einsum('shp,sn->hpn', activated * to_end[:, :, None], b_proj, precision=highest)
    return (output, final_state)

def reference(hidden, embedding, input_gain, w_input, w_groups, w_step, step_bias, decay_rate, skip_gain, conv_weight, mix_gain, w_output, state_store, conv_store, state_slot, prefix_len, block_table, shared_gain, w_attend, cache_pool, w_merge):
    group_heads = MH // G
    scale_factor = HD ** (-0.5)
    positions = jnp.arange(STRETCH)
    causal = positions[:, None] >= positions[None, :]
    key_positions = jnp.arange(MAXB * BLOCK)
    layer_rows = []
    state_rows = []
    for request in range(REQS):
        current = hidden[request * STRETCH:(request + 1) * STRETCH]
        embedded = embedding[request * STRETCH:(request + 1) * STRETCH]
        normed = norm_rows(current, input_gain).astype(jnp.bfloat16)
        paired = jnp.dot(normed, w_input, preferred_element_type=jnp.float32).reshape(STRETCH, MH, 2, P_SIZE)
        gate_part = paired[:, :, 0]
        signal = paired[:, :, 1].reshape(STRETCH, MH * P_SIZE)
        grouped = jnp.dot(normed, w_groups, preferred_element_type=jnp.float32).reshape(STRETCH, 2, G, NS)
        raw_steps = jnp.dot(normed, w_step, preferred_element_type=jnp.float32)
        slot_row = state_slot[request]
        init_state = lax.dynamic_index_in_dim(state_store, slot_row, 0, keepdims=False).reshape(MH, P_SIZE, NS)
        conv_tail = lax.dynamic_index_in_dim(conv_store, slot_row, 0, keepdims=False).astype(jnp.float32)
        padded = jnp.concatenate([conv_tail, signal], axis=0)
        convolved = sum((conv_weight[offset] * padded[offset:offset + STRETCH] for offset in range(CONV)))
        activated = jax.nn.silu(convolved).reshape(STRETCH, MH, P_SIZE)
        step_sizes = jax.nn.softplus(raw_steps + step_bias)
        cumulative = jnp.cumsum(-decay_rate * step_sizes, axis=0)
        outputs_list = []
        finals_list = []
        for group_id in range(G):
            head_span = slice(group_id * group_heads, (group_id + 1) * group_heads)
            piece_out, piece_state = state_block(activated[:, head_span], step_sizes[:, head_span], cumulative[:, head_span], grouped[:, 0, group_id], grouped[:, 1, group_id], init_state[head_span], skip_gain[head_span])
            outputs_list.append(piece_out)
            finals_list.append(piece_state)
        scanned = jnp.concatenate(outputs_list, axis=1)
        final_state = jnp.concatenate(finals_list, axis=0)
        gated = (scanned * jax.nn.silu(gate_part)).reshape(STRETCH, G, group_heads * P_SIZE)
        mean_squares = lax.optimization_barrier(jnp.mean(gated * gated, axis=-1, keepdims=True))
        mixed_rows = ((gated * lax.rsqrt(mean_squares + epsilon)).reshape(STRETCH, MH * P_SIZE) * mix_gain).astype(jnp.bfloat16)
        mamba_sum = jnp.dot(mixed_rows, w_output, preferred_element_type=jnp.float32)
        hidden_next = current.astype(jnp.float32) + mamba_sum
        residual_rounded = hidden_next.astype(jnp.bfloat16)
        joined = jnp.concatenate([residual_rounded, embedded], axis=1)
        shared_normed = norm_rows(joined, shared_gain).astype(jnp.bfloat16)
        projected = jnp.dot(shared_normed, w_attend, preferred_element_type=jnp.float32).astype(jnp.bfloat16)
        projected = projected.reshape(STRETCH, AH, 3, HD)
        queries = jnp.transpose(projected[:, :, 0], (1, 0, 2))
        keys_new = jnp.transpose(projected[:, :, 1], (1, 0, 2))
        values_new = jnp.transpose(projected[:, :, 2], (1, 0, 2))
        blocks = cache_pool[block_table[request]]
        keys_old = jnp.transpose(blocks[:, 0].reshape(MAXB * BLOCK, AH, HD), (1, 0, 2))
        values_old = jnp.transpose(blocks[:, 1].reshape(MAXB * BLOCK, AH, HD), (1, 0, 2))
        prefix_valid = (key_positions < prefix_len[request])[None, :]

        def attend(operands):
            head_queries, head_keys, head_values, old_keys, old_values = operands
            scores_old = jnp.dot(head_queries, old_keys.T, preferred_element_type=jnp.float32) * scale_factor
            scores_old = jnp.where(prefix_valid, scores_old, masked)
            scores_new = jnp.dot(head_queries, head_keys.T, preferred_element_type=jnp.float32) * scale_factor
            scores_new = jnp.where(causal, scores_new, masked)
            row_max = jnp.maximum(lax.optimization_barrier(jnp.max(scores_old, axis=1)), lax.optimization_barrier(jnp.max(scores_new, axis=1)))
            weights_old = jnp.where(prefix_valid, jnp.exp(scores_old - row_max[:, None]), 0.0)
            weights_new = jnp.where(causal, jnp.exp(scores_new - row_max[:, None]), 0.0)
            totals = lax.optimization_barrier(jnp.sum(weights_old, axis=1)) + lax.optimization_barrier(jnp.sum(weights_new, axis=1))
            summed = jnp.dot(weights_old.astype(jnp.bfloat16), old_values, preferred_element_type=jnp.float32)
            summed = summed + jnp.dot(weights_new.astype(jnp.bfloat16), head_values, preferred_element_type=jnp.float32)
            return (summed / totals[:, None]).astype(jnp.bfloat16)
        attended = lax.map(attend, (queries, keys_new, values_new, keys_old, values_old))
        attended = jnp.transpose(attended, (1, 0, 2)).reshape(STRETCH, AH * HD)
        attn_sum = jnp.dot(attended, w_merge, preferred_element_type=jnp.float32)
        layer_rows.append(hidden_next + attn_sum)
        state_rows.append(final_state.reshape(MH, P_SIZE * NS))
    return (jnp.concatenate(layer_rows, axis=0), jnp.stack(state_rows, axis=0))
```

```python
import functools

import jax
import jax.numpy as jnp
from jax import lax
from jax.experimental import pallas as pl
from jax.experimental.pallas import tpu as pltpu
from jax.sharding import PartitionSpec as P

D = 3584
MH = 64
P_SIZE = 64
NS = 64
G = 2
CONV = 4
HD = 224
STRETCH = 512
BLOCK = 128
MAXB = 64
SEQ = 8
SIDE = 4
HEADS = SIDE * SIDE
SHARD = D // HEADS
HALF = SHARD // 2
LANES = STRETCH // 2
PACK = 136
STEPB = 8

MESH = pl.DeviceIdType.MESH
epsilon = 1e-05
masked = -1e30
highest = lax.Precision.HIGHEST
f32 = jnp.float32
bf16 = jnp.bfloat16


def place():
    me = lax.axis_index("head")
    return lax.div(me, SIDE), lax.rem(me, SIDE)


def around(c, by):
    return lax.rem(c + by + SIDE, SIDE)


def coords(half):
    z, y = place()
    return (y, z) if half == 0 else (z, y)


def device(half, c1, c2):
    return c2 * SIDE + c1 if half == 0 else c1 * SIDE + c2


def piece(half, c1, c2):
    return pl.ds(pl.multiple_of(device(half, c1, c2) * SHARD + half * HALF, 16), HALF)


OFFSETS = (0, -1, 1, 2)
LEFT = pl.ds(0, LANES)
RIGHT = pl.ds(LANES, LANES)
FULL = pl.ds(0, STRETCH)


def remote(src, dst, send_sem, recv_sem, dev):
    return pltpu.make_async_remote_copy(
        src_ref=src, dst_ref=dst, send_sem=send_sem, recv_sem=recv_sem,
        device_id={"head": dev}, device_id_type=MESH,
    )


class Gather:
    def __init__(self, own, out, send_sems, recv_sems):
        self.own, self.out, self.ss, self.rs = own, out, send_sems, recv_sems
        self.sent = []

    def go(self, half, idx, src, c1, c2, lanes, to1, to2):
        dst = self.out.at[piece(half, c1, c2), lanes]
        copy = remote(src, dst, self.ss.at[half, idx], self.rs.at[half, idx], device(half, to1, to2))
        copy.start()
        self.sent.append(copy)

    def arrive(self, half, idx, c1, c2, lanes):
        where = self.out.at[piece(half, c1, c2), lanes]
        me1, me2 = coords(half)
        remote(where, where, self.ss.at[half, idx], self.rs.at[half, idx], device(half, around(me1, 1), me2)).wait_recv()

    def start(self):
        for axis in (1, 2):
            for half in (0, 1):
                c1, c2 = coords(half)
                src = self.own.at[pl.ds(half * HALF, HALF), FULL]
                if axis == 1:
                    self.go(half, 0, src, c1, c2, FULL, around(c1, 1), c2)
                    self.go(half, 1, src, c1, c2, FULL, around(c1, -1), c2)
                else:
                    self.go(half, 4, src, c1, c2, FULL, c1, around(c2, 1))
                    self.go(half, 5, src, c1, c2, FULL, c1, around(c2, -1))

    def second(self, half, k):
        c1, c2 = coords(half)
        o1 = around(c1, OFFSETS[k])
        src = self.out.at[piece(half, o1, c2), FULL]
        self.go(half, 4 + 4 * k, src, o1, c2, FULL, c1, around(c2, 1))
        self.go(half, 5 + 4 * k, src, o1, c2, FULL, c1, around(c2, -1))

    def first_near(self):
        for half in (0, 1):
            c1, c2 = coords(half)
            left = around(c1, -1)
            self.arrive(half, 0, left, c2, FULL)
            self.go(half, 2, self.out.at[piece(half, left, c2), LEFT], left, c2, LEFT, around(c1, 1), c2)
            self.second(half, 1)
        for half in (0, 1):
            c1, c2 = coords(half)
            right = around(c1, 1)
            self.arrive(half, 1, right, c2, FULL)
            self.go(half, 3, self.out.at[piece(half, right, c2), RIGHT], right, c2, RIGHT, around(c1, -1), c2)
            self.second(half, 2)

    def first_far(self):
        for half in (0, 1):
            c1, c2 = coords(half)
            far = around(c1, 2)
            self.arrive(half, 2, far, c2, LEFT)
            self.arrive(half, 3, far, c2, RIGHT)
            self.second(half, 3)

    def second_near(self, k):
        for half in (0, 1):
            c1, c2 = coords(half)
            o1 = around(c1, OFFSETS[k])
            for way in (0, 1):
                nb = around(c2, -1 if way == 0 else 1)
                to = around(c2, 1 if way == 0 else -1)
                lanes = LEFT if way == 0 else RIGHT
                self.arrive(half, 4 + 4 * k + way, o1, nb, FULL)
                self.go(half, 6 + 4 * k + way, self.out.at[piece(half, o1, nb), lanes], o1, nb, lanes, c1, to)

    def second_far(self, k):
        for half in (0, 1):
            c1, c2 = coords(half)
            o1 = around(c1, OFFSETS[k])
            far = around(c2, 2)
            self.arrive(half, 6 + 4 * k, o1, far, LEFT)
            self.arrive(half, 7 + 4 * k, o1, far, RIGHT)

    def run(self):
        self.start()
        self.first_near()
        self.second_near(0)
        self.first_far()
        for k in (1, 2, 3):
            self.second_near(k)
        for k in range(SIDE):
            self.second_far(k)

    def finish(self):
        for copy in self.sent:
            copy.wait_send()


GATHER_SEMS = [pltpu.SemaphoreType.DMA((2, 20)), pltpu.SemaphoreType.DMA((2, 20))]

SCATTER_SCRATCH = [
    pltpu.VMEM((D, STRETCH), bf16),
    pltpu.VMEM((2, SIDE, 2, HALF, LANES), bf16),
    pltpu.VMEM((2, SIDE, 2, HALF, STRETCH), bf16),
    pltpu.VMEM((2, SIDE, HALF, STRETCH), bf16),
    pltpu.VMEM((2, 2, HALF, LANES), bf16),
    pltpu.VMEM((2, 2, HALF, STRETCH), bf16),
    pltpu.SemaphoreType.DMA((2, 20)),
    pltpu.SemaphoreType.DMA((2, 20)),
]


class Scatter:
    def __init__(self, part, near1, full1, mid, near2, full2, send_sems, recv_sems):
        self.part, self.near1, self.full1, self.mid = part, near1, full1, mid
        self.near2, self.full2, self.ss, self.rs = near2, full2, send_sems, recv_sems
        self.sent = []

    def go(self, half, idx, src, dst, to1, to2):
        copy = remote(src, dst, self.ss.at[half, idx], self.rs.at[half, idx], device(half, to1, to2))
        copy.start()
        self.sent.append(copy)

    def arrive(self, half, idx, where):
        me1, me2 = coords(half)
        remote(where, where, self.ss.at[half, idx], self.rs.at[half, idx], device(half, around(me1, 1), me2)).wait_recv()

    def one(self, k):
        for half in (0, 1):
            c1, c2 = coords(half)
            o1 = around(c1, OFFSETS[k])
            rows = piece(half, o1, around(c2, 2))
            self.go(half, 4 * k, self.part.at[rows, LEFT], self.near1.at[half, k, 0], c1, around(c2, 1))
            self.go(half, 4 * k + 1, self.part.at[rows, RIGHT], self.near1.at[half, k, 1], c1, around(c2, -1))

    def two(self, k):
        for half in (0, 1):
            c1, c2 = coords(half)
            o1 = around(c1, OFFSETS[k])
            for way in (0, 1):
                to = around(c2, 1 if way == 0 else -1)
                lanes = LEFT if way == 0 else RIGHT
                rows = piece(half, o1, to)
                self.arrive(half, 4 * k + way, self.near1.at[half, k, way])
                mine = self.part[rows, lanes].astype(f32)
                self.part[rows, lanes] = (mine + self.near1[half, k, way].astype(f32)).astype(bf16)
                self.go(half, 4 * k + 2 + way, self.part.at[rows, FULL], self.full1.at[half, k, way], c1, to)

    def three(self, k):
        for half in (0, 1):
            c1, c2 = coords(half)
            o1 = around(c1, OFFSETS[k])
            self.arrive(half, 4 * k + 2, self.full1.at[half, k, 0])
            self.arrive(half, 4 * k + 3, self.full1.at[half, k, 1])
            if k:
                self.mid[half, k] = self.total(half, k).astype(bf16)
                if k == 3:
                    self.go(half, 16, self.mid.at[half, 3, :, LEFT], self.near2.at[half, 0], around(c1, 1), c2)
                    self.go(half, 17, self.mid.at[half, 3, :, RIGHT], self.near2.at[half, 1], around(c1, -1), c2)

    def total(self, half, k):
        c1, c2 = coords(half)
        rows = piece(half, around(c1, OFFSETS[k]), c2)
        return (
            self.part[rows, :].astype(f32)
            + self.full1[half, k, 0].astype(f32)
            + self.full1[half, k, 1].astype(f32)
        )

    def four(self, k):
        way = 0 if k == 2 else 1
        lanes = LEFT if way == 0 else RIGHT
        for half in (0, 1):
            c1, c2 = coords(half)
            self.arrive(half, 16 + way, self.near2.at[half, way])
            mine = self.mid[half, k, :, lanes].astype(f32)
            self.mid[half, k, :, lanes] = (mine + self.near2[half, way].astype(f32)).astype(bf16)
            self.go(half, 18 + way, self.mid.at[half, k], self.full2.at[half, way], around(c1, OFFSETS[k]), c2)

    def run(self):
        for k in (3, 2, 1, 0):
            self.one(k)
        for k in (3, 2, 1, 0):
            self.two(k)
        self.three(3)
        self.three(2)
        self.four(2)
        self.three(1)
        self.four(1)
        self.three(0)

    def result(self, half):
        self.arrive(half, 18, self.full2.at[half, 0])
        self.arrive(half, 19, self.full2.at[half, 1])
        return (
            self.total(half, 0)
            + self.full2[half, 0].astype(f32)
            + self.full2[half, 1].astype(f32)
        )

    def finish(self):
        for copy in self.sent:
            copy.wait_send()


def greet_heads():
    barrier = pltpu.get_barrier_semaphore()
    me = lax.axis_index("head")
    for by in range(1, HEADS):
        pl.semaphore_signal(
            barrier, inc=1, device_id={"head": lax.rem(me + by, HEADS)}, device_id_type=MESH
        )
    return barrier


def gather_kernel(hidden, embed, packed, hidden_all, embed_all, packed_all,
                  h_send, h_recv, e_send, e_recv, p_send, p_recv, local):
    barrier = greet_heads()
    seq = lax.axis_index("seq")
    for by in range(1, SEQ):
        pl.semaphore_signal(
            barrier, inc=1, device_id={"seq": lax.rem(seq + by, SEQ)}, device_id_type=MESH
        )
    me = lax.axis_index("head")
    mine = pl.ds(pl.multiple_of(me * SHARD, 16), SHARD)
    kept = [
        pltpu.make_async_copy(hidden, hidden_all.at[mine, FULL], local.at[0]),
        pltpu.make_async_copy(embed, embed_all.at[mine, FULL], local.at[1]),
        pltpu.make_async_copy(packed, packed_all.at[seq], local.at[2]),
    ]
    for copy in kept:
        copy.start()
    pl.semaphore_wait(barrier, HEADS - 1 + SEQ - 1)
    first = Gather(hidden, hidden_all, h_send, h_recv)
    second = Gather(embed, embed_all, e_send, e_recv)
    first.start()
    states = []
    for by in range(1, SEQ):
        copy = pltpu.make_async_remote_copy(
            src_ref=packed, dst_ref=packed_all.at[seq], send_sem=p_send.at[by - 1], recv_sem=p_recv.at[by - 1],
            device_id={"seq": lax.rem(seq + by, SEQ)}, device_id_type=MESH,
        )
        copy.start()
        states.append(copy)
    first.first_near()
    first.second_near(0)
    first.first_far()
    for k in (1, 2, 3):
        first.second_near(k)
    second.start()
    for k in range(SIDE):
        first.second_far(k)
    second.first_near()
    second.second_near(0)
    second.first_far()
    for k in (1, 2, 3):
        second.second_near(k)
    for k in range(SIDE):
        second.second_far(k)
    for by in range(1, SEQ):
        where = packed_all.at[lax.rem(seq - by + SEQ, SEQ)]
        pltpu.make_async_remote_copy(
            src_ref=where, dst_ref=where, send_sem=p_send.at[by - 1], recv_sem=p_recv.at[by - 1],
            device_id={"seq": lax.rem(seq + by, SEQ)}, device_id_type=MESH,
        ).wait_recv()
    first.finish()
    second.finish()
    for copy in states:
        copy.wait_send()
    for copy in kept:
        copy.wait()


def gather_call(hidden, embed, packed):
    anywhere = pl.BlockSpec(memory_space=pl.ANY)
    return pl.pallas_call(
        gather_kernel,
        out_shape=(
            jax.ShapeDtypeStruct((D, STRETCH), bf16),
            jax.ShapeDtypeStruct((D, STRETCH), bf16),
            jax.ShapeDtypeStruct((SEQ,) + packed.shape, f32),
        ),
        in_specs=[anywhere] * 3,
        out_specs=(anywhere,) * 3,
        scratch_shapes=GATHER_SEMS + GATHER_SEMS + [
            pltpu.SemaphoreType.DMA((SEQ - 1,)),
            pltpu.SemaphoreType.DMA((SEQ - 1,)),
            pltpu.SemaphoreType.DMA((3,)),
        ],
        compiler_params=pltpu.CompilerParams(collective_id=0, has_side_effects=True),
        name="gather_rows",
    )(hidden, embed, packed)


def products(weight, rows, part):
    width = 512

    def chunk(i, _):
        span = pl.ds(pl.multiple_of(i * width, width), width)
        part[span, :] = lax.dot_general(
            weight[:, span], rows, (((0,), (0,)), ((), ())), preferred_element_type=f32
        ).astype(bf16)
        return 0

    lax.fori_loop(0, D // width, chunk, 0)


def mix_kernel(gated, squares, weight, hidden, next_out, all_out,
               part, near1, full1, mid, near2, full2, s_send, s_recv,
               g_send, g_recv, peers, q_send, q_recv, rounded, local):
    barrier = greet_heads()
    pl.semaphore_wait(barrier, HEADS - 1)
    me = lax.axis_index("head")
    group = lax.div(me, 8)
    spot = lax.rem(me, 8)
    out = []
    for by in range(1, 8):
        copy = remote(
            squares, peers.at[by - 1], q_send.at[by - 1], q_recv.at[by - 1],
            group * 8 + lax.rem(spot + by, 8),
        )
        copy.start()
        out.append(copy)
    total = squares[0:1, :]
    for by in range(1, 8):
        out[by - 1].wait_recv()
        total = total + peers[by - 1, 0:1, :]
    scale = lax.rsqrt(total * (1.0 / (MH // G * P_SIZE)) + epsilon)
    products(weight, (gated[...] * scale).astype(bf16), part)
    scatter = Scatter(part, near1, full1, mid, near2, full2, s_send, s_recv)
    scatter.run()
    for half in (0, 1):
        rows = pl.ds(half * HALF, HALF)
        value = hidden[rows, :].astype(f32) + scatter.result(half)
        next_out[rows, :] = value
        rounded[rows, :] = value.astype(bf16)
    mine = pl.ds(pl.multiple_of(me * SHARD, 16), SHARD)
    keep = pltpu.make_async_copy(rounded, all_out.at[mine, FULL], local)
    keep.start()
    gather = Gather(rounded, all_out, g_send, g_recv)
    gather.run()
    gather.finish()
    scatter.finish()
    for copy in out:
        copy.wait_send()
    keep.wait()


def mix_call(gated, squares, weight, hidden):
    vmem = pl.BlockSpec(memory_space=pltpu.VMEM)
    return pl.pallas_call(
        mix_kernel,
        out_shape=(
            jax.ShapeDtypeStruct((SHARD, STRETCH), f32),
            jax.ShapeDtypeStruct((D, STRETCH), bf16),
        ),
        in_specs=[vmem] * 4,
        out_specs=(vmem, pl.BlockSpec(memory_space=pl.ANY)),
        scratch_shapes=SCATTER_SCRATCH + GATHER_SEMS + [
            pltpu.VMEM((7, 8, STRETCH), f32),
            pltpu.SemaphoreType.DMA((7,)),
            pltpu.SemaphoreType.DMA((7,)),
            pltpu.VMEM((SHARD, STRETCH), bf16),
            pltpu.SemaphoreType.DMA,
        ],
        compiler_params=pltpu.CompilerParams(
            collective_id=1, has_side_effects=True, vmem_limit_bytes=40 * 2**20
        ),
        name="mix_rows",
    )(gated, squares, weight, hidden)


def merge_kernel(attended, weight, before, out,
                 part, near1, full1, mid, near2, full2, s_send, s_recv):
    barrier = greet_heads()
    products(weight, attended[...], part)
    pl.semaphore_wait(barrier, HEADS - 1)
    scatter = Scatter(part, near1, full1, mid, near2, full2, s_send, s_recv)
    scatter.run()
    for half in (0, 1):
        rows = pl.ds(half * HALF, HALF)
        out[rows, :] = before[rows, :] + scatter.result(half)
    scatter.finish()


def merge_call(attended, weight, before):
    vmem = pl.BlockSpec(memory_space=pltpu.VMEM)
    return pl.pallas_call(
        merge_kernel,
        out_shape=jax.ShapeDtypeStruct((SHARD, STRETCH), f32),
        in_specs=[vmem] * 3,
        out_specs=vmem,
        scratch_shapes=SCATTER_SCRATCH,
        compiler_params=pltpu.CompilerParams(
            collective_id=2, has_side_effects=True, vmem_limit_bytes=40 * 2**20
        ),
        name="merge_rows",
    )(attended, weight, before)


def attend_kernel(table, length, queries, keys_new, values_new, pool, out, held, sems, acc, top, total):
    scale = HD ** -0.5
    span = STEPB * BLOCK
    limit = length[0]
    blocks = lax.div(limit + BLOCK - 1, BLOCK)
    steps = lax.div(blocks + STEPB - 1, STEPB)

    def fetch(step, slot):
        return [
            pltpu.make_async_copy(
                pool.at[table[step * STEPB + i]], held.at[slot, i], sems.at[slot, i]
            )
            for i in range(STEPB)
        ]

    for copy in fetch(0, 0):
        copy.start()
    q = queries[...]
    scores = lax.dot_general(q, keys_new[...], (((1,), (0,)), ((), ())), preferred_element_type=f32)
    row = lax.broadcasted_iota(jnp.int32, scores.shape, 0)
    col = lax.broadcasted_iota(jnp.int32, scores.shape, 1)
    scores = jnp.where(row >= col, scores, masked)
    high = jnp.max(scores, axis=1, keepdims=True)
    weights = jnp.exp((scores - high) * scale)
    top[...] = high
    total[...] = jnp.sum(weights, axis=1, keepdims=True)
    acc[...] = jnp.dot(weights.astype(bf16), values_new[...], preferred_element_type=f32)

    def step_body(step, _):
        slot = lax.rem(step, 2)

        @pl.when(step + 1 < steps)
        def _():
            for copy in fetch(step + 1, 1 - slot):
                copy.start()

        for copy in fetch(step, slot):
            copy.wait()
        keys = held[slot, :, 0].reshape(span, HD)
        values = held[slot, :, 1].reshape(span, HD)
        scores = lax.dot_general(q, keys, (((1,), (1,)), ((), ())), preferred_element_type=f32)

        def rest(scores):
            old = top[...]
            high = jnp.maximum(old, jnp.max(scores, axis=1, keepdims=True))
            weights = jnp.exp((scores - high) * scale)
            factor = jnp.exp((old - high) * scale)
            top[...] = high
            total[...] = total[...] * factor + jnp.sum(weights, axis=1, keepdims=True)
            acc[...] = acc[...] * factor + jnp.dot(
                weights.astype(bf16), values, preferred_element_type=f32
            )

        @pl.when((step + 1) * span <= limit)
        def _():
            rest(scores)

        @pl.when((step + 1) * span > limit)
        def _():
            where = step * span + lax.broadcasted_iota(jnp.int32, scores.shape, 1)
            rest(jnp.where(where < limit, scores, masked))

        return 0

    lax.fori_loop(0, steps, step_body, 0)
    out[...] = (acc[...] / total[...]).astype(bf16)


def attend_call(table, length, queries, keys_new, values_new, pool):
    vmem = pl.BlockSpec(memory_space=pltpu.VMEM)
    smem = pl.BlockSpec(memory_space=pltpu.SMEM)
    return pl.pallas_call(
        attend_kernel,
        out_shape=jax.ShapeDtypeStruct((STRETCH, HD), bf16),
        in_specs=[smem, smem, vmem, vmem, vmem, pl.BlockSpec(memory_space=pl.ANY)],
        out_specs=vmem,
        scratch_shapes=[
            pltpu.VMEM((2, STEPB, 2, BLOCK, HD), bf16),
            pltpu.SemaphoreType.DMA((2, STEPB)),
            pltpu.VMEM((STRETCH, HD), f32),
            pltpu.VMEM((STRETCH, 1), f32),
            pltpu.VMEM((STRETCH, 1), f32),
        ],
        compiler_params=pltpu.CompilerParams(vmem_limit_bytes=48 * 2**20),
        name="attend_rows",
    )(table, length, queries, keys_new, values_new, pool)


def shift_rows(matrix, by):
    if by == 0:
        return matrix
    return jnp.concatenate([jnp.zeros((by, matrix.shape[1]), f32), matrix[:-by]], axis=0)


def state_block(activated, step_sizes, cumulative, b_proj, c_proj, init_state, skip_gain):
    length = activated.shape[0]
    positions = jnp.arange(length)
    causal = (positions[:, None] >= positions[None, :])[None]
    cums_heads = cumulative.T
    gaps = cums_heads[:, :, None] - cums_heads[:, None, :]
    decays = jnp.where(causal, jnp.exp(jnp.where(causal, gaps, 0.0)), 0.0)
    product = jnp.einsum("tn,sn->ts", c_proj, b_proj, precision=highest)
    weighted = decays * product[None] * step_sizes.T[:, None, :]
    within = jnp.einsum("hts,shp->thp", weighted, activated, precision=highest)
    carried = (
        jnp.einsum("tn,hpn->thp", c_proj, init_state, precision=highest)
        * jnp.exp(cumulative)[:, :, None]
    )
    output = within + carried + skip_gain[None, :, None] * activated
    to_end = jnp.exp(cumulative[-1][None, :] - cumulative) * step_sizes
    final_state = jnp.exp(cumulative[-1])[:, None, None] * init_state + jnp.einsum(
        "shp,sn->hpn", activated * to_end[:, :, None], b_proj, precision=highest
    )
    return (output, final_state)


def body(hidden, embedding, input_gain, w_input, w_groups, w_step, step_bias, decay_rate, skip_gain,
         conv_weight, mix_gain, w_output, state_store, conv_store, state_slot, prefix_len, block_table,
         shared_gain, w_attend, cache_pool, w_merge):
    heads_local = w_step.shape[1]
    my_head = lax.axis_index("head")
    my_seq = lax.axis_index("seq")
    group_id = my_head * heads_local // (MH // G)
    pool = lax.all_gather(cache_pool, "seq", axis=0, tiled=True)

    rows = state_store.shape[0]
    tails = conv_store.astype(f32).reshape(rows, 6, 128)
    packed = jnp.concatenate(
        [state_store.reshape(rows, 128, 128), tails, jnp.zeros((rows, PACK - 134, 128), f32)], axis=1
    )
    hidden_t = hidden.T
    hidden_all, embed_all, packed_all = gather_call(hidden_t, embedding.T, packed)
    held = lax.dynamic_index_in_dim(
        packed_all.reshape(SEQ * rows, PACK, 128), state_slot[my_seq], 0, keepdims=False
    )
    init_state = held[:128].reshape(heads_local, P_SIZE, NS)
    conv_tail = held[128:134].reshape(CONV - 1, heads_local * P_SIZE)

    wide = hidden_all.astype(f32)
    mean = jnp.mean(wide * wide, axis=0, keepdims=True)
    normed = (wide * lax.rsqrt(mean + epsilon) * input_gain[:, None]).astype(bf16)
    over = (((0,), (0,)), ((), ()))
    paired = lax.dot_general(normed, w_input, over, preferred_element_type=f32).reshape(
        STRETCH, heads_local, 2, P_SIZE
    )
    gate_part = paired[:, :, 0]
    signal = paired[:, :, 1].reshape(STRETCH, heads_local * P_SIZE)
    grouped = lax.dot_general(normed, w_groups, over, preferred_element_type=f32)
    b_proj = lax.dynamic_slice_in_dim(grouped, group_id * NS, NS, 1)
    c_proj = lax.dynamic_slice_in_dim(grouped, (G + group_id) * NS, NS, 1)
    raw_steps = lax.dot_general(normed, w_step, over, preferred_element_type=f32)
    padded = jnp.concatenate([conv_tail, signal], axis=0)
    convolved = sum(conv_weight[k] * padded[k : k + STRETCH] for k in range(CONV))
    activated = jax.nn.silu(convolved).reshape(STRETCH, heads_local, P_SIZE)
    step_sizes = jax.nn.softplus(raw_steps + step_bias)
    cumulative = jnp.cumsum(-decay_rate * step_sizes, axis=0)
    scanned, final_state = state_block(
        activated, step_sizes, cumulative, b_proj, c_proj, init_state, skip_gain
    )
    gated = scanned * jax.nn.silu(gate_part)
    squares = jnp.sum(gated * gated, axis=(1, 2))
    gained = (gated.reshape(STRETCH, heads_local * P_SIZE) * mix_gain).T
    hidden_next, residual_all = mix_call(
        gained, jnp.broadcast_to(squares[None, :], (8, STRETCH)), w_output, hidden_t
    )

    res = residual_all.astype(f32)
    emb = embed_all.astype(f32)
    mean = (jnp.sum(res * res, axis=0) + jnp.sum(emb * emb, axis=0)) / (2 * D)
    scale = lax.rsqrt(mean + epsilon)[None, :]
    res = (res * scale * shared_gain[:D, None]).astype(bf16)
    emb = (emb * scale * shared_gain[D:, None]).astype(bf16)
    projected = (
        lax.dot_general(w_attend[:D], res, over, preferred_element_type=f32)
        + lax.dot_general(w_attend[D:], emb, over, preferred_element_type=f32)
    ).astype(bf16)
    attended = attend_call(
        block_table[my_seq], prefix_len[my_seq][None],
        projected[:HD].T, projected[HD : 2 * HD], projected[2 * HD :].T, pool,
    )
    layer_output = merge_call(attended.T, w_merge, hidden_next)
    return (layer_output.T, final_state.reshape(1, heads_local, P_SIZE * NS))


def solution(mesh):
    return jax.shard_map(
        body,
        mesh=mesh,
        in_specs=(
            P("seq", "head"),
            P("seq", "head"),
            P(),
            P(None, "head"),
            P(),
            P(None, "head"),
            P("head"),
            P("head"),
            P("head"),
            P(None, "head"),
            P("head"),
            P("head", None),
            P("seq", "head", None),
            P("seq", None, "head"),
            P(),
            P(),
            P(),
            P(),
            P(None, "head"),
            P("seq", None, None, "head"),
            P("head", None),
        ),
        out_specs=(P("seq", "head"), P("seq", "head", None)),
        check_vma=False,
    )
```

```python
import functools

import jax
import jax.numpy as jnp
from jax import lax
from jax.experimental import pallas as pl
from jax.experimental.pallas import tpu as pltpu
from jax.sharding import PartitionSpec as P

D = 3584
MH = 64
P_SIZE = 64
NS = 64
G = 2
CONV = 4
HD = 224
STRETCH = 512
BLOCK = 128
MAXB = 64
SEQ = 8
SIDE = 4
HEADS = SIDE * SIDE
SHARD = D // HEADS
HALF = SHARD // 2
LANES = STRETCH // 2
STEPB = 8

MESH = pl.DeviceIdType.MESH
epsilon = 1e-05
masked = -1e30
highest = lax.Precision.HIGHEST
f32 = jnp.float32
bf16 = jnp.bfloat16


def place():
    me = lax.axis_index("head")
    return lax.div(me, SIDE), lax.rem(me, SIDE)


def around(c, by):
    return lax.rem(c + by + SIDE, SIDE)


def coords(half):
    z, y = place()
    return (y, z) if half == 0 else (z, y)


def device(half, c1, c2):
    return c2 * SIDE + c1 if half == 0 else c1 * SIDE + c2


def piece(half, c1, c2):
    return pl.ds(pl.multiple_of(device(half, c1, c2) * SHARD + half * HALF, 16), HALF)


OFFSETS = (0, -1, 1, 2)
LEFT = pl.ds(0, LANES)
RIGHT = pl.ds(LANES, LANES)
FULL = pl.ds(0, STRETCH)


def remote(src, dst, send_sem, recv_sem, dev):
    return pltpu.make_async_remote_copy(
        src_ref=src, dst_ref=dst, send_sem=send_sem, recv_sem=recv_sem,
        device_id={"head": dev}, device_id_type=MESH,
    )


class Gather:
    def __init__(self, own, out, send_sems, recv_sems):
        self.own, self.out, self.ss, self.rs = own, out, send_sems, recv_sems
        self.sent = []

    def go(self, half, idx, src, c1, c2, lanes, to1, to2):
        dst = self.out.at[piece(half, c1, c2), lanes]
        copy = remote(src, dst, self.ss.at[half, idx], self.rs.at[half, idx], device(half, to1, to2))
        copy.start()
        self.sent.append(copy)

    def arrive(self, half, idx, c1, c2, lanes):
        where = self.out.at[piece(half, c1, c2), lanes]
        me1, me2 = coords(half)
        remote(where, where, self.ss.at[half, idx], self.rs.at[half, idx], device(half, around(me1, 1), me2)).wait_recv()

    def start(self):
        for axis in (1, 2):
            for half in (0, 1):
                c1, c2 = coords(half)
                src = self.own.at[pl.ds(half * HALF, HALF), FULL]
                if axis == 1:
                    self.go(half, 0, src, c1, c2, FULL, around(c1, 1), c2)
                    self.go(half, 1, src, c1, c2, FULL, around(c1, -1), c2)
                else:
                    self.go(half, 4, src, c1, c2, FULL, c1, around(c2, 1))
                    self.go(half, 5, src, c1, c2, FULL, c1, around(c2, -1))

    def second(self, half, k):
        c1, c2 = coords(half)
        o1 = around(c1, OFFSETS[k])
        src = self.out.at[piece(half, o1, c2), FULL]
        self.go(half, 4 + 4 * k, src, o1, c2, FULL, c1, around(c2, 1))
        self.go(half, 5 + 4 * k, src, o1, c2, FULL, c1, around(c2, -1))

    def first_near(self):
        for half in (0, 1):
            c1, c2 = coords(half)
            left = around(c1, -1)
            self.arrive(half, 0, left, c2, FULL)
            self.go(half, 2, self.out.at[piece(half, left, c2), LEFT], left, c2, LEFT, around(c1, 1), c2)
            self.second(half, 1)
        for half in (0, 1):
            c1, c2 = coords(half)
            right = around(c1, 1)
            self.arrive(half, 1, right, c2, FULL)
            self.go(half, 3, self.out.at[piece(half, right, c2), RIGHT], right, c2, RIGHT, around(c1, -1), c2)
            self.second(half, 2)

    def first_far(self):
        for half in (0, 1):
            c1, c2 = coords(half)
            far = around(c1, 2)
            self.arrive(half, 2, far, c2, LEFT)
            self.arrive(half, 3, far, c2, RIGHT)
            self.second(half, 3)

    def second_near(self, k):
        for half in (0, 1):
            c1, c2 = coords(half)
            o1 = around(c1, OFFSETS[k])
            for way in (0, 1):
                nb = around(c2, -1 if way == 0 else 1)
                to = around(c2, 1 if way == 0 else -1)
                lanes = LEFT if way == 0 else RIGHT
                self.arrive(half, 4 + 4 * k + way, o1, nb, FULL)
                self.go(half, 6 + 4 * k + way, self.out.at[piece(half, o1, nb), lanes], o1, nb, lanes, c1, to)

    def second_far(self, k):
        for half in (0, 1):
            c1, c2 = coords(half)
            o1 = around(c1, OFFSETS[k])
            far = around(c2, 2)
            self.arrive(half, 6 + 4 * k, o1, far, LEFT)
            self.arrive(half, 7 + 4 * k, o1, far, RIGHT)

    def run(self):
        self.start()
        self.first_near()
        self.second_near(0)
        self.first_far()
        for k in (1, 2, 3):
            self.second_near(k)
        for k in range(SIDE):
            self.second_far(k)

    def finish(self):
        for copy in self.sent:
            copy.wait_send()


GATHER_SEMS = [pltpu.SemaphoreType.DMA((2, 20)), pltpu.SemaphoreType.DMA((2, 20))]

SCATTER_SCRATCH = [
    pltpu.VMEM((D, STRETCH), bf16),
    pltpu.VMEM((2, SIDE, 2, HALF, LANES), bf16),
    pltpu.VMEM((2, SIDE, 2, HALF, STRETCH), bf16),
    pltpu.VMEM((2, SIDE, HALF, STRETCH), bf16),
    pltpu.VMEM((2, 2, HALF, LANES), bf16),
    pltpu.VMEM((2, 2, HALF, STRETCH), bf16),
    pltpu.SemaphoreType.DMA((2, 20)),
    pltpu.SemaphoreType.DMA((2, 20)),
]


class Scatter:
    def __init__(self, part, near1, full1, mid, near2, full2, send_sems, recv_sems):
        self.part, self.near1, self.full1, self.mid = part, near1, full1, mid
        self.near2, self.full2, self.ss, self.rs = near2, full2, send_sems, recv_sems
        self.sent = []

    def go(self, half, idx, src, dst, to1, to2):
        copy = remote(src, dst, self.ss.at[half, idx], self.rs.at[half, idx], device(half, to1, to2))
        copy.start()
        self.sent.append(copy)

    def arrive(self, half, idx, where):
        me1, me2 = coords(half)
        remote(where, where, self.ss.at[half, idx], self.rs.at[half, idx], device(half, around(me1, 1), me2)).wait_recv()

    def one(self, k):
        for half in (0, 1):
            c1, c2 = coords(half)
            o1 = around(c1, OFFSETS[k])
            rows = piece(half, o1, around(c2, 2))
            self.go(half, 4 * k, self.part.at[rows, LEFT], self.near1.at[half, k, 0], c1, around(c2, 1))
            self.go(half, 4 * k + 1, self.part.at[rows, RIGHT], self.near1.at[half, k, 1], c1, around(c2, -1))

    def two(self, k):
        for half in (0, 1):
            c1, c2 = coords(half)
            o1 = around(c1, OFFSETS[k])
            for way in (0, 1):
                to = around(c2, 1 if way == 0 else -1)
                lanes = LEFT if way == 0 else RIGHT
                rows = piece(half, o1, to)
                self.arrive(half, 4 * k + way, self.near1.at[half, k, way])
                mine = self.part[rows, lanes].astype(f32)
                self.part[rows, lanes] = (mine + self.near1[half, k, way].astype(f32)).astype(bf16)
                self.go(half, 4 * k + 2 + way, self.part.at[rows, FULL], self.full1.at[half, k, way], c1, to)

    def three(self, k):
        for half in (0, 1):
            c1, c2 = coords(half)
            o1 = around(c1, OFFSETS[k])
            self.arrive(half, 4 * k + 2, self.full1.at[half, k, 0])
            self.arrive(half, 4 * k + 3, self.full1.at[half, k, 1])
            if k:
                self.mid[half, k] = self.total(half, k).astype(bf16)
                if k == 3:
                    self.go(half, 16, self.mid.at[half, 3, :, LEFT], self.near2.at[half, 0], around(c1, 1), c2)
                    self.go(half, 17, self.mid.at[half, 3, :, RIGHT], self.near2.at[half, 1], around(c1, -1), c2)

    def total(self, half, k):
        c1, c2 = coords(half)
        rows = piece(half, around(c1, OFFSETS[k]), c2)
        return (
            self.part[rows, :].astype(f32)
            + self.full1[half, k, 0].astype(f32)
            + self.full1[half, k, 1].astype(f32)
        )

    def four(self, k):
        way = 0 if k == 2 else 1
        lanes = LEFT if way == 0 else RIGHT
        for half in (0, 1):
            c1, c2 = coords(half)
            self.arrive(half, 16 + way, self.near2.at[half, way])
            mine = self.mid[half, k, :, lanes].astype(f32)
            self.mid[half, k, :, lanes] = (mine + self.near2[half, way].astype(f32)).astype(bf16)
            self.go(half, 18 + way, self.mid.at[half, k], self.full2.at[half, way], around(c1, OFFSETS[k]), c2)

    def run(self):
        for k in (3, 2, 1, 0):
            self.one(k)
        for k in (3, 2, 1, 0):
            self.two(k)
        self.three(3)
        self.three(2)
        self.four(2)
        self.three(1)
        self.four(1)
        self.three(0)

    def result(self, half):
        self.arrive(half, 18, self.full2.at[half, 0])
        self.arrive(half, 19, self.full2.at[half, 1])
        return (
            self.total(half, 0)
            + self.full2[half, 0].astype(f32)
            + self.full2[half, 1].astype(f32)
        )

    def finish(self):
        for copy in self.sent:
            copy.wait_send()


def greet_heads():
    barrier = pltpu.get_barrier_semaphore()
    me = lax.axis_index("head")
    for by in range(1, HEADS):
        pl.semaphore_signal(
            barrier, inc=1, device_id={"head": lax.rem(me + by, HEADS)}, device_id_type=MESH
        )
    return barrier


def flat(row, count):
    turned = jnp.broadcast_to(row, (128, count)).T
    return jnp.concatenate([turned] * (STRETCH // 128), axis=1)


def column(table, start, count):
    rows = table.shape[0]
    entry = start + lax.broadcasted_iota(jnp.int32, (count, rows), 0)
    pick = (lax.shift_right_logical(entry, 7) == lax.broadcasted_iota(jnp.int32, (count, rows), 1))
    lines = jnp.dot(pick.astype(f32), table[...], precision=highest, preferred_element_type=f32)
    entry = start + lax.broadcasted_iota(jnp.int32, (count, 128), 0)
    keep = jnp.bitwise_and(entry, 127) == lax.broadcasted_iota(jnp.int32, (count, 128), 1)
    return jnp.sum(jnp.where(keep, lines, 0.0), axis=1, keepdims=True)


def send_sums(mine, peers, send_sems, recv_sems):
    me = lax.axis_index("head")
    out = []
    for by in range(1, HEADS):
        copy = remote(
            mine, peers.at[by - 1], send_sems.at[by - 1], recv_sems.at[by - 1],
            lax.rem(me + by, HEADS),
        )
        copy.start()
        out.append(copy)
    return out


def add_sums(mine, peers, out):
    total = mine[...]
    for by in range(1, HEADS):
        out[by - 1].wait_recv()
        total = total + peers[by - 1]
    return total


def silu(value):
    return value / (1.0 + jnp.exp(-value))


TN = (((0,), (0,)), ((), ()))
NT = (((1,), (1,)), ((), ()))
HL = 4


def scan_kernel(hidden, embed, gain_in, gain_sh, states, tails, slots, w_in, w_gr, w_st, bias, decay, skip,
                conv_w, mix_g, gained_out, squares_out, final_out, embed_all, embed_sq,
                wide, own_h, own_e, win, wgr, paired, grouped, sums, peers, stores, tail_all, lines,
                h_send, h_recv, e_send, e_recv, q_send, q_recv, s_send, s_recv, t_send, t_recv, local):
    seq = lax.axis_index("seq")
    me = lax.axis_index("head")
    loads = [
        pltpu.make_async_copy(w_in, win, local.at[0]),
        pltpu.make_async_copy(w_gr, wgr, local.at[1]),
        pltpu.make_async_copy(states, stores.at[pl.ds(seq * 2, 2)], local.at[2]),
        pltpu.make_async_copy(tails, tail_all.at[pl.ds(seq * 2, 2)], local.at[3]),
    ]
    for copy in loads:
        copy.start()
    barrier = greet_heads()
    for by in range(1, SEQ):
        pl.semaphore_signal(
            barrier, inc=1, device_id={"seq": lax.rem(seq + by, SEQ)}, device_id_type=MESH
        )
    mine = pl.ds(pl.multiple_of(me * SHARD, 16), SHARD)
    value = hidden[...].astype(f32)
    sq_h = jnp.sum(value * value, axis=0, keepdims=True)
    ready = (value * column(gain_in, me * SHARD, SHARD)).astype(bf16)
    own_h[...] = ready
    wide[mine, :] = ready
    pl.semaphore_wait(barrier, HEADS - 1 + SEQ - 1)
    first = Gather(own_h, wide, h_send, h_recv)
    second = Gather(own_e, embed_all, e_send, e_recv)
    first.start()
    value = embed[...].astype(f32)
    sq_e = jnp.sum(value * value, axis=0, keepdims=True)
    own_e[...] = (value * column(gain_sh, D + me * SHARD, SHARD)).astype(bf16)
    line = lax.broadcasted_iota(jnp.int32, (8, STRETCH), 0)
    sums[...] = jnp.where(line == 0, sq_h, jnp.where(line == 1, sq_e, 0.0))
    out = send_sums(sums, peers, q_send, q_recv)
    kept = pltpu.make_async_copy(own_e, embed_all.at[mine, FULL], local.at[4])
    kept.start()
    moved = []
    for by in range(1, SEQ):
        to = {"seq": lax.rem(seq + by, SEQ)}
        for src, dst, ss, rs in ((states, stores, s_send, s_recv), (tails, tail_all, t_send, t_recv)):
            copy = pltpu.make_async_remote_copy(
                src_ref=src, dst_ref=dst.at[pl.ds(seq * 2, 2)], send_sem=ss.at[by - 1], recv_sem=rs.at[by - 1],
                device_id=to, device_id_type=MESH,
            )
            copy.start()
            moved.append(copy)
    first.first_near()
    first.second_near(0)
    first.first_far()
    for k in (1, 2, 3):
        first.second_near(k)
    second.start()
    for k in range(SIDE):
        first.second_far(k)
    total = add_sums(sums, peers, out)
    embed_sq[...] = total
    scale = lax.rsqrt(total[0:1, :] * (1.0 / D) + epsilon)
    for copy in loads:
        copy.wait()

    def project(i, _):
        span = pl.ds(pl.multiple_of(i * 256, 256), 256)
        paired[span, :] = scale * lax.dot_general(win[:, span], wide[...], TN, preferred_element_type=f32)
        return 0

    lax.fori_loop(0, 2, project, 0)
    second.first_near()
    grouped[...] = scale * lax.dot_general(wgr[...], wide[...], TN, preferred_element_type=f32)
    raw = scale * jnp.dot(w_st[...], wide[...], preferred_element_type=f32)
    second.second_near(0)
    second.first_far()
    head = lax.broadcasted_iota(jnp.int32, (HL, STRETCH), 0)

    def by_head(ref):
        line = jnp.zeros((HL, STRETCH), f32)
        for i in range(HL):
            line = jnp.where(head == i, ref[i], line)
        return line

    raw = raw + by_head(bias)
    steps = jnp.maximum(raw, 0.0) + jnp.log1p(jnp.exp(-jnp.abs(raw)))
    cums = -by_head(decay) * steps
    lane = lax.broadcasted_iota(jnp.int32, (HL, STRETCH), 1)
    by = 1
    while by < STRETCH:
        cums = cums + jnp.where(lane >= by, pltpu.roll(cums, by, 1), 0.0)
        by *= 2
    turned = jnp.concatenate([cums, steps, jnp.zeros((128 - 2 * HL, STRETCH), f32)], axis=0).T
    group = lax.div(me, 8)
    b_proj = grouped[pl.ds(pl.multiple_of(group * NS, NS), NS), :]
    c_proj = grouped[pl.ds(pl.multiple_of(G * NS + group * NS, NS), NS), :]
    pairs = lax.dot_general(b_proj.astype(bf16), c_proj.astype(bf16), TN, preferred_element_type=f32)
    src = lax.broadcasted_iota(jnp.int32, pairs.shape, 0)
    dst = lax.broadcasted_iota(jnp.int32, pairs.shape, 1)
    pairs = jnp.where(src <= dst, pairs, 0.0)

    for copy in moved:
        copy.wait_recv()
    slot = slots[seq]
    for h in range(HL):
        for i in range(32):
            lines[pl.ds(h * 32 + i, 1), :] = stores[slot, h : h + 1, i * 128 : (i + 1) * 128]
    p_row = lax.broadcasted_iota(jnp.int32, (P_SIZE, 32), 0)
    p_col = lax.broadcasted_iota(jnp.int32, (P_SIZE, 32), 1)
    even = (p_row == 2 * p_col).astype(f32)
    odd = (p_row == 2 * p_col + 1).astype(f32)
    tail = tail_all[slot]
    t_row = lax.broadcasted_iota(jnp.int32, (8, 128), 0)
    t_col = lax.broadcasted_iota(jnp.int32, (8, 128), 1)
    before = []
    for j in range(2):
        pick = jnp.zeros((8, 128), f32)
        for k in range(CONV - 1):
            pick = jnp.where((t_row == 2 * k + j) & (t_col == 125 + k), 1.0, pick)
        before.append(lax.dot_general(tail, pick, TN, precision=highest, preferred_element_type=f32))
    taps = [flat(conv_w[k : k + 1, :], HL * P_SIZE) for k in range(CONV)]
    mixing = flat(mix_g[...], HL * P_SIZE)
    squares = jnp.zeros((1, STRETCH), f32)
    for h in range(HL):
        chan = slice(h * P_SIZE, (h + 1) * P_SIZE)
        gate = paired[h * 128 : h * 128 + 64, :]
        signal = paired[h * 128 + 64 : h * 128 + 128, :]
        half = (h % 2) * P_SIZE
        padded = jnp.concatenate([before[h // 2][half : half + P_SIZE], signal], axis=1)
        conv = taps[CONV - 1][chan] * signal
        for back in range(1, CONV):
            conv = conv + taps[CONV - 1 - back][chan] * pltpu.roll(padded, back, 1)[:, 128:]
        active = silu(conv)
        cum = cums[h : h + 1, :]
        step = steps[h : h + 1, :]
        mix = jnp.exp(jnp.minimum(cum - turned[:, h : h + 1], 0.0)) * pairs * turned[:, HL + h : HL + h + 1]
        within = jnp.dot(active.astype(bf16), mix.astype(bf16), preferred_element_type=f32)
        rows = lines[h * 32 : (h + 1) * 32, :]
        init = jnp.dot(even, rows[:, :NS], precision=highest, preferred_element_type=f32)
        init = init + jnp.dot(odd, rows[:, NS:], precision=highest, preferred_element_type=f32)
        carried = jnp.dot(init, c_proj, precision=highest, preferred_element_type=f32) * jnp.exp(cum)
        gated = (within + carried + skip[h] * active) * silu(gate)
        squares = squares + jnp.sum(gated * gated, axis=0, keepdims=True)
        gained_out[chan, :] = gated * mixing[chan]
        last = cum[:, STRETCH - 1 :]
        to_end = jnp.exp(last - cum) * step
        final_out[chan, :] = jnp.exp(last) * init + lax.dot_general(
            active * to_end, b_proj, NT, precision=highest, preferred_element_type=f32
        )
        if h:
            second.second_near(h)
    squares_out[...] = jnp.broadcast_to(squares, (8, STRETCH))
    for k in range(SIDE):
        second.second_far(k)
    first.finish()
    second.finish()
    for copy in out + moved:
        copy.wait_send()
    kept.wait()


def scan_call(hidden, embed, gain_in, gain_sh, states, tails, slots, w_in, w_gr, w_st, bias, decay, skip,
              conv_w, mix_g):
    anywhere = pl.BlockSpec(memory_space=pl.ANY)
    vmem = pl.BlockSpec(memory_space=pltpu.VMEM)
    smem = pl.BlockSpec(memory_space=pltpu.SMEM)
    dma = pltpu.SemaphoreType.DMA
    return pl.pallas_call(
        scan_kernel,
        out_shape=(
            jax.ShapeDtypeStruct((HL * P_SIZE, STRETCH), f32),
            jax.ShapeDtypeStruct((8, STRETCH), f32),
            jax.ShapeDtypeStruct((HL * P_SIZE, NS), f32),
            jax.ShapeDtypeStruct((D, STRETCH), bf16),
            jax.ShapeDtypeStruct((8, STRETCH), f32),
        ),
        in_specs=[vmem] * 4 + [anywhere] * 2 + [smem] + [anywhere] * 2 + [vmem] + [smem] * 3 + [vmem] * 2,
        out_specs=(vmem, vmem, vmem, anywhere, vmem),
        scratch_shapes=[
            pltpu.VMEM((D, STRETCH), bf16),
            pltpu.VMEM((SHARD, STRETCH), bf16),
            pltpu.VMEM((SHARD, STRETCH), bf16),
            pltpu.VMEM((D, HL * 128), bf16),
            pltpu.VMEM((D, 2 * G * NS), bf16),
            pltpu.VMEM((HL * 128, STRETCH), f32),
            pltpu.VMEM((2 * G * NS, STRETCH), f32),
            pltpu.VMEM((8, STRETCH), f32),
            pltpu.VMEM((HEADS - 1, 8, STRETCH), f32),
            pltpu.VMEM((2 * SEQ, HL, P_SIZE * NS), f32),
            pltpu.VMEM((2 * SEQ, 8, 128), f32),
            pltpu.VMEM((128, 128), f32),
        ] + GATHER_SEMS + GATHER_SEMS + [
            dma((HEADS - 1,)), dma((HEADS - 1,)), dma((SEQ - 1,)), dma((SEQ - 1,)),
            dma((SEQ - 1,)), dma((SEQ - 1,)), dma((5,)),
        ],
        compiler_params=pltpu.CompilerParams(
            collective_id=0, has_side_effects=True, vmem_limit_bytes=48 * 2**20
        ),
        name="scan_rows",
    )(hidden, embed, gain_in, gain_sh, states, tails, slots, w_in, w_gr, w_st, bias, decay, skip, conv_w, mix_g)


def products(weight, rows, part):
    width = 512

    def chunk(i, _):
        span = pl.ds(pl.multiple_of(i * width, width), width)
        part[span, :] = lax.dot_general(
            weight[:, span], rows, (((0,), (0,)), ((), ())), preferred_element_type=f32
        ).astype(bf16)
        return 0

    lax.fori_loop(0, D // width, chunk, 0)


def mix_kernel(gated, squares, weight, hidden, gain_sh, w_att, embed_all, embed_sq, next_out, proj_out,
               part, near1, full1, mid, near2, full2, s_send, s_recv,
               g_send, g_recv, peers, q_send, q_recv, sums, peers2, r_send, r_recv, rounded, watt, emb, wide,
               acc, local):
    loads = [
        pltpu.make_async_copy(embed_all, emb, local.at[0]),
        pltpu.make_async_copy(w_att, watt, local.at[1]),
    ]
    for copy in loads:
        copy.start()
    barrier = greet_heads()
    pl.semaphore_wait(barrier, HEADS - 1)
    me = lax.axis_index("head")
    group = lax.div(me, 8)
    spot = lax.rem(me, 8)
    out = []
    for by in range(1, 8):
        copy = remote(
            squares, peers.at[by - 1], q_send.at[by - 1], q_recv.at[by - 1],
            group * 8 + lax.rem(spot + by, 8),
        )
        copy.start()
        out.append(copy)
    total = squares[0:1, :]
    for by in range(1, 8):
        out[by - 1].wait_recv()
        total = total + peers[by - 1, 0:1, :]
    scale = lax.rsqrt(total * (1.0 / (MH // G * P_SIZE)) + epsilon)
    products(weight, (gated[...] * scale).astype(bf16), part)
    scatter = Scatter(part, near1, full1, mid, near2, full2, s_send, s_recv)
    for k in (3, 2, 1, 0):
        scatter.one(k)
    for copy in loads:
        copy.wait()

    def from_embed(i):
        acc[i * SHARD : (i + 1) * SHARD, :] = jnp.dot(
            watt[i * SHARD : (i + 1) * SHARD, D:], emb[...], preferred_element_type=f32
        )

    for k in (3, 2, 1, 0):
        scatter.two(k)
    from_embed(0)
    scatter.three(3)
    scatter.three(2)
    from_embed(1)
    scatter.four(2)
    scatter.three(1)
    scatter.four(1)
    scatter.three(0)
    from_embed(2)
    gain = column(gain_sh, me * SHARD, SHARD)
    mine = pl.ds(pl.multiple_of(me * SHARD, 16), SHARD)
    sq = jnp.zeros((1, STRETCH), f32)
    for half in (0, 1):
        rows = pl.ds(half * HALF, HALF)
        value = hidden[rows, :].astype(f32) + scatter.result(half)
        next_out[rows, :] = value
        value = value.astype(bf16).astype(f32)
        sq = sq + jnp.sum(value * value, axis=0, keepdims=True)
        rounded[rows, :] = (value * gain[half * HALF : (half + 1) * HALF]).astype(bf16)
    sums[...] = jnp.broadcast_to(sq, (8, STRETCH))
    gather = Gather(rounded, wide, g_send, g_recv)
    gather.start()
    sent = send_sums(sums, peers2, r_send, r_recv)
    wide[mine, :] = rounded[...]
    gather.first_near()
    gather.second_near(0)
    gather.first_far()
    for k in (1, 2, 3):
        gather.second_near(k)
    for k in range(SIDE):
        gather.second_far(k)
    total = add_sums(sums, peers2, sent)[0:1, :] + embed_sq[1:2, :]
    scale = lax.rsqrt(total * (0.5 / D) + epsilon)
    for i in range(3):
        rows = slice(i * SHARD, (i + 1) * SHARD)
        value = acc[rows, :] + jnp.dot(watt[rows, :D], wide[...], preferred_element_type=f32)
        proj_out[rows, :] = (value * scale).astype(bf16)
    gather.finish()
    scatter.finish()
    for copy in out + sent:
        copy.wait_send()


def mix_call(gated, squares, weight, hidden, gain_sh, w_att, embed_all, embed_sq):
    vmem = pl.BlockSpec(memory_space=pltpu.VMEM)
    anywhere = pl.BlockSpec(memory_space=pl.ANY)
    dma = pltpu.SemaphoreType.DMA
    return pl.pallas_call(
        mix_kernel,
        out_shape=(
            jax.ShapeDtypeStruct((SHARD, STRETCH), f32),
            jax.ShapeDtypeStruct((3 * HD, STRETCH), bf16),
        ),
        in_specs=[vmem] * 5 + [anywhere] * 2 + [vmem],
        out_specs=(vmem, vmem),
        scratch_shapes=SCATTER_SCRATCH + GATHER_SEMS + [
            pltpu.VMEM((7, 8, STRETCH), f32),
            dma((7,)),
            dma((7,)),
            pltpu.VMEM((8, STRETCH), f32),
            pltpu.VMEM((HEADS - 1, 8, STRETCH), f32),
            dma((HEADS - 1,)),
            dma((HEADS - 1,)),
            pltpu.VMEM((SHARD, STRETCH), bf16),
            pltpu.VMEM((3 * HD, 2 * D), bf16),
            pltpu.VMEM((D, STRETCH), bf16),
            pltpu.VMEM((D, STRETCH), bf16),
            pltpu.VMEM((3 * HD, STRETCH), f32),
            dma((2,)),
        ],
        compiler_params=pltpu.CompilerParams(
            collective_id=1, has_side_effects=True, vmem_limit_bytes=56 * 2**20
        ),
        name="mix_rows",
    )(gated, squares, weight, hidden, gain_sh, w_att, embed_all, embed_sq)


def merge_kernel(attended, weight, before, out,
                 part, near1, full1, mid, near2, full2, s_send, s_recv):
    barrier = greet_heads()
    products(weight, attended[...], part)
    pl.semaphore_wait(barrier, HEADS - 1)
    scatter = Scatter(part, near1, full1, mid, near2, full2, s_send, s_recv)
    scatter.run()
    for half in (0, 1):
        rows = pl.ds(half * HALF, HALF)
        out[rows, :] = before[rows, :] + scatter.result(half)
    scatter.finish()


def merge_call(attended, weight, before):
    vmem = pl.BlockSpec(memory_space=pltpu.VMEM)
    return pl.pallas_call(
        merge_kernel,
        out_shape=jax.ShapeDtypeStruct((SHARD, STRETCH), f32),
        in_specs=[vmem] * 3,
        out_specs=vmem,
        scratch_shapes=SCATTER_SCRATCH,
        compiler_params=pltpu.CompilerParams(
            collective_id=2, has_side_effects=True, vmem_limit_bytes=40 * 2**20
        ),
        name="merge_rows",
    )(attended, weight, before)


def turn(value):
    return jnp.concatenate([value, jnp.zeros((256 - HD, STRETCH), f32)], axis=0).T[:, :HD]


def attend_kernel(table, lengths, projected, pool, out, held, sems, acc, top, total):
    seq = lax.axis_index("seq")
    scale = HD ** -0.5 * 1.4426950408889634
    span = STEPB * BLOCK
    limit = lengths[seq]
    blocks = lax.div(limit + BLOCK - 1, BLOCK)
    steps = lax.div(blocks + STEPB - 1, STEPB)

    def fetch(step, slot):
        return [
            pltpu.make_async_copy(
                pool.at[table[seq, step * STEPB + i]],
                held.at[slot, :, :, pl.ds(i * BLOCK, BLOCK)],
                sems.at[slot, i],
            )
            for i in range(STEPB)
        ]

    for copy in fetch(0, 0):
        copy.start()
    q = turn(projected[:HD, :].astype(f32)).astype(bf16)
    scores = jnp.dot(q, projected[HD : 2 * HD, :], preferred_element_type=f32)
    row = lax.broadcasted_iota(jnp.int32, scores.shape, 0)
    col = lax.broadcasted_iota(jnp.int32, scores.shape, 1)
    scores = jnp.where(row >= col, scores, masked)
    high = jnp.max(scores, axis=1, keepdims=True)
    weights = jnp.exp2((scores - high) * scale)
    top[...] = high
    total[...] = jnp.sum(weights, axis=1, keepdims=True)
    acc[...] = lax.dot_general(
        weights.astype(bf16), projected[2 * HD :, :], NT, preferred_element_type=f32
    )

    def step_body(step, _):
        slot = lax.rem(step, 2)

        @pl.when(step + 1 < steps)
        def _():
            for copy in fetch(step + 1, 1 - slot):
                copy.start()

        for copy in fetch(step, slot):
            copy.wait()
        scores = jnp.dot(q, held[slot, 0], preferred_element_type=f32)

        def rest(scores):
            old = top[...]
            high = jnp.maximum(old, jnp.max(scores, axis=1, keepdims=True))
            weights = jnp.exp2((scores - high) * scale)
            factor = jnp.exp2((old - high) * scale)
            top[...] = high
            total[...] = total[...] * factor + jnp.sum(weights, axis=1, keepdims=True)
            acc[...] = acc[...] * factor + lax.dot_general(
                weights.astype(bf16), held[slot, 1], NT, preferred_element_type=f32
            )

        @pl.when((step + 1) * span <= limit)
        def _():
            rest(scores)

        @pl.when((step + 1) * span > limit)
        def _():
            where = step * span + lax.broadcasted_iota(jnp.int32, scores.shape, 1)
            rest(jnp.where(where < limit, scores, masked))

        return 0

    lax.fori_loop(0, steps, step_body, 0)
    value = acc[...] / total[...]
    value = jnp.concatenate([value, jnp.zeros((STRETCH, 256 - HD), f32)], axis=1).T
    out[...] = value[:HD].astype(bf16)


def attend_call(table, lengths, projected, pool):
    vmem = pl.BlockSpec(memory_space=pltpu.VMEM)
    smem = pl.BlockSpec(memory_space=pltpu.SMEM)
    return pl.pallas_call(
        attend_kernel,
        out_shape=jax.ShapeDtypeStruct((HD, STRETCH), bf16),
        in_specs=[smem, smem, vmem, pl.BlockSpec(memory_space=pl.ANY)],
        out_specs=vmem,
        scratch_shapes=[
            pltpu.VMEM((2, 2, HD, STEPB * BLOCK), bf16),
            pltpu.SemaphoreType.DMA((2, STEPB)),
            pltpu.VMEM((STRETCH, HD), f32),
            pltpu.VMEM((STRETCH, 1), f32),
            pltpu.VMEM((STRETCH, 1), f32),
        ],
        compiler_params=pltpu.CompilerParams(vmem_limit_bytes=48 * 2**20),
        name="attend_rows",
    )(table, lengths, projected, pool)


def body(hidden, embedding, input_gain, w_input, w_groups, w_step, step_bias, decay_rate, skip_gain,
         conv_weight, mix_gain, w_output, state_store, conv_store, state_slot, prefix_len, block_table,
         shared_gain, w_attend, cache_pool, w_merge):
    heads_local = w_step.shape[1]
    pool = lax.all_gather(cache_pool.transpose(0, 1, 3, 2), "seq", axis=0, tiled=True)
    rows = state_store.shape[0]
    tails = jnp.pad(conv_store.astype(f32).reshape(rows, 6, 128), ((0, 0), (0, 2), (0, 0)))
    hidden_t = hidden.T
    gain_sh = shared_gain.reshape(2 * D // 128, 128)
    gained, squares, final_state, embed_all, embed_sq = scan_call(
        hidden_t, embedding.T, input_gain.reshape(D // 128, 128), gain_sh, state_store, tails, state_slot,
        w_input, w_groups, w_step.T, step_bias, decay_rate, skip_gain, conv_weight, mix_gain[None, :],
    )
    hidden_next, projected = mix_call(
        gained, squares, w_output, hidden_t, gain_sh, w_attend.T, embed_all, embed_sq
    )
    attended = attend_call(block_table, prefix_len, projected, pool)
    layer_output = merge_call(attended, w_merge, hidden_next)
    return (layer_output.T, final_state.reshape(1, heads_local, P_SIZE * NS))


def solution(mesh):
    return jax.shard_map(
        body,
        mesh=mesh,
        in_specs=(
            P("seq", "head"),
            P("seq", "head"),
            P(),
            P(None, "head"),
            P(),
            P(None, "head"),
            P("head"),
            P("head"),
            P("head"),
            P(None, "head"),
            P("head"),
            P("head", None),
            P("seq", "head", None),
            P("seq", None, "head"),
            P(),
            P(),
            P(),
            P(),
            P(None, "head"),
            P("seq", None, None, "head"),
            P("head", None),
        ),
        out_specs=(P("seq", "head"), P("seq", "head", None)),
        check_vma=False,
    )
```

```python
import functools

import jax
import jax.numpy as jnp
from jax import lax
from jax.experimental import pallas as pl
from jax.experimental.pallas import tpu as pltpu
from jax.sharding import PartitionSpec as P

D = 3584
MH = 64
P_SIZE = 64
NS = 64
G = 2
CONV = 4
HD = 224
STRETCH = 512
BLOCK = 128
MAXB = 64
SEQ = 8
SIDE = 4
HEADS = SIDE * SIDE
SHARD = D // HEADS
HALF = SHARD // 2
LANES = STRETCH // 2
STEPB = 8

MESH = pl.DeviceIdType.MESH
epsilon = 1e-05
masked = -1e30
highest = lax.Precision.HIGHEST
f32 = jnp.float32
bf16 = jnp.bfloat16


def place():
    me = lax.axis_index("head")
    return lax.div(me, SIDE), lax.rem(me, SIDE)


def around(c, by):
    return lax.rem(c + by + SIDE, SIDE)


def coords(half):
    z, y = place()
    return (y, z) if half == 0 else (z, y)


def device(half, c1, c2):
    return c2 * SIDE + c1 if half == 0 else c1 * SIDE + c2


def piece(half, c1, c2):
    return pl.ds(pl.multiple_of(device(half, c1, c2) * SHARD + half * HALF, 16), HALF)


OFFSETS = (0, -1, 1, 2)
LEFT = pl.ds(0, LANES)
RIGHT = pl.ds(LANES, LANES)
FULL = pl.ds(0, STRETCH)


def remote(src, dst, send_sem, recv_sem, dev):
    return pltpu.make_async_remote_copy(
        src_ref=src, dst_ref=dst, send_sem=send_sem, recv_sem=recv_sem,
        device_id={"head": dev}, device_id_type=MESH,
    )


class Gather:
    def __init__(self, own, out, send_sems, recv_sems):
        self.own, self.out, self.ss, self.rs = own, out, send_sems, recv_sems
        self.sent = []

    def go(self, half, idx, src, c1, c2, lanes, to1, to2):
        dst = self.out.at[piece(half, c1, c2), lanes]
        copy = remote(src, dst, self.ss.at[half, idx], self.rs.at[half, idx], device(half, to1, to2))
        copy.start()
        self.sent.append(copy)

    def arrive(self, half, idx, c1, c2, lanes):
        where = self.out.at[piece(half, c1, c2), lanes]
        me1, me2 = coords(half)
        remote(where, where, self.ss.at[half, idx], self.rs.at[half, idx], device(half, around(me1, 1), me2)).wait_recv()

    def start(self):
        for axis in (1, 2):
            for half in (0, 1):
                c1, c2 = coords(half)
                src = self.own.at[pl.ds(half * HALF, HALF), FULL]
                if axis == 1:
                    self.go(half, 0, src, c1, c2, FULL, around(c1, 1), c2)
                    self.go(half, 1, src, c1, c2, FULL, around(c1, -1), c2)
                else:
                    self.go(half, 4, src, c1, c2, FULL, c1, around(c2, 1))
                    self.go(half, 5, src, c1, c2, FULL, c1, around(c2, -1))

    def second(self, half, k):
        c1, c2 = coords(half)
        o1 = around(c1, OFFSETS[k])
        src = self.out.at[piece(half, o1, c2), FULL]
        self.go(half, 4 + 4 * k, src, o1, c2, FULL, c1, around(c2, 1))
        self.go(half, 5 + 4 * k, src, o1, c2, FULL, c1, around(c2, -1))

    def first_near(self):
        for half in (0, 1):
            c1, c2 = coords(half)
            left = around(c1, -1)
            self.arrive(half, 0, left, c2, FULL)
            self.go(half, 2, self.out.at[piece(half, left, c2), LEFT], left, c2, LEFT, around(c1, 1), c2)
            self.second(half, 1)
        for half in (0, 1):
            c1, c2 = coords(half)
            right = around(c1, 1)
            self.arrive(half, 1, right, c2, FULL)
            self.go(half, 3, self.out.at[piece(half, right, c2), RIGHT], right, c2, RIGHT, around(c1, -1), c2)
            self.second(half, 2)

    def first_far(self):
        for half in (0, 1):
            c1, c2 = coords(half)
            far = around(c1, 2)
            self.arrive(half, 2, far, c2, LEFT)
            self.arrive(half, 3, far, c2, RIGHT)
            self.second(half, 3)

    def second_near(self, k):
        for half in (0, 1):
            c1, c2 = coords(half)
            o1 = around(c1, OFFSETS[k])
            for way in (0, 1):
                nb = around(c2, -1 if way == 0 else 1)
                to = around(c2, 1 if way == 0 else -1)
                lanes = LEFT if way == 0 else RIGHT
                self.arrive(half, 4 + 4 * k + way, o1, nb, FULL)
                self.go(half, 6 + 4 * k + way, self.out.at[piece(half, o1, nb), lanes], o1, nb, lanes, c1, to)

    def second_far(self, k):
        for half in (0, 1):
            c1, c2 = coords(half)
            o1 = around(c1, OFFSETS[k])
            far = around(c2, 2)
            self.arrive(half, 6 + 4 * k, o1, far, LEFT)
            self.arrive(half, 7 + 4 * k, o1, far, RIGHT)

    def run(self):
        self.start()
        self.first_near()
        self.second_near(0)
        self.first_far()
        for k in (1, 2, 3):
            self.second_near(k)
        for k in range(SIDE):
            self.second_far(k)

    def finish(self):
        for copy in self.sent:
            copy.wait_send()


GATHER_SEMS = [pltpu.SemaphoreType.DMA((2, 20)), pltpu.SemaphoreType.DMA((2, 20))]

SCATTER_SCRATCH = [
    pltpu.VMEM((D, STRETCH), bf16),
    pltpu.VMEM((2, SIDE, 2, HALF, LANES), bf16),
    pltpu.VMEM((2, SIDE, 2, HALF, STRETCH), bf16),
    pltpu.VMEM((2, SIDE, HALF, STRETCH), bf16),
    pltpu.VMEM((2, 2, HALF, LANES), bf16),
    pltpu.VMEM((2, 2, HALF, STRETCH), bf16),
    pltpu.SemaphoreType.DMA((2, 20)),
    pltpu.SemaphoreType.DMA((2, 20)),
]


class Scatter:
    def __init__(self, part, near1, full1, mid, near2, full2, send_sems, recv_sems):
        self.part, self.near1, self.full1, self.mid = part, near1, full1, mid
        self.near2, self.full2, self.ss, self.rs = near2, full2, send_sems, recv_sems
        self.sent = []

    def go(self, half, idx, src, dst, to1, to2):
        copy = remote(src, dst, self.ss.at[half, idx], self.rs.at[half, idx], device(half, to1, to2))
        copy.start()
        self.sent.append(copy)

    def arrive(self, half, idx, where):
        me1, me2 = coords(half)
        remote(where, where, self.ss.at[half, idx], self.rs.at[half, idx], device(half, around(me1, 1), me2)).wait_recv()

    def one(self, k):
        for half in (0, 1):
            c1, c2 = coords(half)
            o1 = around(c1, OFFSETS[k])
            rows = piece(half, o1, around(c2, 2))
            self.go(half, 4 * k, self.part.at[rows, LEFT], self.near1.at[half, k, 0], c1, around(c2, 1))
            self.go(half, 4 * k + 1, self.part.at[rows, RIGHT], self.near1.at[half, k, 1], c1, around(c2, -1))

    def two(self, k):
        for half in (0, 1):
            c1, c2 = coords(half)
            o1 = around(c1, OFFSETS[k])
            for way in (0, 1):
                to = around(c2, 1 if way == 0 else -1)
                lanes = LEFT if way == 0 else RIGHT
                rows = piece(half, o1, to)
                self.arrive(half, 4 * k + way, self.near1.at[half, k, way])
                mine = self.part[rows, lanes].astype(f32)
                self.part[rows, lanes] = (mine + self.near1[half, k, way].astype(f32)).astype(bf16)
                self.go(half, 4 * k + 2 + way, self.part.at[rows, FULL], self.full1.at[half, k, way], c1, to)

    def three(self, k):
        for half in (0, 1):
            c1, c2 = coords(half)
            o1 = around(c1, OFFSETS[k])
            self.arrive(half, 4 * k + 2, self.full1.at[half, k, 0])
            self.arrive(half, 4 * k + 3, self.full1.at[half, k, 1])
            if k:
                self.mid[half, k] = self.total(half, k).astype(bf16)
                if k == 3:
                    self.go(half, 16, self.mid.at[half, 3, :, LEFT], self.near2.at[half, 0], around(c1, 1), c2)
                    self.go(half, 17, self.mid.at[half, 3, :, RIGHT], self.near2.at[half, 1], around(c1, -1), c2)

    def total(self, half, k):
        c1, c2 = coords(half)
        rows = piece(half, around(c1, OFFSETS[k]), c2)
        return (
            self.part[rows, :].astype(f32)
            + self.full1[half, k, 0].astype(f32)
            + self.full1[half, k, 1].astype(f32)
        )

    def four(self, k):
        way = 0 if k == 2 else 1
        lanes = LEFT if way == 0 else RIGHT
        for half in (0, 1):
            c1, c2 = coords(half)
            self.arrive(half, 16 + way, self.near2.at[half, way])
            mine = self.mid[half, k, :, lanes].astype(f32)
            self.mid[half, k, :, lanes] = (mine + self.near2[half, way].astype(f32)).astype(bf16)
            self.go(half, 18 + way, self.mid.at[half, k], self.full2.at[half, way], around(c1, OFFSETS[k]), c2)

    def run(self):
        for k in (3, 2, 1, 0):
            self.one(k)
        for k in (3, 2, 1, 0):
            self.two(k)
        self.three(3)
        self.three(2)
        self.four(2)
        self.three(1)
        self.four(1)
        self.three(0)

    def result(self, half):
        self.arrive(half, 18, self.full2.at[half, 0])
        self.arrive(half, 19, self.full2.at[half, 1])
        return (
            self.total(half, 0)
            + self.full2[half, 0].astype(f32)
            + self.full2[half, 1].astype(f32)
        )

    def finish(self):
        for copy in self.sent:
            copy.wait_send()


def greet_heads():
    barrier = pltpu.get_barrier_semaphore()
    me = lax.axis_index("head")
    for by in range(1, HEADS):
        pl.semaphore_signal(
            barrier, inc=1, device_id={"head": lax.rem(me + by, HEADS)}, device_id_type=MESH
        )
    return barrier


def flat(row, count):
    turned = jnp.broadcast_to(row, (128, count)).T
    return jnp.concatenate([turned] * (STRETCH // 128), axis=1)


def column(table, start, count):
    rows = table.shape[0]
    entry = start + lax.broadcasted_iota(jnp.int32, (count, rows), 0)
    pick = (lax.shift_right_logical(entry, 7) == lax.broadcasted_iota(jnp.int32, (count, rows), 1))
    lines = jnp.dot(pick.astype(f32), table[...], precision=highest, preferred_element_type=f32)
    entry = start + lax.broadcasted_iota(jnp.int32, (count, 128), 0)
    keep = jnp.bitwise_and(entry, 127) == lax.broadcasted_iota(jnp.int32, (count, 128), 1)
    return jnp.sum(jnp.where(keep, lines, 0.0), axis=1, keepdims=True)


def send_sums(mine, peers, send_sems, recv_sems):
    me = lax.axis_index("head")
    out = []
    for by in range(1, HEADS):
        copy = remote(
            mine, peers.at[by - 1], send_sems.at[by - 1], recv_sems.at[by - 1],
            lax.rem(me + by, HEADS),
        )
        copy.start()
        out.append(copy)
    return out


def add_sums(mine, peers, out):
    total = mine[...]
    for by in range(1, HEADS):
        out[by - 1].wait_recv()
        total = total + peers[by - 1]
    return total


def silu(value):
    return value / (1.0 + jnp.exp(-value))


TN = (((0,), (0,)), ((), ()))
NT = (((1,), (1,)), ((), ()))
HL = 4


def products(weight, rows, part):
    width = 512

    def chunk(i, _):
        span = pl.ds(pl.multiple_of(i * width, width), width)
        part[span, :] = lax.dot_general(
            weight[:, span], rows, (((0,), (0,)), ((), ())), preferred_element_type=f32
        ).astype(bf16)
        return 0

    lax.fori_loop(0, D // width, chunk, 0)


def mix_kernel(gated, squares, weight, hidden, gain_sh, w_att, embed_all, embed_sq, next_out, proj_out,
               part, near1, full1, mid, near2, full2, s_send, s_recv,
               g_send, g_recv, peers, q_send, q_recv, sums, peers2, r_send, r_recv, rounded, watt, emb, wide,
               acc, local):
    loads = [
        pltpu.make_async_copy(embed_all, emb, local.at[0]),
        pltpu.make_async_copy(w_att, watt, local.at[1]),
    ]
    for copy in loads:
        copy.start()
    barrier = greet_heads()
    pl.semaphore_wait(barrier, HEADS - 1)
    me = lax.axis_index("head")
    group = lax.div(me, 8)
    spot = lax.rem(me, 8)
    out = []
    for by in range(1, 8):
        copy = remote(
            squares, peers.at[by - 1], q_send.at[by - 1], q_recv.at[by - 1],
            group * 8 + lax.rem(spot + by, 8),
        )
        copy.start()
        out.append(copy)
    total = squares[0:1, :]
    for by in range(1, 8):
        out[by - 1].wait_recv()
        total = total + peers[by - 1, 0:1, :]
    scale = lax.rsqrt(total * (1.0 / (MH // G * P_SIZE)) + epsilon)
    products(weight, (gated[...] * scale).astype(bf16), part)
    scatter = Scatter(part, near1, full1, mid, near2, full2, s_send, s_recv)
    for k in (3, 2, 1, 0):
        scatter.one(k)
    for copy in loads:
        copy.wait()

    def from_embed(i):
        acc[i * SHARD : (i + 1) * SHARD, :] = jnp.dot(
            watt[i * SHARD : (i + 1) * SHARD, D:], emb[...], preferred_element_type=f32
        )

    for k in (3, 2, 1, 0):
        scatter.two(k)
    from_embed(0)
    scatter.three(3)
    scatter.three(2)
    from_embed(1)
    scatter.four(2)
    scatter.three(1)
    scatter.four(1)
    scatter.three(0)
    from_embed(2)
    gain = column(gain_sh, me * SHARD, SHARD)
    mine = pl.ds(pl.multiple_of(me * SHARD, 16), SHARD)
    sq = jnp.zeros((1, STRETCH), f32)
    for half in (0, 1):
        rows = pl.ds(half * HALF, HALF)
        value = hidden[rows, :].astype(f32) + scatter.result(half)
        next_out[rows, :] = value
        value = value.astype(bf16).astype(f32)
        sq = sq + jnp.sum(value * value, axis=0, keepdims=True)
        rounded[rows, :] = (value * gain[half * HALF : (half + 1) * HALF]).astype(bf16)
    sums[...] = jnp.broadcast_to(sq, (8, STRETCH))
    gather = Gather(rounded, wide, g_send, g_recv)
    gather.start()
    sent = send_sums(sums, peers2, r_send, r_recv)
    wide[mine, :] = rounded[...]
    gather.first_near()
    gather.second_near(0)
    gather.first_far()
    for k in (1, 2, 3):
        gather.second_near(k)
    for k in range(SIDE):
        gather.second_far(k)
    total = add_sums(sums, peers2, sent)[0:1, :] + embed_sq[1:2, :]
    scale = lax.rsqrt(total * (0.5 / D) + epsilon)
    for i in range(3):
        rows = slice(i * SHARD, (i + 1) * SHARD)
        value = acc[rows, :] + jnp.dot(watt[rows, :D], wide[...], preferred_element_type=f32)
        proj_out[rows, :] = (value * scale).astype(bf16)
    gather.finish()
    scatter.finish()
    for copy in out + sent:
        copy.wait_send()


def mix_call(gated, squares, weight, hidden, gain_sh, w_att, embed_all, embed_sq):
    vmem = pl.BlockSpec(memory_space=pltpu.VMEM)
    anywhere = pl.BlockSpec(memory_space=pl.ANY)
    dma = pltpu.SemaphoreType.DMA
    return pl.pallas_call(
        mix_kernel,
        out_shape=(
            jax.ShapeDtypeStruct((SHARD, STRETCH), f32),
            jax.ShapeDtypeStruct((3 * HD, STRETCH), bf16),
        ),
        in_specs=[vmem] * 5 + [anywhere] * 2 + [vmem],
        out_specs=(vmem, vmem),
        scratch_shapes=SCATTER_SCRATCH + GATHER_SEMS + [
            pltpu.VMEM((7, 8, STRETCH), f32),
            dma((7,)),
            dma((7,)),
            pltpu.VMEM((8, STRETCH), f32),
            pltpu.VMEM((HEADS - 1, 8, STRETCH), f32),
            dma((HEADS - 1,)),
            dma((HEADS - 1,)),
            pltpu.VMEM((SHARD, STRETCH), bf16),
            pltpu.VMEM((3 * HD, 2 * D), bf16),
            pltpu.VMEM((D, STRETCH), bf16),
            pltpu.VMEM((D, STRETCH), bf16),
            pltpu.VMEM((3 * HD, STRETCH), f32),
            dma((2,)),
        ],
        compiler_params=pltpu.CompilerParams(
            collective_id=1, has_side_effects=True, vmem_limit_bytes=56 * 2**20
        ),
        name="mix_rows",
    )(gated, squares, weight, hidden, gain_sh, w_att, embed_all, embed_sq)


CHUNKS = 4
BLOCKS = 20


class Pool:
    def __init__(self, own, out, send_sems, recv_sems):
        self.own, self.out, self.ss, self.rs = own, out, send_sems, recv_sems
        seq = lax.axis_index("seq")
        self.x, self.core = lax.div(seq, 2), lax.rem(seq, 2)
        self.sent = []

    def slab(self, by, core, ch):
        per = BLOCKS // CHUNKS
        return self.out.at[pl.ds((around(self.x, by) * 2 + core) * BLOCKS + ch * per, per)]

    def copy(self, idx, src, dst, by, core):
        return pltpu.make_async_remote_copy(
            src_ref=src, dst_ref=dst, send_sem=self.ss.at[idx], recv_sem=self.rs.at[idx],
            device_id={"seq": around(self.x, by) * 2 + core}, device_id_type=MESH,
        )

    def go(self, idx, src, dst, by, core):
        copy = self.copy(idx, src, dst, by, core)
        copy.start()
        self.sent.append(copy)

    def arrive(self, idx, dst):
        self.copy(idx, dst, dst, 1, self.core).wait_recv()

    def start(self):
        per = BLOCKS // CHUNKS
        for near, far in ((0, 2), (1, 3), (2, 0), (3, 1)):
            for base, ch, by in ((0, near, 1), (4, far, -1)):
                self.go(base + ch, self.own.at[pl.ds(ch * per, per)], self.slab(0, self.core, ch), by, self.core)
        for ch in range(CHUNKS):
            self.go(12 + ch, self.own.at[pl.ds(ch * per, per)], self.slab(0, self.core, ch), 0, 1 - self.core)

    def share(self, j, by, ch):
        where = self.slab(by, self.core, ch)
        self.go(12 + 4 * j + ch, where, where, 0, 1 - self.core)

    def relay(self, ch):
        left = self.slab(-1, self.core, ch)
        right = self.slab(1, self.core, ch)
        if ch < 2:
            self.arrive(ch, left)
            self.go(8 + ch, left, left, 1, self.core)
            self.share(1, -1, ch)
        else:
            self.arrive(4 + ch, right)
            self.go(8 + ch, right, right, -1, self.core)
            self.share(2, 1, ch)

    def rest(self, ch):
        if ch < 2:
            self.arrive(4 + ch, self.slab(1, self.core, ch))
            self.share(2, 1, ch)
        else:
            self.arrive(ch, self.slab(-1, self.core, ch))
            self.share(1, -1, ch)

    def far(self, ch):
        self.arrive(8 + ch, self.slab(2, self.core, ch))
        self.share(3, 2, ch)

    def finish(self):
        for j, by in enumerate((0, -1, 1, 2)):
            for ch in range(CHUNKS):
                self.arrive(12 + 4 * j + ch, self.slab(by, 1 - self.core, ch))
        for copy in self.sent:
            copy.wait_send()


def front_kernel(hidden_in, embed_in, gain_in_in, gain_sh_in, states, tails, slots, w_in, w_gr, w_st, bias, decay,
                 skip, conv_in, mix_in, w_out_in, w_att, pool_in,
                 next_out, proj_out, final_out, pool_out,
                 hidden, embed, gain_in, gain_sh, conv_w, mix_g, weight,
                 wide, own_h, own_e, win, wgr, paired, grouped, sums, peers, stores, tail_all, lines, gained, watt,
                 emb, wide2, acc, squares, peers3, sums2, peers2, rounded,
                 part, near1, full1, mid, near2, full2, x_send, x_recv,
                 h_send, h_recv, e_send, e_recv, g_send, g_recv, q_send, q_recv, s_send, s_recv, t_send, t_recv,
                 u_send, u_recv, r_send, r_recv, p_send, p_recv, local, here):
    seq = lax.axis_index("seq")
    me = lax.axis_index("head")
    small = [
        pltpu.make_async_copy(src, dst, here.at[i])
        for i, (src, dst) in enumerate((
            (hidden_in, hidden), (gain_in_in, gain_in), (embed_in, embed), (gain_sh_in, gain_sh),
            (conv_in, conv_w), (mix_in, mix_g), (w_out_in, weight),
        ))
    ]
    for copy in small:
        copy.start()
    loads = [
        pltpu.make_async_copy(w_in, win, local.at[0]),
        pltpu.make_async_copy(w_gr, wgr, local.at[1]),
        pltpu.make_async_copy(states, stores.at[pl.ds(seq * 2, 2)], local.at[2]),
        pltpu.make_async_copy(tails, tail_all.at[seq], local.at[3]),
        pltpu.make_async_copy(w_att, watt, local.at[4]),
        pltpu.make_async_copy(pool_in, pool_out.at[pl.ds(seq * BLOCKS, BLOCKS)], local.at[5]),
    ]
    for copy in loads:
        copy.start()
    barrier = greet_heads()
    for by in range(1, SEQ):
        pl.semaphore_signal(
            barrier, inc=1, device_id={"seq": lax.rem(seq + by, SEQ)}, device_id_type=MESH
        )
    mine = pl.ds(pl.multiple_of(me * SHARD, 16), SHARD)
    small[0].wait()
    small[1].wait()
    value = hidden[...].astype(f32)
    sq_h = jnp.sum(value * value, axis=0, keepdims=True)
    ready = (value * column(gain_in, me * SHARD, SHARD)).astype(bf16)
    own_h[...] = ready
    wide[mine, :] = ready
    pl.semaphore_wait(barrier, HEADS - 1 + SEQ - 1)
    first = Gather(own_h, wide, h_send, h_recv)
    second = Gather(own_e, emb, e_send, e_recv)
    blocks = Pool(pool_in, pool_out, p_send, p_recv)
    first.start()
    for copy in small[2:]:
        copy.wait()
    value = embed[...].astype(f32)
    sq_e = jnp.sum(value * value, axis=0, keepdims=True)
    ready = (value * column(gain_sh, D + me * SHARD, SHARD)).astype(bf16)
    own_e[...] = ready
    emb[mine, :] = ready
    line = lax.broadcasted_iota(jnp.int32, (8, STRETCH), 0)
    sums[...] = jnp.where(line == 0, sq_h, jnp.where(line == 1, sq_e, 0.0))
    out = send_sums(sums, peers, q_send, q_recv)
    moved = []
    for by in range(1, SEQ):
        to = {"seq": lax.rem(seq + by, SEQ)}
        for src, dst, ss, rs in (
            (states, stores.at[pl.ds(seq * 2, 2)], s_send, s_recv), (tails, tail_all.at[seq], t_send, t_recv)
        ):
            copy = pltpu.make_async_remote_copy(
                src_ref=src, dst_ref=dst, send_sem=ss.at[by - 1], recv_sem=rs.at[by - 1],
                device_id=to, device_id_type=MESH,
            )
            copy.start()
            moved.append(copy)
    first.first_near()
    blocks.start()
    first.second_near(0)
    first.first_far()
    for k in (1, 2, 3):
        first.second_near(k)
    second.start()
    for k in range(SIDE):
        first.second_far(k)
    total = add_sums(sums, peers, out)
    embed_sq = total[1:2, :]
    scale = lax.rsqrt(total[0:1, :] * (1.0 / D) + epsilon)
    for copy in loads:
        copy.wait()

    def project(i, _):
        span = pl.ds(pl.multiple_of(i * 256, 256), 256)
        paired[span, :] = scale * lax.dot_general(win[:, span], wide[...], TN, preferred_element_type=f32)
        return 0

    lax.fori_loop(0, 2, project, 0)
    blocks.relay(0)
    blocks.relay(2)
    second.first_near()
    grouped[...] = scale * lax.dot_general(wgr[...], wide[...], TN, preferred_element_type=f32)
    raw = scale * jnp.dot(w_st[...], wide[...], preferred_element_type=f32)
    second.second_near(0)
    second.first_far()
    head = lax.broadcasted_iota(jnp.int32, (HL, STRETCH), 0)

    def by_head(ref):
        line = jnp.zeros((HL, STRETCH), f32)
        for i in range(HL):
            line = jnp.where(head == i, ref[i], line)
        return line

    raw = raw + by_head(bias)
    steps = jnp.maximum(raw, 0.0) + jnp.log1p(jnp.exp(-jnp.abs(raw)))
    cums = -by_head(decay) * steps
    lane = lax.broadcasted_iota(jnp.int32, (HL, STRETCH), 1)
    by = 1
    while by < STRETCH:
        cums = cums + jnp.where(lane >= by, pltpu.roll(cums, by, 1), 0.0)
        by *= 2
    turned = jnp.concatenate([cums, steps, jnp.zeros((128 - 2 * HL, STRETCH), f32)], axis=0).T
    group = lax.div(me, 8)
    b_proj = grouped[pl.ds(pl.multiple_of(group * NS, NS), NS), :]
    c_proj = grouped[pl.ds(pl.multiple_of(G * NS + group * NS, NS), NS), :]
    pairs = lax.dot_general(b_proj.astype(bf16), c_proj.astype(bf16), TN, preferred_element_type=f32)
    src = lax.broadcasted_iota(jnp.int32, pairs.shape, 0)
    dst = lax.broadcasted_iota(jnp.int32, pairs.shape, 1)
    pairs = jnp.where(src <= dst, pairs, 0.0)

    for copy in moved:
        copy.wait_recv()
    slot = slots[seq]
    for h in range(HL):
        for i in range(32):
            lines[pl.ds(h * 32 + i, 1), :] = stores[slot, h : h + 1, i * 128 : (i + 1) * 128]
    p_row = lax.broadcasted_iota(jnp.int32, (P_SIZE, 32), 0)
    p_col = lax.broadcasted_iota(jnp.int32, (P_SIZE, 32), 1)
    even = (p_row == 2 * p_col).astype(f32)
    odd = (p_row == 2 * p_col + 1).astype(f32)
    lane = lax.broadcasted_iota(jnp.int32, (HL * P_SIZE, 128), 1)
    before = jnp.zeros((HL * P_SIZE, 128), f32)
    for k in range(CONV - 1):
        row = tail_all[lax.div(slot, 2), k, pl.ds(lax.rem(slot, 2), 1), :]
        turn_row = jnp.broadcast_to(row, (128, HL * P_SIZE)).T
        before = jnp.where(lane == 125 + k, turn_row, before)
    taps = [flat(conv_w[k : k + 1, :], HL * P_SIZE) for k in range(CONV)]
    mixing = flat(mix_g[...], HL * P_SIZE)
    square = jnp.zeros((1, STRETCH), f32)
    for h in range(HL):
        chan = slice(h * P_SIZE, (h + 1) * P_SIZE)
        gate = paired[h * 128 : h * 128 + 64, :]
        signal = paired[h * 128 + 64 : h * 128 + 128, :]
        padded = jnp.concatenate([before[chan], signal], axis=1)
        conv = taps[CONV - 1][chan] * signal
        for back in range(1, CONV):
            conv = conv + taps[CONV - 1 - back][chan] * pltpu.roll(padded, back, 1)[:, 128:]
        active = silu(conv)
        cum = cums[h : h + 1, :]
        step = steps[h : h + 1, :]
        mix = jnp.exp(jnp.minimum(cum - turned[:, h : h + 1], 0.0)) * pairs * turned[:, HL + h : HL + h + 1]
        within = jnp.dot(active.astype(bf16), mix.astype(bf16), preferred_element_type=f32)
        rows = lines[h * 32 : (h + 1) * 32, :]
        init = jnp.dot(even, rows[:, :NS], precision=highest, preferred_element_type=f32)
        init = init + jnp.dot(odd, rows[:, NS:], precision=highest, preferred_element_type=f32)
        carried = jnp.dot(init, c_proj, precision=highest, preferred_element_type=f32) * jnp.exp(cum)
        gated = (within + carried + skip[h] * active) * silu(gate)
        square = square + jnp.sum(gated * gated, axis=0, keepdims=True)
        gained[chan, :] = gated * mixing[chan]
        last = cum[:, STRETCH - 1 :]
        to_end = jnp.exp(last - cum) * step
        final_out[chan, :] = jnp.exp(last) * init + lax.dot_general(
            active * to_end, b_proj, NT, precision=highest, preferred_element_type=f32
        )
        if h:
            second.second_near(h)
    squares[...] = jnp.broadcast_to(square, (8, STRETCH))
    group = lax.div(me, 8)
    spot = lax.rem(me, 8)
    met = []
    for by in range(1, 8):
        copy = remote(
            squares, peers3.at[by - 1], u_send.at[by - 1], u_recv.at[by - 1],
            group * 8 + lax.rem(spot + by, 8),
        )
        copy.start()
        met.append(copy)
    for k in range(SIDE):
        second.second_far(k)
    blocks.relay(1)
    blocks.relay(3)
    total = square
    for by in range(1, 8):
        met[by - 1].wait_recv()
        total = total + peers3[by - 1, 0:1, :]
    scale = lax.rsqrt(total * (1.0 / (MH // G * P_SIZE)) + epsilon)
    products(weight, (gained[...] * scale).astype(bf16), part)
    scatter = Scatter(part, near1, full1, mid, near2, full2, x_send, x_recv)
    for k in (3, 2, 1, 0):
        scatter.one(k)
    for k in (3, 2, 1, 0):
        scatter.two(k)
    acc[...] = jnp.dot(watt[:, D:], emb[...], preferred_element_type=f32)
    scatter.three(3)
    scatter.three(2)
    for ch in range(CHUNKS):
        blocks.rest(ch)
    scatter.four(2)
    scatter.three(1)
    scatter.four(1)
    scatter.three(0)
    gain = column(gain_sh, me * SHARD, SHARD)
    mine = pl.ds(pl.multiple_of(me * SHARD, 16), SHARD)
    sq = jnp.zeros((1, STRETCH), f32)
    for half in (0, 1):
        rows = pl.ds(half * HALF, HALF)
        value = hidden[rows, :].astype(f32) + scatter.result(half)
        next_out[rows, :] = value
        value = value.astype(bf16).astype(f32)
        sq = sq + jnp.sum(value * value, axis=0, keepdims=True)
        rounded[rows, :] = (value * gain[half * HALF : (half + 1) * HALF]).astype(bf16)
    sums2[...] = jnp.broadcast_to(sq, (8, STRETCH))
    gather = Gather(rounded, wide2, g_send, g_recv)
    gather.start()
    sent = send_sums(sums2, peers2, r_send, r_recv)
    wide2[mine, :] = rounded[...]
    gather.first_near()
    gather.second_near(0)
    gather.first_far()
    for k in (1, 2, 3):
        gather.second_near(k)
    for ch in range(CHUNKS):
        blocks.far(ch)
    for k in range(SIDE):
        gather.second_far(k)
    total = add_sums(sums2, peers2, sent)[0:1, :] + embed_sq
    scale = lax.rsqrt(total * (0.5 / D) + epsilon)
    value = acc[...] + jnp.dot(watt[:, :D], wide2[...], preferred_element_type=f32)
    proj_out[...] = (value * scale).astype(bf16)
    gather.finish()
    scatter.finish()
    blocks.finish()
    first.finish()
    second.finish()
    for copy in out + moved + met + sent:
        copy.wait_send()


def front_call(*args):
    anywhere = pl.BlockSpec(memory_space=pl.ANY)
    vmem = pl.BlockSpec(memory_space=pltpu.VMEM)
    smem = pl.BlockSpec(memory_space=pltpu.SMEM)
    dma = pltpu.SemaphoreType.DMA
    return pl.pallas_call(
        front_kernel,
        out_shape=(
            jax.ShapeDtypeStruct((SHARD, STRETCH), f32),
            jax.ShapeDtypeStruct((3 * HD, STRETCH), bf16),
            jax.ShapeDtypeStruct((HL * P_SIZE, NS), f32),
            jax.ShapeDtypeStruct((SEQ * BLOCKS, 2, HD, BLOCK), bf16),
        ),
        in_specs=[anywhere] * 6 + [smem] + [anywhere] * 2 + [vmem] + [smem] * 3 + [anywhere] * 5,
        out_specs=(vmem, vmem, vmem, anywhere),
        scratch_shapes=[
            pltpu.VMEM((SHARD, STRETCH), bf16),
            pltpu.VMEM((SHARD, STRETCH), bf16),
            pltpu.VMEM((D // 128, 128), f32),
            pltpu.VMEM((2 * D // 128, 128), f32),
            pltpu.VMEM((CONV, HL * P_SIZE), f32),
            pltpu.VMEM((1, HL * P_SIZE), f32),
            pltpu.VMEM((HL * P_SIZE, D), bf16),
            pltpu.VMEM((D, STRETCH), bf16),
            pltpu.VMEM((SHARD, STRETCH), bf16),
            pltpu.VMEM((SHARD, STRETCH), bf16),
            pltpu.VMEM((D, HL * 128), bf16),
            pltpu.VMEM((D, 2 * G * NS), bf16),
            pltpu.VMEM((HL * 128, STRETCH), f32),
            pltpu.VMEM((2 * G * NS, STRETCH), f32),
            pltpu.VMEM((8, STRETCH), f32),
            pltpu.VMEM((HEADS - 1, 8, STRETCH), f32),
            pltpu.VMEM((2 * SEQ, HL, P_SIZE * NS), f32),
            pltpu.VMEM((SEQ, CONV - 1, 2, HL * P_SIZE), f32),
            pltpu.VMEM((128, 128), f32),
            pltpu.VMEM((HL * P_SIZE, STRETCH), f32),
            pltpu.VMEM((3 * HD, 2 * D), bf16),
            pltpu.VMEM((D, STRETCH), bf16),
            pltpu.VMEM((D, STRETCH), bf16),
            pltpu.VMEM((3 * HD, STRETCH), f32),
            pltpu.VMEM((8, STRETCH), f32),
            pltpu.VMEM((7, 8, STRETCH), f32),
            pltpu.VMEM((8, STRETCH), f32),
            pltpu.VMEM((HEADS - 1, 8, STRETCH), f32),
            pltpu.VMEM((SHARD, STRETCH), bf16),
        ] + SCATTER_SCRATCH + GATHER_SEMS + GATHER_SEMS + GATHER_SEMS + [
            dma((HEADS - 1,)), dma((HEADS - 1,)),
            dma((SEQ - 1,)), dma((SEQ - 1,)),
            dma((SEQ - 1,)), dma((SEQ - 1,)),
            dma((7,)), dma((7,)),
            dma((HEADS - 1,)), dma((HEADS - 1,)),
            dma((28,)), dma((28,)),
            dma((6,)), dma((7,)),
        ],
        compiler_params=pltpu.CompilerParams(
            collective_id=0, has_side_effects=True, vmem_limit_bytes=60 * 2**20
        ),
        name="front_rows",
    )(*args)


def merge_kernel(attended, weight, before, out,
                 part, near1, full1, mid, near2, full2, s_send, s_recv):
    barrier = greet_heads()
    products(weight, attended[...], part)
    pl.semaphore_wait(barrier, HEADS - 1)
    scatter = Scatter(part, near1, full1, mid, near2, full2, s_send, s_recv)
    scatter.run()
    for half in (0, 1):
        rows = pl.ds(half * HALF, HALF)
        out[rows, :] = before[rows, :] + scatter.result(half)
    scatter.finish()


def merge_call(attended, weight, before):
    vmem = pl.BlockSpec(memory_space=pltpu.VMEM)
    return pl.pallas_call(
        merge_kernel,
        out_shape=jax.ShapeDtypeStruct((SHARD, STRETCH), f32),
        in_specs=[vmem] * 3,
        out_specs=vmem,
        scratch_shapes=SCATTER_SCRATCH,
        compiler_params=pltpu.CompilerParams(
            collective_id=2, has_side_effects=True, vmem_limit_bytes=40 * 2**20
        ),
        name="merge_rows",
    )(attended, weight, before)


def turn(value):
    return jnp.concatenate([value, jnp.zeros((256 - HD, STRETCH), f32)], axis=0).T[:, :HD]


def attend_kernel(table, lengths, projected, pool, out, held, sems, acc, top, total):
    seq = lax.axis_index("seq")
    scale = HD ** -0.5 * 1.4426950408889634
    span = STEPB * BLOCK
    limit = lengths[seq]
    blocks = lax.div(limit + BLOCK - 1, BLOCK)
    steps = lax.div(blocks + STEPB - 1, STEPB)

    def fetch(step, slot):
        return [
            pltpu.make_async_copy(
                pool.at[table[seq, step * STEPB + i]],
                held.at[slot, :, :, pl.ds(i * BLOCK, BLOCK)],
                sems.at[slot, i],
            )
            for i in range(STEPB)
        ]

    for copy in fetch(0, 0):
        copy.start()
    q = turn(projected[:HD, :].astype(f32)).astype(bf16)
    scores = jnp.dot(q, projected[HD : 2 * HD, :], preferred_element_type=f32)
    row = lax.broadcasted_iota(jnp.int32, scores.shape, 0)
    col = lax.broadcasted_iota(jnp.int32, scores.shape, 1)
    scores = jnp.where(row >= col, scores, masked)
    high = jnp.max(scores, axis=1, keepdims=True)
    weights = jnp.exp2((scores - high) * scale)
    top[...] = high
    total[...] = jnp.sum(weights, axis=1, keepdims=True)
    acc[...] = lax.dot_general(
        weights.astype(bf16), projected[2 * HD :, :], NT, preferred_element_type=f32
    )

    def step_body(step, _):
        slot = lax.rem(step, 2)

        @pl.when(step + 1 < steps)
        def _():
            for copy in fetch(step + 1, 1 - slot):
                copy.start()

        for copy in fetch(step, slot):
            copy.wait()
        scores = jnp.dot(q, held[slot, 0], preferred_element_type=f32)

        def rest(scores):
            old = top[...]
            high = jnp.maximum(old, jnp.max(scores, axis=1, keepdims=True))
            weights = jnp.exp2((scores - high) * scale)
            factor = jnp.exp2((old - high) * scale)
            top[...] = high
            total[...] = total[...] * factor + jnp.sum(weights, axis=1, keepdims=True)
            acc[...] = acc[...] * factor + lax.dot_general(
                weights.astype(bf16), held[slot, 1], NT, preferred_element_type=f32
            )

        @pl.when((step + 1) * span <= limit)
        def _():
            rest(scores)

        @pl.when((step + 1) * span > limit)
        def _():
            where = step * span + lax.broadcasted_iota(jnp.int32, scores.shape, 1)
            rest(jnp.where(where < limit, scores, masked))

        return 0

    lax.fori_loop(0, steps, step_body, 0)
    value = acc[...] / total[...]
    value = jnp.concatenate([value, jnp.zeros((STRETCH, 256 - HD), f32)], axis=1).T
    out[...] = value[:HD].astype(bf16)


def attend_call(table, lengths, projected, pool):
    vmem = pl.BlockSpec(memory_space=pltpu.VMEM)
    smem = pl.BlockSpec(memory_space=pltpu.SMEM)
    return pl.pallas_call(
        attend_kernel,
        out_shape=jax.ShapeDtypeStruct((HD, STRETCH), bf16),
        in_specs=[smem, smem, vmem, pl.BlockSpec(memory_space=pl.ANY)],
        out_specs=vmem,
        scratch_shapes=[
            pltpu.VMEM((2, 2, HD, STEPB * BLOCK), bf16),
            pltpu.SemaphoreType.DMA((2, STEPB)),
            pltpu.VMEM((STRETCH, HD), f32),
            pltpu.VMEM((STRETCH, 1), f32),
            pltpu.VMEM((STRETCH, 1), f32),
        ],
        compiler_params=pltpu.CompilerParams(vmem_limit_bytes=48 * 2**20),
        name="attend_rows",
    )(table, lengths, projected, pool)


def body(hidden, embedding, input_gain, w_input, w_groups, w_step, step_bias, decay_rate, skip_gain,
         conv_weight, mix_gain, w_output, state_store, conv_store, state_slot, prefix_len, block_table,
         shared_gain, w_attend, cache_pool, w_merge):
    heads_local = w_step.shape[1]
    hidden_next, projected, final_state, pool = front_call(
        hidden.T, embedding.T, input_gain.reshape(D // 128, 128), shared_gain.reshape(2 * D // 128, 128),
        state_store, conv_store.transpose(1, 0, 2).astype(f32), state_slot, w_input, w_groups, w_step.T,
        step_bias, decay_rate, skip_gain, conv_weight, mix_gain[None, :], w_output, w_attend.T,
        cache_pool.transpose(0, 1, 3, 2),
    )
    attended = attend_call(block_table, prefix_len, projected, pool)
    layer_output = merge_call(attended, w_merge, hidden_next)
    return (layer_output.T, final_state.reshape(1, heads_local, P_SIZE * NS))


def solution(mesh):
    return jax.shard_map(
        body,
        mesh=mesh,
        in_specs=(
            P("seq", "head"),
            P("seq", "head"),
            P(),
            P(None, "head"),
            P(),
            P(None, "head"),
            P("head"),
            P("head"),
            P("head"),
            P(None, "head"),
            P("head"),
            P("head", None),
            P("seq", "head", None),
            P("seq", None, "head"),
            P(),
            P(),
            P(),
            P(),
            P(None, "head"),
            P("seq", None, None, "head"),
            P("head", None),
        ),
        out_specs=(P("seq", "head"), P("seq", "head", None)),
        check_vma=False,
    )
```

```python
import functools

import jax
import jax.numpy as jnp
from jax import lax
from jax.experimental import pallas as pl
from jax.experimental.pallas import tpu as pltpu
from jax.sharding import PartitionSpec as P

D = 3584
MH = 64
P_SIZE = 64
NS = 64
G = 2
CONV = 4
HD = 224
STRETCH = 512
BLOCK = 128
MAXB = 64
SEQ = 8
SIDE = 4
HEADS = SIDE * SIDE
SHARD = D // HEADS
HALF = SHARD // 2
LANES = STRETCH // 2
STEPB = 8

MESH = pl.DeviceIdType.MESH
epsilon = 1e-05
masked = -1e30
highest = lax.Precision.HIGHEST
f32 = jnp.float32
bf16 = jnp.bfloat16


def place():
    me = lax.axis_index("head")
    return lax.div(me, SIDE), lax.rem(me, SIDE)


def around(c, by):
    return lax.rem(c + by + SIDE, SIDE)


def coords(half):
    z, y = place()
    return (y, z) if half == 0 else (z, y)


def device(half, c1, c2):
    return c2 * SIDE + c1 if half == 0 else c1 * SIDE + c2


def piece(half, c1, c2):
    return pl.ds(pl.multiple_of(device(half, c1, c2) * SHARD + half * HALF, 16), HALF)


OFFSETS = (0, -1, 1, 2)
LEFT = pl.ds(0, LANES)
RIGHT = pl.ds(LANES, LANES)
FULL = pl.ds(0, STRETCH)


def remote(src, dst, send_sem, recv_sem, dev):
    return pltpu.make_async_remote_copy(
        src_ref=src, dst_ref=dst, send_sem=send_sem, recv_sem=recv_sem,
        device_id={"head": dev}, device_id_type=MESH,
    )


class Gather:
    def __init__(self, own, out, send_sems, recv_sems):
        self.own, self.out, self.ss, self.rs = own, out, send_sems, recv_sems
        self.sent = []

    def go(self, half, idx, src, c1, c2, lanes, to1, to2):
        dst = self.out.at[piece(half, c1, c2), lanes]
        copy = remote(src, dst, self.ss.at[half, idx], self.rs.at[half, idx], device(half, to1, to2))
        copy.start()
        self.sent.append(copy)

    def arrive(self, half, idx, c1, c2, lanes):
        where = self.out.at[piece(half, c1, c2), lanes]
        me1, me2 = coords(half)
        remote(where, where, self.ss.at[half, idx], self.rs.at[half, idx], device(half, around(me1, 1), me2)).wait_recv()

    def start(self):
        for axis in (1, 2):
            for half in (0, 1):
                c1, c2 = coords(half)
                src = self.own.at[pl.ds(half * HALF, HALF), FULL]
                if axis == 1:
                    self.go(half, 0, src, c1, c2, FULL, around(c1, 1), c2)
                    self.go(half, 1, src, c1, c2, FULL, around(c1, -1), c2)
                else:
                    self.go(half, 4, src, c1, c2, FULL, c1, around(c2, 1))
                    self.go(half, 5, src, c1, c2, FULL, c1, around(c2, -1))

    def second(self, half, k):
        c1, c2 = coords(half)
        o1 = around(c1, OFFSETS[k])
        src = self.out.at[piece(half, o1, c2), FULL]
        self.go(half, 4 + 4 * k, src, o1, c2, FULL, c1, around(c2, 1))
        self.go(half, 5 + 4 * k, src, o1, c2, FULL, c1, around(c2, -1))

    def first_near(self):
        for half in (0, 1):
            c1, c2 = coords(half)
            left = around(c1, -1)
            self.arrive(half, 0, left, c2, FULL)
            self.go(half, 2, self.out.at[piece(half, left, c2), LEFT], left, c2, LEFT, around(c1, 1), c2)
            self.second(half, 1)
        for half in (0, 1):
            c1, c2 = coords(half)
            right = around(c1, 1)
            self.arrive(half, 1, right, c2, FULL)
            self.go(half, 3, self.out.at[piece(half, right, c2), RIGHT], right, c2, RIGHT, around(c1, -1), c2)
            self.second(half, 2)

    def first_far(self):
        for half in (0, 1):
            c1, c2 = coords(half)
            far = around(c1, 2)
            self.arrive(half, 2, far, c2, LEFT)
            self.arrive(half, 3, far, c2, RIGHT)
            self.second(half, 3)

    def second_near(self, k):
        for half in (0, 1):
            c1, c2 = coords(half)
            o1 = around(c1, OFFSETS[k])
            for way in (0, 1):
                nb = around(c2, -1 if way == 0 else 1)
                to = around(c2, 1 if way == 0 else -1)
                lanes = LEFT if way == 0 else RIGHT
                self.arrive(half, 4 + 4 * k + way, o1, nb, FULL)
                self.go(half, 6 + 4 * k + way, self.out.at[piece(half, o1, nb), lanes], o1, nb, lanes, c1, to)

    def second_far(self, k):
        for half in (0, 1):
            c1, c2 = coords(half)
            o1 = around(c1, OFFSETS[k])
            far = around(c2, 2)
            self.arrive(half, 6 + 4 * k, o1, far, LEFT)
            self.arrive(half, 7 + 4 * k, o1, far, RIGHT)

    def run(self):
        self.start()
        self.first_near()
        self.second_near(0)
        self.first_far()
        for k in (1, 2, 3):
            self.second_near(k)
        for k in range(SIDE):
            self.second_far(k)

    def finish(self):
        for copy in self.sent:
            copy.wait_send()


GATHER_SEMS = [pltpu.SemaphoreType.DMA((2, 20)), pltpu.SemaphoreType.DMA((2, 20))]

SCATTER_SCRATCH = [
    pltpu.VMEM((D, STRETCH), bf16),
    pltpu.VMEM((2, SIDE, 2, HALF, LANES), bf16),
    pltpu.VMEM((2, SIDE, 2, HALF, STRETCH), bf16),
    pltpu.VMEM((2, SIDE, HALF, STRETCH), bf16),
    pltpu.VMEM((2, 2, HALF, LANES), bf16),
    pltpu.VMEM((2, 2, HALF, STRETCH), bf16),
    pltpu.SemaphoreType.DMA((2, 20)),
    pltpu.SemaphoreType.DMA((2, 20)),
]


class Scatter:
    def __init__(self, part, near1, full1, mid, near2, full2, send_sems, recv_sems):
        self.part, self.near1, self.full1, self.mid = part, near1, full1, mid
        self.near2, self.full2, self.ss, self.rs = near2, full2, send_sems, recv_sems
        self.sent = []

    def go(self, half, idx, src, dst, to1, to2):
        copy = remote(src, dst, self.ss.at[half, idx], self.rs.at[half, idx], device(half, to1, to2))
        copy.start()
        self.sent.append(copy)

    def arrive(self, half, idx, where):
        me1, me2 = coords(half)
        remote(where, where, self.ss.at[half, idx], self.rs.at[half, idx], device(half, around(me1, 1), me2)).wait_recv()

    def one(self, k):
        for half in (0, 1):
            c1, c2 = coords(half)
            o1 = around(c1, OFFSETS[k])
            rows = piece(half, o1, around(c2, 2))
            self.go(half, 4 * k, self.part.at[rows, LEFT], self.near1.at[half, k, 0], c1, around(c2, 1))
            self.go(half, 4 * k + 1, self.part.at[rows, RIGHT], self.near1.at[half, k, 1], c1, around(c2, -1))

    def two(self, k):
        for half in (0, 1):
            c1, c2 = coords(half)
            o1 = around(c1, OFFSETS[k])
            for way in (0, 1):
                to = around(c2, 1 if way == 0 else -1)
                lanes = LEFT if way == 0 else RIGHT
                rows = piece(half, o1, to)
                self.arrive(half, 4 * k + way, self.near1.at[half, k, way])
                mine = self.part[rows, lanes].astype(f32)
                self.part[rows, lanes] = (mine + self.near1[half, k, way].astype(f32)).astype(bf16)
                self.go(half, 4 * k + 2 + way, self.part.at[rows, FULL], self.full1.at[half, k, way], c1, to)

    def three(self, k):
        for half in (0, 1):
            c1, c2 = coords(half)
            o1 = around(c1, OFFSETS[k])
            self.arrive(half, 4 * k + 2, self.full1.at[half, k, 0])
            self.arrive(half, 4 * k + 3, self.full1.at[half, k, 1])
            if k:
                self.mid[half, k] = self.total(half, k).astype(bf16)
                if k == 3:
                    self.go(half, 16, self.mid.at[half, 3, :, LEFT], self.near2.at[half, 0], around(c1, 1), c2)
                    self.go(half, 17, self.mid.at[half, 3, :, RIGHT], self.near2.at[half, 1], around(c1, -1), c2)

    def total(self, half, k):
        c1, c2 = coords(half)
        rows = piece(half, around(c1, OFFSETS[k]), c2)
        return (
            self.part[rows, :].astype(f32)
            + self.full1[half, k, 0].astype(f32)
            + self.full1[half, k, 1].astype(f32)
        )

    def four(self, k):
        way = 0 if k == 2 else 1
        lanes = LEFT if way == 0 else RIGHT
        for half in (0, 1):
            c1, c2 = coords(half)
            self.arrive(half, 16 + way, self.near2.at[half, way])
            mine = self.mid[half, k, :, lanes].astype(f32)
            self.mid[half, k, :, lanes] = (mine + self.near2[half, way].astype(f32)).astype(bf16)
            self.go(half, 18 + way, self.mid.at[half, k], self.full2.at[half, way], around(c1, OFFSETS[k]), c2)

    def run(self):
        for k in (3, 2, 1, 0):
            self.one(k)
        for k in (3, 2, 1, 0):
            self.two(k)
        self.three(3)
        self.three(2)
        self.four(2)
        self.three(1)
        self.four(1)
        self.three(0)

    def result(self, half):
        self.arrive(half, 18, self.full2.at[half, 0])
        self.arrive(half, 19, self.full2.at[half, 1])
        return (
            self.total(half, 0)
            + self.full2[half, 0].astype(f32)
            + self.full2[half, 1].astype(f32)
        )

    def finish(self):
        for copy in self.sent:
            copy.wait_send()


def greet_heads():
    barrier = pltpu.get_barrier_semaphore()
    me = lax.axis_index("head")
    for by in range(1, HEADS):
        pl.semaphore_signal(
            barrier, inc=1, device_id={"head": lax.rem(me + by, HEADS)}, device_id_type=MESH
        )
    return barrier


def flat(row, count):
    turned = jnp.broadcast_to(row, (128, count)).T
    return jnp.concatenate([turned] * (STRETCH // 128), axis=1)


def column(table, start, count):
    rows = table.shape[0]
    entry = start + lax.broadcasted_iota(jnp.int32, (count, rows), 0)
    pick = (lax.shift_right_logical(entry, 7) == lax.broadcasted_iota(jnp.int32, (count, rows), 1))
    lines = jnp.dot(pick.astype(f32), table[...], precision=highest, preferred_element_type=f32)
    entry = start + lax.broadcasted_iota(jnp.int32, (count, 128), 0)
    keep = jnp.bitwise_and(entry, 127) == lax.broadcasted_iota(jnp.int32, (count, 128), 1)
    return jnp.sum(jnp.where(keep, lines, 0.0), axis=1, keepdims=True)


def send_sums(mine, peers, send_sems, recv_sems):
    me = lax.axis_index("head")
    out = []
    for by in range(1, HEADS):
        copy = remote(
            mine, peers.at[by - 1], send_sems.at[by - 1], recv_sems.at[by - 1],
            lax.rem(me + by, HEADS),
        )
        copy.start()
        out.append(copy)
    return out


def add_sums(mine, peers, out):
    total = mine[...]
    for by in range(1, HEADS):
        out[by - 1].wait_recv()
        total = total + peers[by - 1]
    return total


def silu(value):
    return value / (1.0 + jnp.exp(-value))


TN = (((0,), (0,)), ((), ()))
NT = (((1,), (1,)), ((), ()))
HL = 4


def products(weight, rows, part):
    width = 512

    def chunk(i, _):
        span = pl.ds(pl.multiple_of(i * width, width), width)
        part[span, :] = lax.dot_general(
            weight[:, span], rows, (((0,), (0,)), ((), ())), preferred_element_type=f32
        ).astype(bf16)
        return 0

    lax.fori_loop(0, D // width, chunk, 0)


def mix_kernel(gated, squares, weight, hidden, gain_sh, w_att, embed_all, embed_sq, next_out, proj_out,
               part, near1, full1, mid, near2, full2, s_send, s_recv,
               g_send, g_recv, peers, q_send, q_recv, sums, peers2, r_send, r_recv, rounded, watt, emb, wide,
               acc, local):
    loads = [
        pltpu.make_async_copy(embed_all, emb, local.at[0]),
        pltpu.make_async_copy(w_att, watt, local.at[1]),
    ]
    for copy in loads:
        copy.start()
    barrier = greet_heads()
    pl.semaphore_wait(barrier, HEADS - 1)
    me = lax.axis_index("head")
    group = lax.div(me, 8)
    spot = lax.rem(me, 8)
    out = []
    for by in range(1, 8):
        copy = remote(
            squares, peers.at[by - 1], q_send.at[by - 1], q_recv.at[by - 1],
            group * 8 + lax.rem(spot + by, 8),
        )
        copy.start()
        out.append(copy)
    total = squares[0:1, :]
    for by in range(1, 8):
        out[by - 1].wait_recv()
        total = total + peers[by - 1, 0:1, :]
    scale = lax.rsqrt(total * (1.0 / (MH // G * P_SIZE)) + epsilon)
    products(weight, (gated[...] * scale).astype(bf16), part)
    scatter = Scatter(part, near1, full1, mid, near2, full2, s_send, s_recv)
    for k in (3, 2, 1, 0):
        scatter.one(k)
    for copy in loads:
        copy.wait()

    def from_embed(i):
        acc[i * SHARD : (i + 1) * SHARD, :] = jnp.dot(
            watt[i * SHARD : (i + 1) * SHARD, D:], emb[...], preferred_element_type=f32
        )

    for k in (3, 2, 1, 0):
        scatter.two(k)
    from_embed(0)
    scatter.three(3)
    scatter.three(2)
    from_embed(1)
    scatter.four(2)
    scatter.three(1)
    scatter.four(1)
    scatter.three(0)
    from_embed(2)
    gain = column(gain_sh, me * SHARD, SHARD)
    mine = pl.ds(pl.multiple_of(me * SHARD, 16), SHARD)
    sq = jnp.zeros((1, STRETCH), f32)
    for half in (0, 1):
        rows = pl.ds(half * HALF, HALF)
        value = hidden[rows, :].astype(f32) + scatter.result(half)
        next_out[rows, :] = value
        value = value.astype(bf16).astype(f32)
        sq = sq + jnp.sum(value * value, axis=0, keepdims=True)
        rounded[rows, :] = (value * gain[half * HALF : (half + 1) * HALF]).astype(bf16)
    sums[...] = jnp.broadcast_to(sq, (8, STRETCH))
    gather = Gather(rounded, wide, g_send, g_recv)
    gather.start()
    sent = send_sums(sums, peers2, r_send, r_recv)
    wide[mine, :] = rounded[...]
    gather.first_near()
    gather.second_near(0)
    gather.first_far()
    for k in (1, 2, 3):
        gather.second_near(k)
    for k in range(SIDE):
        gather.second_far(k)
    total = add_sums(sums, peers2, sent)[0:1, :] + embed_sq[1:2, :]
    scale = lax.rsqrt(total * (0.5 / D) + epsilon)
    for i in range(3):
        rows = slice(i * SHARD, (i + 1) * SHARD)
        value = acc[rows, :] + jnp.dot(watt[rows, :D], wide[...], preferred_element_type=f32)
        proj_out[rows, :] = (value * scale).astype(bf16)
    gather.finish()
    scatter.finish()
    for copy in out + sent:
        copy.wait_send()


def mix_call(gated, squares, weight, hidden, gain_sh, w_att, embed_all, embed_sq):
    vmem = pl.BlockSpec(memory_space=pltpu.VMEM)
    anywhere = pl.BlockSpec(memory_space=pl.ANY)
    dma = pltpu.SemaphoreType.DMA
    return pl.pallas_call(
        mix_kernel,
        out_shape=(
            jax.ShapeDtypeStruct((SHARD, STRETCH), f32),
            jax.ShapeDtypeStruct((3 * HD, STRETCH), bf16),
        ),
        in_specs=[vmem] * 5 + [anywhere] * 2 + [vmem],
        out_specs=(vmem, vmem),
        scratch_shapes=SCATTER_SCRATCH + GATHER_SEMS + [
            pltpu.VMEM((7, 8, STRETCH), f32),
            dma((7,)),
            dma((7,)),
            pltpu.VMEM((8, STRETCH), f32),
            pltpu.VMEM((HEADS - 1, 8, STRETCH), f32),
            dma((HEADS - 1,)),
            dma((HEADS - 1,)),
            pltpu.VMEM((SHARD, STRETCH), bf16),
            pltpu.VMEM((3 * HD, 2 * D), bf16),
            pltpu.VMEM((D, STRETCH), bf16),
            pltpu.VMEM((D, STRETCH), bf16),
            pltpu.VMEM((3 * HD, STRETCH), f32),
            dma((2,)),
        ],
        compiler_params=pltpu.CompilerParams(
            collective_id=1, has_side_effects=True, vmem_limit_bytes=56 * 2**20
        ),
        name="mix_rows",
    )(gated, squares, weight, hidden, gain_sh, w_att, embed_all, embed_sq)


CHUNKS = 4
BLOCKS = 20


class Pool:
    def __init__(self, own, out, send_sems, recv_sems):
        self.own, self.out, self.ss, self.rs = own, out, send_sems, recv_sems
        seq = lax.axis_index("seq")
        self.x, self.core = lax.div(seq, 2), lax.rem(seq, 2)
        self.sent = []

    def slab(self, by, core, ch):
        per = BLOCKS // CHUNKS
        return self.out.at[pl.ds((around(self.x, by) * 2 + core) * BLOCKS + ch * per, per)]

    def copy(self, idx, src, dst, by, core):
        return pltpu.make_async_remote_copy(
            src_ref=src, dst_ref=dst, send_sem=self.ss.at[idx], recv_sem=self.rs.at[idx],
            device_id={"seq": around(self.x, by) * 2 + core}, device_id_type=MESH,
        )

    def go(self, idx, src, dst, by, core):
        copy = self.copy(idx, src, dst, by, core)
        copy.start()
        self.sent.append(copy)

    def arrive(self, idx, dst):
        self.copy(idx, dst, dst, 1, self.core).wait_recv()

    def start(self):
        per = BLOCKS // CHUNKS
        for near, far in ((0, 2), (1, 3), (2, 0), (3, 1)):
            for base, ch, by in ((0, near, 1), (4, far, -1)):
                self.go(base + ch, self.own.at[pl.ds(ch * per, per)], self.slab(0, self.core, ch), by, self.core)
        for ch in range(CHUNKS):
            self.go(12 + ch, self.own.at[pl.ds(ch * per, per)], self.slab(0, self.core, ch), 0, 1 - self.core)

    def share(self, j, by, ch):
        where = self.slab(by, self.core, ch)
        self.go(12 + 4 * j + ch, where, where, 0, 1 - self.core)

    def relay(self, ch):
        left = self.slab(-1, self.core, ch)
        right = self.slab(1, self.core, ch)
        if ch < 2:
            self.arrive(ch, left)
            self.go(8 + ch, left, left, 1, self.core)
            self.share(1, -1, ch)
        else:
            self.arrive(4 + ch, right)
            self.go(8 + ch, right, right, -1, self.core)
            self.share(2, 1, ch)

    def rest(self, ch):
        if ch < 2:
            self.arrive(4 + ch, self.slab(1, self.core, ch))
            self.share(2, 1, ch)
        else:
            self.arrive(ch, self.slab(-1, self.core, ch))
            self.share(1, -1, ch)

    def far(self, ch):
        self.arrive(8 + ch, self.slab(2, self.core, ch))
        self.share(3, 2, ch)

    def finish(self):
        for j, by in enumerate((0, -1, 1, 2)):
            for ch in range(CHUNKS):
                self.arrive(12 + 4 * j + ch, self.slab(by, 1 - self.core, ch))
        for copy in self.sent:
            copy.wait_send()


def front_kernel(hidden_in, embed_in, gain_in_in, gain_sh_in, states, tails, slots, w_in, w_gr, w_st, bias, decay,
                 skip, conv_in, mix_in, w_out_in, w_att, pool_in,
                 next_out, proj_out, final_out, pool_out,
                 hidden, embed, gain_in, gain_sh, conv_w, mix_g, weight,
                 wide, own_h, own_e, win, wgr, paired, grouped, sums, peers, stores, tail_all, lines, gained, watt,
                 emb, wide2, acc, squares, peers3, sums2, peers2, rounded,
                 part, near1, full1, mid, near2, full2, x_send, x_recv,
                 h_send, h_recv, e_send, e_recv, g_send, g_recv, q_send, q_recv, s_send, s_recv, t_send, t_recv,
                 u_send, u_recv, r_send, r_recv, p_send, p_recv, local, here):
    seq = lax.axis_index("seq")
    me = lax.axis_index("head")
    small = [
        pltpu.make_async_copy(src, dst, here.at[i])
        for i, (src, dst) in enumerate((
            (hidden_in, hidden), (gain_in_in, gain_in), (embed_in, embed), (gain_sh_in, gain_sh),
            (conv_in, conv_w), (mix_in, mix_g), (w_out_in, weight),
        ))
    ]
    for copy in small:
        copy.start()
    loads = [
        pltpu.make_async_copy(w_in, win, local.at[0]),
        pltpu.make_async_copy(w_gr, wgr, local.at[1]),
        pltpu.make_async_copy(states, stores.at[pl.ds(seq * 2, 2)], local.at[2]),
        pltpu.make_async_copy(tails, tail_all.at[seq], local.at[3]),
        pltpu.make_async_copy(w_att, watt, local.at[4]),
        pltpu.make_async_copy(pool_in, pool_out.at[pl.ds(seq * BLOCKS, BLOCKS)], local.at[5]),
    ]
    for copy in loads:
        copy.start()
    barrier = greet_heads()
    for by in range(1, SEQ):
        pl.semaphore_signal(
            barrier, inc=1, device_id={"seq": lax.rem(seq + by, SEQ)}, device_id_type=MESH
        )
    mine = pl.ds(pl.multiple_of(me * SHARD, 16), SHARD)
    small[0].wait()
    small[1].wait()
    value = hidden[...].astype(f32)
    sq_h = jnp.sum(value * value, axis=0, keepdims=True)
    ready = (value * column(gain_in, me * SHARD, SHARD)).astype(bf16)
    own_h[...] = ready
    wide[mine, :] = ready
    pl.semaphore_wait(barrier, HEADS - 1 + SEQ - 1)
    first = Gather(own_h, wide, h_send, h_recv)
    second = Gather(own_e, emb, e_send, e_recv)
    blocks = Pool(pool_in, pool_out, p_send, p_recv)
    first.start()
    for copy in small[2:]:
        copy.wait()
    value = embed[...].astype(f32)
    sq_e = jnp.sum(value * value, axis=0, keepdims=True)
    ready = (value * column(gain_sh, D + me * SHARD, SHARD)).astype(bf16)
    own_e[...] = ready
    emb[mine, :] = ready
    line = lax.broadcasted_iota(jnp.int32, (8, STRETCH), 0)
    sums[...] = jnp.where(line == 0, sq_h, jnp.where(line == 1, sq_e, 0.0))
    out = send_sums(sums, peers, q_send, q_recv)
    moved = []
    for by in range(1, SEQ):
        to = {"seq": lax.rem(seq + by, SEQ)}
        for src, dst, ss, rs in (
            (states, stores.at[pl.ds(seq * 2, 2)], s_send, s_recv), (tails, tail_all.at[seq], t_send, t_recv)
        ):
            copy = pltpu.make_async_remote_copy(
                src_ref=src, dst_ref=dst, send_sem=ss.at[by - 1], recv_sem=rs.at[by - 1],
                device_id=to, device_id_type=MESH,
            )
            copy.start()
            moved.append(copy)
    first.first_near()
    blocks.start()
    first.second_near(0)
    first.first_far()
    for k in (1, 2, 3):
        first.second_near(k)
    second.start()
    for k in range(SIDE):
        first.second_far(k)
    total = add_sums(sums, peers, out)
    embed_sq = total[1:2, :]
    scale = lax.rsqrt(total[0:1, :] * (1.0 / D) + epsilon)
    for copy in loads[:4]:
        copy.wait()

    def project(i, _):
        span = pl.ds(pl.multiple_of(i * 256, 256), 256)
        paired[span, :] = scale * lax.dot_general(win[:, span], wide[...], TN, preferred_element_type=f32)
        return 0

    lax.fori_loop(0, 2, project, 0)
    blocks.relay(0)
    blocks.relay(2)
    second.first_near()
    grouped[...] = scale * lax.dot_general(wgr[...], wide[...], TN, preferred_element_type=f32)
    raw = scale * jnp.dot(w_st[...], wide[...], preferred_element_type=f32)
    second.second_near(0)
    second.first_far()
    head = lax.broadcasted_iota(jnp.int32, (HL, STRETCH), 0)

    def by_head(ref):
        line = jnp.zeros((HL, STRETCH), f32)
        for i in range(HL):
            line = jnp.where(head == i, ref[i], line)
        return line

    raw = raw + by_head(bias)
    steps = jnp.maximum(raw, 0.0) + jnp.log1p(jnp.exp(-jnp.abs(raw)))
    cums = -by_head(decay) * steps
    lane = lax.broadcasted_iota(jnp.int32, (HL, STRETCH), 1)
    by = 1
    while by < STRETCH:
        cums = cums + jnp.where(lane >= by, pltpu.roll(cums, by, 1), 0.0)
        by *= 2
    turned = jnp.concatenate([cums, steps, jnp.zeros((128 - 2 * HL, STRETCH), f32)], axis=0).T
    group = lax.div(me, 8)
    b_proj = grouped[pl.ds(pl.multiple_of(group * NS, NS), NS), :]
    c_proj = grouped[pl.ds(pl.multiple_of(G * NS + group * NS, NS), NS), :]
    pairs = lax.dot_general(b_proj.astype(bf16), c_proj.astype(bf16), TN, preferred_element_type=f32)
    src = lax.broadcasted_iota(jnp.int32, pairs.shape, 0)
    dst = lax.broadcasted_iota(jnp.int32, pairs.shape, 1)
    pairs = jnp.where(src <= dst, pairs, 0.0)

    for copy in moved:
        copy.wait_recv()
    slot = slots[seq]
    for h in range(HL):
        for i in range(32):
            lines[pl.ds(h * 32 + i, 1), :] = stores[slot, h : h + 1, i * 128 : (i + 1) * 128]
    p_row = lax.broadcasted_iota(jnp.int32, (P_SIZE, 32), 0)
    p_col = lax.broadcasted_iota(jnp.int32, (P_SIZE, 32), 1)
    even = (p_row == 2 * p_col).astype(f32)
    odd = (p_row == 2 * p_col + 1).astype(f32)
    lane = lax.broadcasted_iota(jnp.int32, (HL * P_SIZE, 128), 1)
    before = jnp.zeros((HL * P_SIZE, 128), f32)
    for k in range(CONV - 1):
        row = tail_all[lax.div(slot, 2), k, pl.ds(lax.rem(slot, 2), 1), :]
        turn_row = jnp.broadcast_to(row, (128, HL * P_SIZE)).T
        before = jnp.where(lane == 125 + k, turn_row, before)
    taps = [flat(conv_w[k : k + 1, :], HL * P_SIZE) for k in range(CONV)]
    mixing = flat(mix_g[...], HL * P_SIZE)
    square = jnp.zeros((1, STRETCH), f32)
    for h in range(HL):
        chan = slice(h * P_SIZE, (h + 1) * P_SIZE)
        gate = paired[h * 128 : h * 128 + 64, :]
        signal = paired[h * 128 + 64 : h * 128 + 128, :]
        padded = jnp.concatenate([before[chan], signal], axis=1)
        conv = taps[CONV - 1][chan] * signal
        for back in range(1, CONV):
            conv = conv + taps[CONV - 1 - back][chan] * pltpu.roll(padded, back, 1)[:, 128:]
        active = silu(conv)
        cum = cums[h : h + 1, :]
        step = steps[h : h + 1, :]
        mix = jnp.exp(jnp.minimum(cum - turned[:, h : h + 1], 0.0)) * pairs * turned[:, HL + h : HL + h + 1]
        within = jnp.dot(active.astype(bf16), mix.astype(bf16), preferred_element_type=f32)
        rows = lines[h * 32 : (h + 1) * 32, :]
        init = jnp.dot(even, rows[:, :NS], precision=highest, preferred_element_type=f32)
        init = init + jnp.dot(odd, rows[:, NS:], precision=highest, preferred_element_type=f32)
        carried = jnp.dot(init, c_proj, precision=highest, preferred_element_type=f32) * jnp.exp(cum)
        gated = (within + carried + skip[h] * active) * silu(gate)
        square = square + jnp.sum(gated * gated, axis=0, keepdims=True)
        gained[chan, :] = gated * mixing[chan]
        last = cum[:, STRETCH - 1 :]
        to_end = jnp.exp(last - cum) * step
        final_out[chan, :] = jnp.exp(last) * init + lax.dot_general(
            active * to_end, b_proj, NT, precision=highest, preferred_element_type=f32
        )
        if h:
            second.second_near(h)
    squares[...] = jnp.broadcast_to(square, (8, STRETCH))
    group = lax.div(me, 8)
    spot = lax.rem(me, 8)
    met = []
    for by in range(1, 8):
        copy = remote(
            squares, peers3.at[by - 1], u_send.at[by - 1], u_recv.at[by - 1],
            group * 8 + lax.rem(spot + by, 8),
        )
        copy.start()
        met.append(copy)
    for k in range(SIDE):
        second.second_far(k)
    blocks.relay(1)
    blocks.relay(3)
    total = square
    for by in range(1, 8):
        met[by - 1].wait_recv()
        total = total + peers3[by - 1, 0:1, :]
    scale = lax.rsqrt(total * (1.0 / (MH // G * P_SIZE)) + epsilon)
    products(weight, (gained[...] * scale).astype(bf16), part)
    scatter = Scatter(part, near1, full1, mid, near2, full2, x_send, x_recv)
    for k in (3, 2, 1, 0):
        scatter.one(k)
    for k in (3, 2, 1, 0):
        scatter.two(k)
    loads[4].wait()
    acc[...] = jnp.dot(watt[:, D:], emb[...], preferred_element_type=f32)
    scatter.three(3)
    scatter.three(2)
    for ch in range(CHUNKS):
        blocks.rest(ch)
    scatter.four(2)
    scatter.three(1)
    scatter.four(1)
    scatter.three(0)
    gain = column(gain_sh, me * SHARD, SHARD)
    mine = pl.ds(pl.multiple_of(me * SHARD, 16), SHARD)
    sq = jnp.zeros((1, STRETCH), f32)
    for half in (0, 1):
        rows = pl.ds(half * HALF, HALF)
        value = hidden[rows, :].astype(f32) + scatter.result(half)
        next_out[rows, :] = value
        value = value.astype(bf16).astype(f32)
        sq = sq + jnp.sum(value * value, axis=0, keepdims=True)
        rounded[rows, :] = (value * gain[half * HALF : (half + 1) * HALF]).astype(bf16)
    sums2[...] = jnp.broadcast_to(sq, (8, STRETCH))
    gather = Gather(rounded, wide2, g_send, g_recv)
    gather.start()
    sent = send_sums(sums2, peers2, r_send, r_recv)
    wide2[mine, :] = rounded[...]
    gather.first_near()
    gather.second_near(0)
    gather.first_far()
    for k in (1, 2, 3):
        gather.second_near(k)
    for ch in range(CHUNKS):
        blocks.far(ch)
    for k in range(SIDE):
        gather.second_far(k)
    total = add_sums(sums2, peers2, sent)[0:1, :] + embed_sq
    scale = lax.rsqrt(total * (0.5 / D) + epsilon)
    value = acc[...] + jnp.dot(watt[:, :D], wide2[...], preferred_element_type=f32)
    proj_out[...] = (value * scale).astype(bf16)
    gather.finish()
    scatter.finish()
    loads[5].wait()
    blocks.finish()
    first.finish()
    second.finish()
    for copy in out + moved + met + sent:
        copy.wait_send()


def front_call(*args):
    anywhere = pl.BlockSpec(memory_space=pl.ANY)
    vmem = pl.BlockSpec(memory_space=pltpu.VMEM)
    smem = pl.BlockSpec(memory_space=pltpu.SMEM)
    dma = pltpu.SemaphoreType.DMA
    return pl.pallas_call(
        front_kernel,
        out_shape=(
            jax.ShapeDtypeStruct((SHARD, STRETCH), f32),
            jax.ShapeDtypeStruct((3 * HD, STRETCH), bf16),
            jax.ShapeDtypeStruct((HL * P_SIZE, NS), f32),
            jax.ShapeDtypeStruct((SEQ * BLOCKS, 2, HD, BLOCK), bf16),
        ),
        in_specs=[anywhere] * 6 + [smem] + [anywhere] * 2 + [vmem] + [smem] * 3 + [anywhere] * 5,
        out_specs=(vmem, vmem, vmem, anywhere),
        scratch_shapes=[
            pltpu.VMEM((SHARD, STRETCH), bf16),
            pltpu.VMEM((SHARD, STRETCH), bf16),
            pltpu.VMEM((D // 128, 128), f32),
            pltpu.VMEM((2 * D // 128, 128), f32),
            pltpu.VMEM((CONV, HL * P_SIZE), f32),
            pltpu.VMEM((1, HL * P_SIZE), f32),
            pltpu.VMEM((HL * P_SIZE, D), bf16),
            pltpu.VMEM((D, STRETCH), bf16),
            pltpu.VMEM((SHARD, STRETCH), bf16),
            pltpu.VMEM((SHARD, STRETCH), bf16),
            pltpu.VMEM((D, HL * 128), bf16),
            pltpu.VMEM((D, 2 * G * NS), bf16),
            pltpu.VMEM((HL * 128, STRETCH), f32),
            pltpu.VMEM((2 * G * NS, STRETCH), f32),
            pltpu.VMEM((8, STRETCH), f32),
            pltpu.VMEM((HEADS - 1, 8, STRETCH), f32),
            pltpu.VMEM((2 * SEQ, HL, P_SIZE * NS), f32),
            pltpu.VMEM((SEQ, CONV - 1, 2, HL * P_SIZE), f32),
            pltpu.VMEM((128, 128), f32),
            pltpu.VMEM((HL * P_SIZE, STRETCH), f32),
            pltpu.VMEM((3 * HD, 2 * D), bf16),
            pltpu.VMEM((D, STRETCH), bf16),
            pltpu.VMEM((D, STRETCH), bf16),
            pltpu.VMEM((3 * HD, STRETCH), f32),
            pltpu.VMEM((8, STRETCH), f32),
            pltpu.VMEM((7, 8, STRETCH), f32),
            pltpu.VMEM((8, STRETCH), f32),
            pltpu.VMEM((HEADS - 1, 8, STRETCH), f32),
            pltpu.VMEM((SHARD, STRETCH), bf16),
        ] + SCATTER_SCRATCH + GATHER_SEMS + GATHER_SEMS + GATHER_SEMS + [
            dma((HEADS - 1,)), dma((HEADS - 1,)),
            dma((SEQ - 1,)), dma((SEQ - 1,)),
            dma((SEQ - 1,)), dma((SEQ - 1,)),
            dma((7,)), dma((7,)),
            dma((HEADS - 1,)), dma((HEADS - 1,)),
            dma((28,)), dma((28,)),
            dma((6,)), dma((7,)),
        ],
        compiler_params=pltpu.CompilerParams(
            collective_id=0, has_side_effects=True, vmem_limit_bytes=60 * 2**20
        ),
        name="front_rows",
    )(*args)


def merge_kernel(attended, weight, before, out,
                 part, near1, full1, mid, near2, full2, s_send, s_recv):
    barrier = greet_heads()
    products(weight, attended[...], part)
    pl.semaphore_wait(barrier, HEADS - 1)
    scatter = Scatter(part, near1, full1, mid, near2, full2, s_send, s_recv)
    scatter.run()
    for half in (0, 1):
        rows = pl.ds(half * HALF, HALF)
        out[rows, :] = before[rows, :] + scatter.result(half)
    scatter.finish()


def merge_call(attended, weight, before):
    vmem = pl.BlockSpec(memory_space=pltpu.VMEM)
    return pl.pallas_call(
        merge_kernel,
        out_shape=jax.ShapeDtypeStruct((SHARD, STRETCH), f32),
        in_specs=[vmem] * 3,
        out_specs=vmem,
        scratch_shapes=SCATTER_SCRATCH,
        compiler_params=pltpu.CompilerParams(
            collective_id=2, has_side_effects=True, vmem_limit_bytes=40 * 2**20
        ),
        name="merge_rows",
    )(attended, weight, before)


def turn(value):
    return jnp.concatenate([value, jnp.zeros((256 - HD, STRETCH), f32)], axis=0).T[:, :HD]


def attend_kernel(table, lengths, projected, pool, out, held, sems, acc, top, total):
    seq = lax.axis_index("seq")
    scale = HD ** -0.5 * 1.4426950408889634
    span = STEPB * BLOCK
    limit = lengths[seq]
    blocks = lax.div(limit + BLOCK - 1, BLOCK)
    steps = lax.div(blocks + STEPB - 1, STEPB)

    def fetch(step, slot):
        return [
            pltpu.make_async_copy(
                pool.at[table[seq, step * STEPB + i]],
                held.at[slot, :, :, pl.ds(i * BLOCK, BLOCK)],
                sems.at[slot, i],
            )
            for i in range(STEPB)
        ]

    for copy in fetch(0, 0):
        copy.start()
    q = turn(projected[:HD, :].astype(f32)).astype(bf16)
    scores = jnp.dot(q, projected[HD : 2 * HD, :], preferred_element_type=f32)
    row = lax.broadcasted_iota(jnp.int32, scores.shape, 0)
    col = lax.broadcasted_iota(jnp.int32, scores.shape, 1)
    scores = jnp.where(row >= col, scores, masked)
    high = jnp.max(scores, axis=1, keepdims=True)
    weights = jnp.exp2((scores - high) * scale)
    top[...] = high
    total[...] = jnp.sum(weights, axis=1, keepdims=True)
    acc[...] = lax.dot_general(
        weights.astype(bf16), projected[2 * HD :, :], NT, preferred_element_type=f32
    )

    def step_body(step, _):
        slot = lax.rem(step, 2)

        @pl.when(step + 1 < steps)
        def _():
            for copy in fetch(step + 1, 1 - slot):
                copy.start()

        for copy in fetch(step, slot):
            copy.wait()
        scores = jnp.dot(q, held[slot, 0], preferred_element_type=f32)

        def rest(scores):
            old = top[...]
            high = jnp.maximum(old, jnp.max(scores, axis=1, keepdims=True))
            weights = jnp.exp2((scores - high) * scale)
            factor = jnp.exp2((old - high) * scale)
            top[...] = high
            total[...] = total[...] * factor + jnp.sum(weights, axis=1, keepdims=True)
            acc[...] = acc[...] * factor + lax.dot_general(
                weights.astype(bf16), held[slot, 1], NT, preferred_element_type=f32
            )

        @pl.when((step + 1) * span <= limit)
        def _():
            rest(scores)

        @pl.when((step + 1) * span > limit)
        def _():
            where = step * span + lax.broadcasted_iota(jnp.int32, scores.shape, 1)
            rest(jnp.where(where < limit, scores, masked))

        return 0

    lax.fori_loop(0, steps, step_body, 0)
    value = acc[...] / total[...]
    value = jnp.concatenate([value, jnp.zeros((STRETCH, 256 - HD), f32)], axis=1).T
    out[...] = value[:HD].astype(bf16)


def attend_call(table, lengths, projected, pool):
    vmem = pl.BlockSpec(memory_space=pltpu.VMEM)
    smem = pl.BlockSpec(memory_space=pltpu.SMEM)
    return pl.pallas_call(
        attend_kernel,
        out_shape=jax.ShapeDtypeStruct((HD, STRETCH), bf16),
        in_specs=[smem, smem, vmem, pl.BlockSpec(memory_space=pl.ANY)],
        out_specs=vmem,
        scratch_shapes=[
            pltpu.VMEM((2, 2, HD, STEPB * BLOCK), bf16),
            pltpu.SemaphoreType.DMA((2, STEPB)),
            pltpu.VMEM((STRETCH, HD), f32),
            pltpu.VMEM((STRETCH, 1), f32),
            pltpu.VMEM((STRETCH, 1), f32),
        ],
        compiler_params=pltpu.CompilerParams(vmem_limit_bytes=48 * 2**20),
        name="attend_rows",
    )(table, lengths, projected, pool)


def body(hidden, embedding, input_gain, w_input, w_groups, w_step, step_bias, decay_rate, skip_gain,
         conv_weight, mix_gain, w_output, state_store, conv_store, state_slot, prefix_len, block_table,
         shared_gain, w_attend, cache_pool, w_merge):
    heads_local = w_step.shape[1]
    hidden_next, projected, final_state, pool = front_call(
        hidden.T, embedding.T, input_gain.reshape(D // 128, 128), shared_gain.reshape(2 * D // 128, 128),
        state_store, conv_store.transpose(1, 0, 2).astype(f32), state_slot, w_input, w_groups, w_step.T,
        step_bias, decay_rate, skip_gain, conv_weight, mix_gain[None, :], w_output, w_attend.T,
        cache_pool.transpose(0, 1, 3, 2),
    )
    attended = attend_call(block_table, prefix_len, projected, pool)
    layer_output = merge_call(attended, w_merge, hidden_next)
    return (layer_output.T, final_state.reshape(1, heads_local, P_SIZE * NS))


def solution(mesh):
    return jax.shard_map(
        body,
        mesh=mesh,
        in_specs=(
            P("seq", "head"),
            P("seq", "head"),
            P(),
            P(None, "head"),
            P(),
            P(None, "head"),
            P("head"),
            P("head"),
            P("head"),
            P(None, "head"),
            P("head"),
            P("head", None),
            P("seq", "head", None),
            P("seq", None, "head"),
            P(),
            P(),
            P(),
            P(),
            P(None, "head"),
            P("seq", None, None, "head"),
            P("head", None),
        ),
        out_specs=(P("seq", "head"), P("seq", "head", None)),
        check_vma=False,
    )
```

```python
import functools

import jax
import jax.numpy as jnp
from jax import lax
from jax.experimental import pallas as pl
from jax.experimental.pallas import tpu as pltpu
from jax.sharding import PartitionSpec as P

D = 3584
MH = 64
P_SIZE = 64
NS = 64
G = 2
CONV = 4
HD = 224
STRETCH = 512
BLOCK = 128
MAXB = 64
SEQ = 8
SIDE = 4
HEADS = SIDE * SIDE
SHARD = D // HEADS
HALF = SHARD // 2
LANES = STRETCH // 2
STEPB = 8

MESH = pl.DeviceIdType.MESH
epsilon = 1e-05
masked = -1e30
highest = lax.Precision.HIGHEST
f32 = jnp.float32
bf16 = jnp.bfloat16


def place():
    me = lax.axis_index("head")
    return lax.div(me, SIDE), lax.rem(me, SIDE)


def around(c, by):
    return lax.rem(c + by + SIDE, SIDE)


def coords(half):
    z, y = place()
    return (y, z) if half == 0 else (z, y)


def device(half, c1, c2):
    return c2 * SIDE + c1 if half == 0 else c1 * SIDE + c2


def piece(half, c1, c2):
    return pl.ds(pl.multiple_of(device(half, c1, c2) * SHARD + half * HALF, 16), HALF)


OFFSETS = (0, -1, 1, 2)
LEFT = pl.ds(0, LANES)
RIGHT = pl.ds(LANES, LANES)
FULL = pl.ds(0, STRETCH)


def remote(src, dst, send_sem, recv_sem, dev):
    return pltpu.make_async_remote_copy(
        src_ref=src, dst_ref=dst, send_sem=send_sem, recv_sem=recv_sem,
        device_id={"head": dev}, device_id_type=MESH,
    )


class Gather:
    def __init__(self, own, out, send_sems, recv_sems):
        self.own, self.out, self.ss, self.rs = own, out, send_sems, recv_sems
        self.sent = []

    def go(self, half, idx, src, c1, c2, lanes, to1, to2):
        dst = self.out.at[piece(half, c1, c2), lanes]
        copy = remote(src, dst, self.ss.at[half, idx], self.rs.at[half, idx], device(half, to1, to2))
        copy.start()
        self.sent.append(copy)

    def arrive(self, half, idx, c1, c2, lanes):
        where = self.out.at[piece(half, c1, c2), lanes]
        me1, me2 = coords(half)
        remote(where, where, self.ss.at[half, idx], self.rs.at[half, idx], device(half, around(me1, 1), me2)).wait_recv()

    def start(self):
        for axis in (1, 2):
            for half in (0, 1):
                c1, c2 = coords(half)
                src = self.own.at[pl.ds(half * HALF, HALF), FULL]
                if axis == 1:
                    self.go(half, 0, src, c1, c2, FULL, around(c1, 1), c2)
                    self.go(half, 1, src, c1, c2, FULL, around(c1, -1), c2)
                else:
                    self.go(half, 4, src, c1, c2, FULL, c1, around(c2, 1))
                    self.go(half, 5, src, c1, c2, FULL, c1, around(c2, -1))

    def second(self, half, k):
        c1, c2 = coords(half)
        o1 = around(c1, OFFSETS[k])
        src = self.out.at[piece(half, o1, c2), FULL]
        self.go(half, 4 + 4 * k, src, o1, c2, FULL, c1, around(c2, 1))
        self.go(half, 5 + 4 * k, src, o1, c2, FULL, c1, around(c2, -1))

    def first_near(self):
        for half in (0, 1):
            c1, c2 = coords(half)
            left = around(c1, -1)
            self.arrive(half, 0, left, c2, FULL)
            self.go(half, 2, self.out.at[piece(half, left, c2), LEFT], left, c2, LEFT, around(c1, 1), c2)
            self.second(half, 1)
        for half in (0, 1):
            c1, c2 = coords(half)
            right = around(c1, 1)
            self.arrive(half, 1, right, c2, FULL)
            self.go(half, 3, self.out.at[piece(half, right, c2), RIGHT], right, c2, RIGHT, around(c1, -1), c2)
            self.second(half, 2)

    def first_far(self):
        for half in (0, 1):
            c1, c2 = coords(half)
            far = around(c1, 2)
            self.arrive(half, 2, far, c2, LEFT)
            self.arrive(half, 3, far, c2, RIGHT)
            self.second(half, 3)

    def second_near(self, k, halves=(0, 1)):
        for half in halves:
            c1, c2 = coords(half)
            o1 = around(c1, OFFSETS[k])
            for way in (0, 1):
                nb = around(c2, -1 if way == 0 else 1)
                to = around(c2, 1 if way == 0 else -1)
                lanes = LEFT if way == 0 else RIGHT
                self.arrive(half, 4 + 4 * k + way, o1, nb, FULL)
                self.go(half, 6 + 4 * k + way, self.out.at[piece(half, o1, nb), lanes], o1, nb, lanes, c1, to)

    def second_far(self, k, halves=(0, 1)):
        for half in halves:
            c1, c2 = coords(half)
            o1 = around(c1, OFFSETS[k])
            far = around(c2, 2)
            self.arrive(half, 6 + 4 * k, o1, far, LEFT)
            self.arrive(half, 7 + 4 * k, o1, far, RIGHT)

    def run(self, use, between):
        self.first_near()
        self.second_near(0)
        self.first_far()
        self.second_near(1)
        self.second_far(0, (1,))
        use(0)
        self.second_near(2)
        self.second_near(3)
        between()
        self.second_far(1, (1,))
        use(-1)
        self.second_far(2, (1,))
        use(1)
        self.second_far(3, (1,))
        for k in range(SIDE):
            self.second_far(k, (0,))
        use(2)

    def finish(self):
        for copy in self.sent:
            copy.wait_send()


GATHER_SEMS = [pltpu.SemaphoreType.DMA((2, 20)), pltpu.SemaphoreType.DMA((2, 20))]

SCATTER_SCRATCH = [
    pltpu.VMEM((D, STRETCH), bf16),
    pltpu.VMEM((2, SIDE, 2, HALF, LANES), bf16),
    pltpu.VMEM((2, SIDE, 2, HALF, STRETCH), bf16),
    pltpu.VMEM((2, SIDE, HALF, STRETCH), bf16),
    pltpu.VMEM((2, 2, HALF, LANES), bf16),
    pltpu.VMEM((2, 2, HALF, STRETCH), bf16),
    pltpu.SemaphoreType.DMA((2, 20)),
    pltpu.SemaphoreType.DMA((2, 20)),
]


class Scatter:
    def __init__(self, part, near1, full1, mid, near2, full2, send_sems, recv_sems):
        self.part, self.near1, self.full1, self.mid = part, near1, full1, mid
        self.near2, self.full2, self.ss, self.rs = near2, full2, send_sems, recv_sems
        self.sent = []

    def go(self, half, idx, src, dst, to1, to2):
        copy = remote(src, dst, self.ss.at[half, idx], self.rs.at[half, idx], device(half, to1, to2))
        copy.start()
        self.sent.append(copy)

    def arrive(self, half, idx, where):
        me1, me2 = coords(half)
        remote(where, where, self.ss.at[half, idx], self.rs.at[half, idx], device(half, around(me1, 1), me2)).wait_recv()

    def one(self, k, halves):
        for half in halves:
            c1, c2 = coords(half)
            o1 = around(c1, OFFSETS[k])
            rows = piece(half, o1, around(c2, 2))
            self.go(half, 4 * k, self.part.at[rows, LEFT], self.near1.at[half, k, 0], c1, around(c2, 1))
            self.go(half, 4 * k + 1, self.part.at[rows, RIGHT], self.near1.at[half, k, 1], c1, around(c2, -1))

    def two(self, k):
        for half in (0, 1):
            c1, c2 = coords(half)
            o1 = around(c1, OFFSETS[k])
            for way in (0, 1):
                to = around(c2, 1 if way == 0 else -1)
                lanes = LEFT if way == 0 else RIGHT
                rows = piece(half, o1, to)
                self.arrive(half, 4 * k + way, self.near1.at[half, k, way])
                mine = self.part[rows, lanes].astype(f32)
                self.part[rows, lanes] = (mine + self.near1[half, k, way].astype(f32)).astype(bf16)
                self.go(half, 4 * k + 2 + way, self.part.at[rows, FULL], self.full1.at[half, k, way], c1, to)

    def three(self, k):
        for half in (0, 1):
            c1, c2 = coords(half)
            o1 = around(c1, OFFSETS[k])
            self.arrive(half, 4 * k + 2, self.full1.at[half, k, 0])
            self.arrive(half, 4 * k + 3, self.full1.at[half, k, 1])
            if k:
                self.mid[half, k] = self.total(half, k).astype(bf16)
                if k == 3:
                    self.go(half, 16, self.mid.at[half, 3, :, LEFT], self.near2.at[half, 0], around(c1, 1), c2)
                    self.go(half, 17, self.mid.at[half, 3, :, RIGHT], self.near2.at[half, 1], around(c1, -1), c2)

    def total(self, half, k):
        c1, c2 = coords(half)
        rows = piece(half, around(c1, OFFSETS[k]), c2)
        return (
            self.part[rows, :].astype(f32)
            + self.full1[half, k, 0].astype(f32)
            + self.full1[half, k, 1].astype(f32)
        )

    def four(self, k):
        way = 0 if k == 2 else 1
        lanes = LEFT if way == 0 else RIGHT
        for half in (0, 1):
            c1, c2 = coords(half)
            self.arrive(half, 16 + way, self.near2.at[half, way])
            mine = self.mid[half, k, :, lanes].astype(f32)
            self.mid[half, k, :, lanes] = (mine + self.near2[half, way].astype(f32)).astype(bf16)
            self.go(half, 18 + way, self.mid.at[half, k], self.full2.at[half, way], around(c1, OFFSETS[k]), c2)

    def run(self, weight, rows, early=(), late=()):
        for by in (2, -1, 1, 0):
            products(weight, rows, self.part, by)
        for k in (3, 2, 1, 0):
            self.one(k, (0, 1))
        for step in early:
            step()
        self.two(3)
        self.two(2)
        self.two(1)
        self.three(3)
        self.two(0)
        for step in late:
            step()
        self.three(2)
        self.four(2)
        self.three(1)
        self.four(1)
        self.three(0)

    def result(self, half):
        self.arrive(half, 18, self.full2.at[half, 0])
        self.arrive(half, 19, self.full2.at[half, 1])
        return (
            self.total(half, 0)
            + self.full2[half, 0].astype(f32)
            + self.full2[half, 1].astype(f32)
        )

    def finish(self):
        for copy in self.sent:
            copy.wait_send()


def greet_heads():
    barrier = pltpu.get_barrier_semaphore()
    me = lax.axis_index("head")
    for by in range(1, HEADS):
        pl.semaphore_signal(
            barrier, inc=1, device_id={"head": lax.rem(me + by, HEADS)}, device_id_type=MESH
        )
    return barrier


def flat(row, count):
    turned = jnp.broadcast_to(row, (128, count)).T
    return jnp.concatenate([turned] * (STRETCH // 128), axis=1)


def column(table, start, count):
    rows = table.shape[0]
    entry = start + lax.broadcasted_iota(jnp.int32, (count, rows), 0)
    pick = (lax.shift_right_logical(entry, 7) == lax.broadcasted_iota(jnp.int32, (count, rows), 1))
    lines = jnp.dot(pick.astype(f32), table[...], precision=highest, preferred_element_type=f32)
    entry = start + lax.broadcasted_iota(jnp.int32, (count, 128), 0)
    keep = jnp.bitwise_and(entry, 127) == lax.broadcasted_iota(jnp.int32, (count, 128), 1)
    return jnp.sum(jnp.where(keep, lines, 0.0), axis=1, keepdims=True)


def send_sums(mine, peers, send_sems, recv_sems):
    me = lax.axis_index("head")
    out = []
    for by in range(1, HEADS):
        copy = remote(
            mine, peers.at[by - 1], send_sems.at[by - 1], recv_sems.at[by - 1],
            lax.rem(me + by, HEADS),
        )
        copy.start()
        out.append(copy)
    return out


def add_sums(mine, peers, out):
    total = mine[...]
    for by in range(1, HEADS):
        out[by - 1].wait_recv()
        total = total + peers[by - 1]
    return total


def silu(value):
    return value / (1.0 + jnp.exp(-value))


TN = (((0,), (0,)), ((), ()))
NT = (((1,), (1,)), ((), ()))
HL = 4


ROW = SIDE * SHARD


def row_of(by):
    return pl.ds(pl.multiple_of(around(place()[0], by) * ROW, 128), ROW)


def products(weight, rows, part, by):
    span = row_of(by)
    part[span, :] = lax.dot_general(
        weight[:, span], rows, TN, preferred_element_type=f32
    ).astype(bf16)


CHUNKS = 4
BLOCKS = 20


class Pool:
    def __init__(self, own, out, send_sems, recv_sems):
        self.own, self.out, self.ss, self.rs = own, out, send_sems, recv_sems
        seq = lax.axis_index("seq")
        self.x, self.core = lax.div(seq, 2), lax.rem(seq, 2)
        self.sent = []

    def slab(self, by, ch):
        per = BLOCKS // CHUNKS
        return self.out.at[pl.ds(around(self.x, by) * BLOCKS + ch * per, per)]

    def copy(self, idx, src, dst, by):
        return pltpu.make_async_remote_copy(
            src_ref=src, dst_ref=dst, send_sem=self.ss.at[idx], recv_sem=self.rs.at[idx],
            device_id={"seq": around(self.x, by) * 2 + self.core}, device_id_type=MESH,
        )

    def go(self, idx, src, dst, by):
        copy = self.copy(idx, src, dst, by)
        copy.start()
        self.sent.append(copy)

    def arrive(self, idx, dst):
        self.copy(idx, dst, dst, 1).wait_recv()

    def spread(self, right, left):
        per = BLOCKS // CHUNKS
        for base, ch, by in ((0, right, 1), (4, left, -1)):
            self.go(base + ch, self.own.at[pl.ds(ch * per, per)], self.slab(0, ch), by)

    def relay(self, ch):
        way = -1 if ch < 2 else 1
        where = self.slab(way, ch)
        self.arrive(ch if ch < 2 else 4 + ch, where)
        self.go(8 + ch, where, where, -way)

    def finish(self):
        for ch in range(CHUNKS):
            if ch < 2:
                self.arrive(4 + ch, self.slab(1, ch))
            else:
                self.arrive(ch, self.slab(-1, ch))
            self.arrive(8 + ch, self.slab(2, ch))
        for copy in self.sent:
            copy.wait_send()


def front_kernel(hidden_in, embed_in, gain_in_in, gain_sh_in, states, tails, slots, w_in, w_gr, w_st, bias, decay,
                 skip, conv_in, mix_in, w_out_in, w_att, pool_in,
                 next_out, proj_out, final_out, pool_out, other_out,
                 hidden, embed, gain_in, gain_sh, conv_w, mix_g, weight,
                 wide, own_h, own_e, win, wgr, paired, grouped, sums, peers, stores, tail_all, lines, gained, watt,
                 emb, wide2, acc, squares, peers3, sums2, peers2, rounded,
                 part, near1, full1, mid, near2, full2, x_send, x_recv,
                 h_send, h_recv, e_send, e_recv, g_send, g_recv, q_send, q_recv, s_send, s_recv, t_send, t_recv,
                 u_send, u_recv, r_send, r_recv, p_send, p_recv, local, here, raws, mine_q, v_send, v_recv):
    seq = lax.axis_index("seq")
    me = lax.axis_index("head")
    small = [
        pltpu.make_async_copy(src, dst, here.at[i])
        for i, (src, dst) in enumerate((
            (hidden_in, hidden), (gain_in_in, gain_in), (embed_in, embed), (gain_sh_in, gain_sh),
            (conv_in, conv_w), (mix_in, mix_g), (w_out_in, weight),
        ))
    ]
    for copy in small:
        copy.start()
    loads = [
        pltpu.make_async_copy(w_in, win, local.at[0]),
        pltpu.make_async_copy(w_gr, wgr, local.at[1]),
        pltpu.make_async_copy(states, stores.at[pl.ds(seq * 2, 2)], local.at[2]),
        pltpu.make_async_copy(tails, tail_all.at[seq], local.at[3]),
        pltpu.make_async_copy(w_att, watt, local.at[4]),
        pltpu.make_async_copy(pool_in, pool_out.at[pl.ds(lax.div(seq, 2) * BLOCKS, BLOCKS)], local.at[5]),
    ]
    for copy in loads:
        copy.start()
    barrier = greet_heads()
    for by in range(1, SEQ):
        pl.semaphore_signal(
            barrier, inc=1, device_id={"seq": lax.rem(seq + by, SEQ)}, device_id_type=MESH
        )
    mine = pl.ds(pl.multiple_of(me * SHARD, 16), SHARD)
    small[0].wait()
    small[1].wait()
    value = hidden[...].astype(f32)
    sq_h = jnp.sum(value * value, axis=0, keepdims=True)
    ready = (value * column(gain_in, me * SHARD, SHARD)).astype(bf16)
    own_h[...] = ready
    wide[mine, :] = ready
    pl.semaphore_wait(barrier, HEADS - 1 + SEQ - 1)
    first = Gather(own_h, wide, h_send, h_recv)
    second = Gather(own_e, emb, e_send, e_recv)
    blocks = Pool(pool_in, pool_out, p_send, p_recv)
    first.start()
    for copy in small[2:]:
        copy.wait()
    value = embed[...].astype(f32)
    sq_e = jnp.sum(value * value, axis=0, keepdims=True)
    ready = (value * column(gain_sh, D + me * SHARD, SHARD)).astype(bf16)
    own_e[...] = ready
    emb[mine, :] = ready
    line = lax.broadcasted_iota(jnp.int32, (8, STRETCH), 0)
    sums[...] = jnp.where(line == 0, sq_h, jnp.where(line == 1, sq_e, 0.0))
    out = send_sums(sums, peers, q_send, q_recv)
    x, core = lax.div(seq, 2), lax.rem(seq, 2)
    held = (
        (states, stores, lambda at: stores.at[pl.ds(at * 2, 2)], s_send, s_recv),
        (tails, tail_all, lambda at: tail_all.at[at], t_send, t_recv),
    )
    moved = []

    def send_state(idx, src, dst, ss, rs, to):
        copy = pltpu.make_async_remote_copy(
            src_ref=src, dst_ref=dst, send_sem=ss.at[idx], recv_sem=rs.at[idx],
            device_id={"seq": to}, device_id_type=MESH,
        )
        copy.start()
        moved.append(copy)

    for src, _, at, ss, rs in held:
        for by in range(1, SIDE):
            send_state(by - 1, src, at(seq), ss, rs, around(x, by) * 2 + core)
        send_state(3, src, at(seq), ss, rs, x * 2 + 1 - core)

    def pass_states():
        for _, _, at, ss, rs in held:
            for by in range(1, SIDE):
                where = at(around(x, -by) * 2 + core)
                pltpu.make_async_remote_copy(
                    src_ref=where, dst_ref=where, send_sem=ss.at[by - 1], recv_sem=rs.at[by - 1],
                    device_id={"seq": x * 2 + 1 - core}, device_id_type=MESH,
                ).wait_recv()
                send_state(3 + by, where, where, ss, rs, x * 2 + 1 - core)

    def wait_states():
        for _, _, at, ss, rs in held:
            for by in range(SIDE):
                where = at(around(x, -by) * 2 + 1 - core)
                pltpu.make_async_remote_copy(
                    src_ref=where, dst_ref=where, send_sem=ss.at[3 + by], recv_sem=rs.at[3 + by],
                    device_id={"seq": x * 2 + 1 - core}, device_id_type=MESH,
                ).wait_recv()

    blocks.spread(0, 2)
    paired[...] = jnp.zeros_like(paired)
    grouped[...] = jnp.zeros_like(grouped)
    raws[...] = jnp.zeros_like(raws)
    for copy in loads[:2]:
        copy.wait()

    def project(by):
        span = row_of(by)
        rows = wide[span, :]
        paired[...] += lax.dot_general(win[span, :], rows, TN, preferred_element_type=f32)
        grouped[...] += lax.dot_general(wgr[span, :], rows, TN, preferred_element_type=f32)
        raws[...] += jnp.dot(w_st[:, span], rows, preferred_element_type=f32)

    def between():
        second.start()
        pass_states()
        blocks.spread(1, 3)
        blocks.relay(0)
        blocks.relay(2)
        blocks.spread(2, 0)

    first.run(project, between)
    total = add_sums(sums, peers, out)
    embed_sq = total[1:2, :]
    scale = lax.rsqrt(total[0:1, :] * (1.0 / D) + epsilon)
    raw = raws[...] * scale
    head = lax.broadcasted_iota(jnp.int32, (HL, STRETCH), 0)

    def by_head(ref):
        line = jnp.zeros((HL, STRETCH), f32)
        for i in range(HL):
            line = jnp.where(head == i, ref[i], line)
        return line

    raw = raw + by_head(bias)
    steps = jnp.maximum(raw, 0.0) + jnp.log1p(jnp.exp(-jnp.abs(raw)))
    cums = -by_head(decay) * steps
    lane = lax.broadcasted_iota(jnp.int32, (HL, STRETCH), 1)
    by = 1
    while by < STRETCH:
        cums = cums + jnp.where(lane >= by, pltpu.roll(cums, by, 1), 0.0)
        by *= 2
    turned = jnp.concatenate([cums, steps, jnp.zeros((128 - 2 * HL, STRETCH), f32)], axis=0).T
    group = lax.div(me, 8)
    b_proj = scale * grouped[pl.ds(pl.multiple_of(group * NS, NS), NS), :]
    c_proj = scale * grouped[pl.ds(pl.multiple_of(G * NS + group * NS, NS), NS), :]
    pairs = lax.dot_general(b_proj.astype(bf16), c_proj.astype(bf16), TN, preferred_element_type=f32)
    src = lax.broadcasted_iota(jnp.int32, pairs.shape, 0)
    dst = lax.broadcasted_iota(jnp.int32, pairs.shape, 1)
    pairs = jnp.where(src <= dst, pairs, 0.0)

    for copy in loads[2:4]:
        copy.wait()
    wait_states()
    slot = slots[seq]
    for h in range(HL):
        for i in range(32):
            lines[pl.ds(h * 32 + i, 1), :] = stores[slot, h : h + 1, i * 128 : (i + 1) * 128]
    p_row = lax.broadcasted_iota(jnp.int32, (P_SIZE, 32), 0)
    p_col = lax.broadcasted_iota(jnp.int32, (P_SIZE, 32), 1)
    even = (p_row == 2 * p_col).astype(f32)
    odd = (p_row == 2 * p_col + 1).astype(f32)
    lane = lax.broadcasted_iota(jnp.int32, (HL * P_SIZE, 128), 1)
    before = jnp.zeros((HL * P_SIZE, 128), f32)
    for k in range(CONV - 1):
        row = tail_all[lax.div(slot, 2), k, pl.ds(lax.rem(slot, 2), 1), :]
        turn_row = jnp.broadcast_to(row, (128, HL * P_SIZE)).T
        before = jnp.where(lane == 125 + k, turn_row, before)
    taps = [flat(conv_w[k : k + 1, :], HL * P_SIZE) for k in range(CONV)]
    mixing = flat(mix_g[...], HL * P_SIZE)
    second.first_near()
    square = jnp.zeros((1, STRETCH), f32)
    for h in range(HL):
        chan = slice(h * P_SIZE, (h + 1) * P_SIZE)
        gate = scale * paired[h * 128 : h * 128 + 64, :]
        signal = scale * paired[h * 128 + 64 : h * 128 + 128, :]
        padded = jnp.concatenate([before[chan], signal], axis=1)
        conv = taps[CONV - 1][chan] * signal
        for back in range(1, CONV):
            conv = conv + taps[CONV - 1 - back][chan] * pltpu.roll(padded, back, 1)[:, 128:]
        active = silu(conv)
        cum = cums[h : h + 1, :]
        step = steps[h : h + 1, :]
        mix = jnp.exp(jnp.minimum(cum - turned[:, h : h + 1], 0.0)) * pairs * turned[:, HL + h : HL + h + 1]
        within = jnp.dot(active.astype(bf16), mix.astype(bf16), preferred_element_type=f32)
        rows = lines[h * 32 : (h + 1) * 32, :]
        init = jnp.dot(even, rows[:, :NS], precision=highest, preferred_element_type=f32)
        init = init + jnp.dot(odd, rows[:, NS:], precision=highest, preferred_element_type=f32)
        carried = jnp.dot(init, c_proj, precision=highest, preferred_element_type=f32) * jnp.exp(cum)
        gated = (within + carried + skip[h] * active) * silu(gate)
        square = square + jnp.sum(gated * gated, axis=0, keepdims=True)
        gained[chan, :] = gated * mixing[chan]
        last = cum[:, STRETCH - 1 :]
        to_end = jnp.exp(last - cum) * step
        final_out[chan, :] = jnp.exp(last) * init + lax.dot_general(
            active * to_end, b_proj, NT, precision=highest, preferred_element_type=f32
        )
        if h == 1:
            second.second_near(0)
    squares[...] = jnp.broadcast_to(square, (8, STRETCH))
    group = lax.div(me, 8)
    spot = lax.rem(me, 8)
    met = []
    for by in range(1, 8):
        copy = remote(
            squares, peers3.at[by - 1], u_send.at[by - 1], u_recv.at[by - 1],
            group * 8 + lax.rem(spot + by, 8),
        )
        copy.start()
        met.append(copy)
    second.first_far()
    total = square
    for by in range(1, 8):
        met[by - 1].wait_recv()
        total = total + peers3[by - 1, 0:1, :]
    scale = lax.rsqrt(total * (1.0 / (MH // G * P_SIZE)) + epsilon)
    scatter = Scatter(part, near1, full1, mid, near2, full2, x_send, x_recv)
    scatter.run(
        weight, (gained[...] * scale).astype(bf16),
        [lambda: second.second_near(1)],
        [lambda: second.second_near(2), lambda: blocks.relay(1), lambda: blocks.relay(3),
         lambda: blocks.spread(3, 1), lambda: second.second_near(3)],
    )
    gain = column(gain_sh, me * SHARD, SHARD)
    mine = pl.ds(pl.multiple_of(me * SHARD, 16), SHARD)
    sq = jnp.zeros((1, STRETCH), f32)
    for half in (0, 1):
        rows = pl.ds(half * HALF, HALF)
        value = hidden[rows, :].astype(f32) + scatter.result(half)
        next_out[rows, :] = value
        value = value.astype(bf16).astype(f32)
        sq = sq + jnp.sum(value * value, axis=0, keepdims=True)
        rounded[rows, :] = (value * gain[half * HALF : (half + 1) * HALF]).astype(bf16)
    sums2[...] = jnp.broadcast_to(sq, (8, STRETCH))
    gather = Gather(rounded, wide2, g_send, g_recv)
    gather.start()
    sent = send_sums(sums2, peers2, r_send, r_recv)
    wide2[mine, :] = rounded[...]
    loads[4].wait()
    for k in range(SIDE):
        second.second_far(k)
    acc[...] = jnp.dot(watt[:, D:], emb[...], preferred_element_type=f32)

    def attend_rows(by):
        span = row_of(by)
        acc[...] += jnp.dot(watt[:, span], wide2[span, :], preferred_element_type=f32)

    gather.run(attend_rows, lambda: None)
    total = add_sums(sums2, peers2, sent)[0:1, :] + embed_sq
    scale = lax.rsqrt(total * (0.5 / D) + epsilon)
    value = acc[...]
    mine_q[...] = (value[:HD] * scale).astype(bf16)
    swap = pltpu.make_async_remote_copy(
        src_ref=mine_q, dst_ref=other_out, send_sem=v_send, recv_sem=v_recv,
        device_id={"seq": x * 2 + 1 - core}, device_id_type=MESH,
    )
    swap.start()
    proj_out[...] = (value * scale).astype(bf16)
    gather.finish()
    scatter.finish()
    loads[5].wait()
    blocks.finish()
    swap.wait()
    first.finish()
    second.finish()
    for copy in out + moved + met + sent:
        copy.wait_send()


def front_call(*args):
    anywhere = pl.BlockSpec(memory_space=pl.ANY)
    vmem = pl.BlockSpec(memory_space=pltpu.VMEM)
    smem = pl.BlockSpec(memory_space=pltpu.SMEM)
    dma = pltpu.SemaphoreType.DMA
    return pl.pallas_call(
        front_kernel,
        out_shape=(
            jax.ShapeDtypeStruct((SHARD, STRETCH), f32),
            jax.ShapeDtypeStruct((3 * HD, STRETCH), bf16),
            jax.ShapeDtypeStruct((HL * P_SIZE, NS), f32),
            jax.ShapeDtypeStruct((SIDE * BLOCKS, 2, HD, BLOCK), bf16),
            jax.ShapeDtypeStruct((HD, STRETCH), bf16),
        ),
        in_specs=[anywhere] * 6 + [smem] + [anywhere] * 2 + [vmem] + [smem] * 3 + [anywhere] * 5,
        out_specs=(vmem, vmem, vmem, anywhere, anywhere),
        scratch_shapes=[
            pltpu.VMEM((SHARD, STRETCH), bf16),
            pltpu.VMEM((SHARD, STRETCH), bf16),
            pltpu.VMEM((D // 128, 128), f32),
            pltpu.VMEM((2 * D // 128, 128), f32),
            pltpu.VMEM((CONV, HL * P_SIZE), f32),
            pltpu.VMEM((1, HL * P_SIZE), f32),
            pltpu.VMEM((HL * P_SIZE, D), bf16),
            pltpu.VMEM((D, STRETCH), bf16),
            pltpu.VMEM((SHARD, STRETCH), bf16),
            pltpu.VMEM((SHARD, STRETCH), bf16),
            pltpu.VMEM((D, HL * 128), bf16),
            pltpu.VMEM((D, 2 * G * NS), bf16),
            pltpu.VMEM((HL * 128, STRETCH), f32),
            pltpu.VMEM((2 * G * NS, STRETCH), f32),
            pltpu.VMEM((8, STRETCH), f32),
            pltpu.VMEM((HEADS - 1, 8, STRETCH), f32),
            pltpu.VMEM((2 * SEQ, HL, P_SIZE * NS), f32),
            pltpu.VMEM((SEQ, CONV - 1, 2, HL * P_SIZE), f32),
            pltpu.VMEM((128, 128), f32),
            pltpu.VMEM((HL * P_SIZE, STRETCH), f32),
            pltpu.VMEM((3 * HD, 2 * D), bf16),
            pltpu.VMEM((D, STRETCH), bf16),
            pltpu.VMEM((D, STRETCH), bf16),
            pltpu.VMEM((3 * HD, STRETCH), f32),
            pltpu.VMEM((8, STRETCH), f32),
            pltpu.VMEM((7, 8, STRETCH), f32),
            pltpu.VMEM((8, STRETCH), f32),
            pltpu.VMEM((HEADS - 1, 8, STRETCH), f32),
            pltpu.VMEM((SHARD, STRETCH), bf16),
        ] + SCATTER_SCRATCH + GATHER_SEMS + GATHER_SEMS + GATHER_SEMS + [
            dma((HEADS - 1,)), dma((HEADS - 1,)),
            dma((SEQ - 1,)), dma((SEQ - 1,)),
            dma((SEQ - 1,)), dma((SEQ - 1,)),
            dma((7,)), dma((7,)),
            dma((HEADS - 1,)), dma((HEADS - 1,)),
            dma((12,)), dma((12,)),
            dma((6,)), dma((7,)),
            pltpu.VMEM((HL, STRETCH), f32),
            pltpu.VMEM((HD, STRETCH), bf16),
            dma,
            dma,
        ],
        compiler_params=pltpu.CompilerParams(
            collective_id=0, has_side_effects=True, vmem_limit_bytes=60 * 2**20
        ),
        name="front_rows",
    )(*args)


def merge_kernel(own_part, other_part, weight, before, out,
                 part, near1, full1, mid, near2, full2, s_send, s_recv, got, v_send, v_recv):
    barrier = greet_heads()
    seq = lax.axis_index("seq")
    to = {"seq": seq + 1 - 2 * lax.rem(seq, 2)}
    pl.semaphore_signal(barrier, inc=1, device_id=to, device_id_type=MESH)
    pl.semaphore_wait(barrier, HEADS)
    swap = pltpu.make_async_remote_copy(
        src_ref=other_part, dst_ref=got, send_sem=v_send, recv_sem=v_recv, device_id=to, device_id_type=MESH
    )
    swap.start()
    swap.wait()
    scale = HD ** -0.5 * 1.4426950408889634
    high = jnp.maximum(own_part[HD : HD + 1, :], got[HD : HD + 1, :])
    one = jnp.exp2((own_part[HD : HD + 1, :] - high) * scale)
    two = jnp.exp2((got[HD : HD + 1, :] - high) * scale)
    total = own_part[HD + 1 : HD + 2, :] * one + got[HD + 1 : HD + 2, :] * two
    attended = ((own_part[:HD, :] * one + got[:HD, :] * two) / total).astype(bf16)
    scatter = Scatter(part, near1, full1, mid, near2, full2, s_send, s_recv)
    scatter.run(weight, attended)
    for half in (0, 1):
        rows = pl.ds(half * HALF, HALF)
        out[rows, :] = before[rows, :] + scatter.result(half)
    scatter.finish()


def merge_call(own_part, other_part, weight, before):
    vmem = pl.BlockSpec(memory_space=pltpu.VMEM)
    return pl.pallas_call(
        merge_kernel,
        out_shape=jax.ShapeDtypeStruct((SHARD, STRETCH), f32),
        in_specs=[vmem] * 4,
        out_specs=vmem,
        scratch_shapes=SCATTER_SCRATCH + [
            pltpu.VMEM((PARTS, STRETCH), f32), pltpu.SemaphoreType.DMA, pltpu.SemaphoreType.DMA
        ],
        compiler_params=pltpu.CompilerParams(
            collective_id=2, has_side_effects=True, vmem_limit_bytes=40 * 2**20
        ),
        name="merge_rows",
    )(own_part, other_part, weight, before)


def turn(value):
    return jnp.concatenate([value, jnp.zeros((256 - HD, STRETCH), f32)], axis=0).T[:, :HD]


PARTS = 256


def attend_kernel(table, lengths, projected, other, pool, own_out, other_out, held, sems, acc, top, total, ids):
    seq = lax.axis_index("seq")
    core = lax.rem(seq, 2)
    scale = HD ** -0.5 * 1.4426950408889634
    span = STEPB * BLOCK

    def listing(which, request):
        limit = lengths[request]
        count = lax.div(limit + BLOCK - 1, BLOCK)

        def look(j, found):
            block = table[request, j]
            holder = lax.div(block, BLOCKS)
            ids[which, found] = lax.div(holder, 2) * BLOCKS + lax.rem(block, BLOCKS)
            return found + (lax.rem(holder, 2) == core).astype(jnp.int32)

        found = lax.fori_loop(0, count, look, 0)
        for i in range(STEPB):
            ids[which, found + i] = 0
        last = lax.rem(lax.div(table[request, count - 1], BLOCKS), 2) == core
        return found * BLOCK - jnp.where(last, count * BLOCK - limit, 0)

    def fetch(which, step, slot):
        return [
            pltpu.make_async_copy(
                pool.at[ids[which, step * STEPB + i]],
                held.at[which, slot, :, :, pl.ds(i * BLOCK, BLOCK)],
                sems.at[which, slot, i],
            )
            for i in range(STEPB)
        ]

    def begin(which, request):
        keys = listing(which, request)

        @pl.when(keys > 0)
        def _():
            for copy in fetch(which, 0, 0):
                copy.start()

        return keys

    def prefix(which, keys, q):
        steps = lax.div(keys + span - 1, span)

        def step_body(step, _):
            slot = lax.rem(step, 2)

            @pl.when(step + 1 < steps)
            def _():
                for copy in fetch(which, step + 1, 1 - slot):
                    copy.start()

            for copy in fetch(which, step, slot):
                copy.wait()
            scores = jnp.dot(q, held[which, slot, 0], preferred_element_type=f32)

            def rest(scores):
                old = top[...]
                high = jnp.maximum(old, jnp.max(scores, axis=1, keepdims=True))
                weights = jnp.exp2((scores - high) * scale)
                factor = jnp.exp2((old - high) * scale)
                top[...] = high
                total[...] = total[...] * factor + jnp.sum(weights, axis=1, keepdims=True)
                acc[...] = acc[...] * factor + lax.dot_general(
                    weights.astype(bf16), held[which, slot, 1], NT, preferred_element_type=f32
                )

            @pl.when((step + 1) * span <= keys)
            def _():
                rest(scores)

            @pl.when((step + 1) * span > keys)
            def _():
                where = step * span + lax.broadcasted_iota(jnp.int32, scores.shape, 1)
                rest(jnp.where(where < keys, scores, masked))

            return 0

        lax.fori_loop(0, steps, step_body, 0)

    def result():
        fill = jnp.zeros((STRETCH, PARTS - HD - 2), f32)
        return jnp.concatenate([acc[...], top[...], total[...], fill], axis=1).T

    own_keys = begin(0, seq)
    other_keys = begin(1, seq + 1 - 2 * core)
    q = turn(projected[:HD, :].astype(f32)).astype(bf16)
    scores = jnp.dot(q, projected[HD : 2 * HD, :], preferred_element_type=f32)
    row = lax.broadcasted_iota(jnp.int32, scores.shape, 0)
    col = lax.broadcasted_iota(jnp.int32, scores.shape, 1)
    scores = jnp.where(row >= col, scores, masked)
    high = jnp.max(scores, axis=1, keepdims=True)
    weights = jnp.exp2((scores - high) * scale)
    top[...] = high
    total[...] = jnp.sum(weights, axis=1, keepdims=True)
    acc[...] = lax.dot_general(
        weights.astype(bf16), projected[2 * HD :, :], NT, preferred_element_type=f32
    )
    prefix(0, own_keys, q)
    own_out[...] = result()
    top[...] = jnp.full_like(top, masked)
    total[...] = jnp.zeros_like(total)
    acc[...] = jnp.zeros_like(acc)
    prefix(1, other_keys, turn(other[...].astype(f32)).astype(bf16))
    other_out[...] = result()


def attend_call(table, lengths, projected, other, pool):
    vmem = pl.BlockSpec(memory_space=pltpu.VMEM)
    smem = pl.BlockSpec(memory_space=pltpu.SMEM)
    return pl.pallas_call(
        attend_kernel,
        out_shape=(jax.ShapeDtypeStruct((PARTS, STRETCH), f32),) * 2,
        in_specs=[smem, smem, vmem, vmem, pl.BlockSpec(memory_space=pl.ANY)],
        out_specs=(vmem, vmem),
        scratch_shapes=[
            pltpu.VMEM((2, 2, 2, HD, STEPB * BLOCK), bf16),
            pltpu.SemaphoreType.DMA((2, 2, STEPB)),
            pltpu.VMEM((STRETCH, HD), f32),
            pltpu.VMEM((STRETCH, 1), f32),
            pltpu.VMEM((STRETCH, 1), f32),
            pltpu.SMEM((2, MAXB + STEPB), jnp.int32),
        ],
        compiler_params=pltpu.CompilerParams(vmem_limit_bytes=48 * 2**20),
        name="attend_rows",
    )(table, lengths, projected, other, pool)


def body(hidden, embedding, input_gain, w_input, w_groups, w_step, step_bias, decay_rate, skip_gain,
         conv_weight, mix_gain, w_output, state_store, conv_store, state_slot, prefix_len, block_table,
         shared_gain, w_attend, cache_pool, w_merge):
    heads_local = w_step.shape[1]
    hidden_next, projected, final_state, pool, other = front_call(
        hidden.T, embedding.T, input_gain.reshape(D // 128, 128), shared_gain.reshape(2 * D // 128, 128),
        state_store, conv_store.transpose(1, 0, 2).astype(f32), state_slot, w_input, w_groups, w_step.T,
        step_bias, decay_rate, skip_gain, conv_weight, mix_gain[None, :], w_output, w_attend.T,
        cache_pool.transpose(0, 1, 3, 2),
    )
    own_part, other_part = attend_call(block_table, prefix_len, projected, other, pool)
    layer_output = merge_call(own_part, other_part, w_merge, hidden_next)
    return (layer_output.T, final_state.reshape(1, heads_local, P_SIZE * NS))


def solution(mesh):
    return jax.shard_map(
        body,
        mesh=mesh,
        in_specs=(
            P("seq", "head"),
            P("seq", "head"),
            P(),
            P(None, "head"),
            P(),
            P(None, "head"),
            P("head"),
            P("head"),
            P("head"),
            P(None, "head"),
            P("head"),
            P("head", None),
            P("seq", "head", None),
            P("seq", None, "head"),
            P(),
            P(),
            P(),
            P(),
            P(None, "head"),
            P("seq", None, None, "head"),
            P("head", None),
        ),
        out_specs=(P("seq", "head"), P("seq", "head", None)),
        check_vma=False,
    )
```

```python
import functools

import jax
import jax.numpy as jnp
from jax import lax
from jax.experimental import pallas as pl
from jax.experimental.pallas import tpu as pltpu
from jax.sharding import PartitionSpec as P

D = 3584
MH = 64
P_SIZE = 64
NS = 64
G = 2
CONV = 4
HD = 224
STRETCH = 512
BLOCK = 128
MAXB = 64
SEQ = 8
SIDE = 4
HEADS = SIDE * SIDE
SHARD = D // HEADS
HALF = SHARD // 2
LANES = STRETCH // 2
STEPB = 8

MESH = pl.DeviceIdType.MESH
epsilon = 1e-05
masked = -1e30
highest = lax.Precision.HIGHEST
f32 = jnp.float32
bf16 = jnp.bfloat16


def place():
    me = lax.axis_index("head")
    return lax.div(me, SIDE), lax.rem(me, SIDE)


def around(c, by):
    return lax.rem(c + by + SIDE, SIDE)


def coords(half):
    z, y = place()
    return (y, z) if half == 0 else (z, y)


def device(half, c1, c2):
    return c2 * SIDE + c1 if half == 0 else c1 * SIDE + c2


def piece(half, c1, c2):
    return pl.ds(pl.multiple_of(device(half, c1, c2) * SHARD + half * HALF, 16), HALF)


OFFSETS = (0, -1, 1, 2)
LEFT = pl.ds(0, LANES)
RIGHT = pl.ds(LANES, LANES)
FULL = pl.ds(0, STRETCH)


def remote(src, dst, send_sem, recv_sem, dev):
    return pltpu.make_async_remote_copy(
        src_ref=src, dst_ref=dst, send_sem=send_sem, recv_sem=recv_sem,
        device_id={"head": dev}, device_id_type=MESH,
    )


class Gather:
    def __init__(self, own, out, send_sems, recv_sems):
        self.own, self.out, self.ss, self.rs = own, out, send_sems, recv_sems
        self.sent = []

    def go(self, half, idx, src, c1, c2, lanes, to1, to2):
        dst = self.out.at[piece(half, c1, c2), lanes]
        copy = remote(src, dst, self.ss.at[half, idx], self.rs.at[half, idx], device(half, to1, to2))
        copy.start()
        self.sent.append(copy)

    def arrive(self, half, idx, c1, c2, lanes):
        where = self.out.at[piece(half, c1, c2), lanes]
        me1, me2 = coords(half)
        remote(where, where, self.ss.at[half, idx], self.rs.at[half, idx], device(half, around(me1, 1), me2)).wait_recv()

    def start(self):
        for axis in (1, 2):
            for half in (0, 1):
                c1, c2 = coords(half)
                src = self.own.at[pl.ds(half * HALF, HALF), FULL]
                if axis == 1:
                    self.go(half, 0, src, c1, c2, FULL, around(c1, 1), c2)
                    self.go(half, 1, src, c1, c2, FULL, around(c1, -1), c2)
                else:
                    self.go(half, 4, src, c1, c2, FULL, c1, around(c2, 1))
                    self.go(half, 5, src, c1, c2, FULL, c1, around(c2, -1))

    def second(self, half, k):
        c1, c2 = coords(half)
        o1 = around(c1, OFFSETS[k])
        src = self.out.at[piece(half, o1, c2), FULL]
        self.go(half, 4 + 4 * k, src, o1, c2, FULL, c1, around(c2, 1))
        self.go(half, 5 + 4 * k, src, o1, c2, FULL, c1, around(c2, -1))

    def first_near(self):
        for half in (0, 1):
            c1, c2 = coords(half)
            left = around(c1, -1)
            self.arrive(half, 0, left, c2, FULL)
            self.go(half, 2, self.out.at[piece(half, left, c2), LEFT], left, c2, LEFT, around(c1, 1), c2)
            self.second(half, 1)
        for half in (0, 1):
            c1, c2 = coords(half)
            right = around(c1, 1)
            self.arrive(half, 1, right, c2, FULL)
            self.go(half, 3, self.out.at[piece(half, right, c2), RIGHT], right, c2, RIGHT, around(c1, -1), c2)
            self.second(half, 2)

    def first_far(self):
        for half in (0, 1):
            c1, c2 = coords(half)
            far = around(c1, 2)
            self.arrive(half, 2, far, c2, LEFT)
            self.arrive(half, 3, far, c2, RIGHT)
            self.second(half, 3)

    def second_near(self, k, halves=(0, 1)):
        for half in halves:
            c1, c2 = coords(half)
            o1 = around(c1, OFFSETS[k])
            for way in (0, 1):
                nb = around(c2, -1 if way == 0 else 1)
                to = around(c2, 1 if way == 0 else -1)
                lanes = LEFT if way == 0 else RIGHT
                self.arrive(half, 4 + 4 * k + way, o1, nb, FULL)
                self.go(half, 6 + 4 * k + way, self.out.at[piece(half, o1, nb), lanes], o1, nb, lanes, c1, to)

    def second_far(self, k, halves=(0, 1)):
        for half in halves:
            c1, c2 = coords(half)
            o1 = around(c1, OFFSETS[k])
            far = around(c2, 2)
            self.arrive(half, 6 + 4 * k, o1, far, LEFT)
            self.arrive(half, 7 + 4 * k, o1, far, RIGHT)

    def run(self, use, between):
        self.first_near()
        self.second_near(0)
        self.first_far()
        self.second_near(1)
        self.second_far(0, (1,))
        use(0)
        self.second_near(2)
        self.second_near(3)
        between()
        self.second_far(1, (1,))
        use(-1)
        self.second_far(2, (1,))
        use(1)
        self.second_far(3, (1,))
        for k in range(SIDE):
            self.second_far(k, (0,))
        use(2)

    def finish(self):
        for copy in self.sent:
            copy.wait_send()


GATHER_SEMS = [pltpu.SemaphoreType.DMA((2, 20)), pltpu.SemaphoreType.DMA((2, 20))]

SCATTER_SCRATCH = [
    pltpu.VMEM((D, STRETCH), bf16),
    pltpu.VMEM((2, SIDE, 2, HALF, LANES), bf16),
    pltpu.VMEM((2, SIDE, 2, HALF, STRETCH), bf16),
    pltpu.VMEM((2, SIDE, HALF, STRETCH), bf16),
    pltpu.VMEM((2, 2, HALF, LANES), bf16),
    pltpu.VMEM((2, 2, HALF, STRETCH), bf16),
    pltpu.SemaphoreType.DMA((2, 20)),
    pltpu.SemaphoreType.DMA((2, 20)),
]


class Scatter:
    def __init__(self, part, near1, full1, mid, near2, full2, send_sems, recv_sems):
        self.part, self.near1, self.full1, self.mid = part, near1, full1, mid
        self.near2, self.full2, self.ss, self.rs = near2, full2, send_sems, recv_sems
        self.sent = []

    def go(self, half, idx, src, dst, to1, to2):
        copy = remote(src, dst, self.ss.at[half, idx], self.rs.at[half, idx], device(half, to1, to2))
        copy.start()
        self.sent.append(copy)

    def arrive(self, half, idx, where):
        me1, me2 = coords(half)
        remote(where, where, self.ss.at[half, idx], self.rs.at[half, idx], device(half, around(me1, 1), me2)).wait_recv()

    def one(self, k, halves):
        for half in halves:
            c1, c2 = coords(half)
            o1 = around(c1, OFFSETS[k])
            rows = piece(half, o1, around(c2, 2))
            self.go(half, 4 * k, self.part.at[rows, LEFT], self.near1.at[half, k, 0], c1, around(c2, 1))
            self.go(half, 4 * k + 1, self.part.at[rows, RIGHT], self.near1.at[half, k, 1], c1, around(c2, -1))

    def two(self, k):
        for half in (0, 1):
            c1, c2 = coords(half)
            o1 = around(c1, OFFSETS[k])
            for way in (0, 1):
                to = around(c2, 1 if way == 0 else -1)
                lanes = LEFT if way == 0 else RIGHT
                rows = piece(half, o1, to)
                self.arrive(half, 4 * k + way, self.near1.at[half, k, way])
                mine = self.part[rows, lanes].astype(f32)
                self.part[rows, lanes] = (mine + self.near1[half, k, way].astype(f32)).astype(bf16)
                self.go(half, 4 * k + 2 + way, self.part.at[rows, FULL], self.full1.at[half, k, way], c1, to)

    def three(self, k):
        for half in (0, 1):
            c1, c2 = coords(half)
            o1 = around(c1, OFFSETS[k])
            self.arrive(half, 4 * k + 2, self.full1.at[half, k, 0])
            self.arrive(half, 4 * k + 3, self.full1.at[half, k, 1])
            if k:
                self.mid[half, k] = self.total(half, k).astype(bf16)
                if k == 3:
                    self.go(half, 16, self.mid.at[half, 3, :, LEFT], self.near2.at[half, 0], around(c1, 1), c2)
                    self.go(half, 17, self.mid.at[half, 3, :, RIGHT], self.near2.at[half, 1], around(c1, -1), c2)

    def total(self, half, k):
        c1, c2 = coords(half)
        rows = piece(half, around(c1, OFFSETS[k]), c2)
        return (
            self.part[rows, :].astype(f32)
            + self.full1[half, k, 0].astype(f32)
            + self.full1[half, k, 1].astype(f32)
        )

    def four(self, k):
        way = 0 if k == 2 else 1
        lanes = LEFT if way == 0 else RIGHT
        for half in (0, 1):
            c1, c2 = coords(half)
            self.arrive(half, 16 + way, self.near2.at[half, way])
            mine = self.mid[half, k, :, lanes].astype(f32)
            self.mid[half, k, :, lanes] = (mine + self.near2[half, way].astype(f32)).astype(bf16)
            self.go(half, 18 + way, self.mid.at[half, k], self.full2.at[half, way], around(c1, OFFSETS[k]), c2)

    def run(self, weight, rows, early=(), late=()):
        for by in (2, -1, 1, 0):
            products(weight, rows, self.part, by)
        for k in (3, 2, 1, 0):
            self.one(k, (0, 1))
        for step in early:
            step()
        self.two(3)
        self.two(2)
        self.two(1)
        self.three(3)
        self.two(0)
        for step in late:
            step()
        self.three(2)
        self.four(2)
        self.three(1)
        self.four(1)
        self.three(0)

    def result(self, half):
        self.arrive(half, 18, self.full2.at[half, 0])
        self.arrive(half, 19, self.full2.at[half, 1])
        return (
            self.total(half, 0)
            + self.full2[half, 0].astype(f32)
            + self.full2[half, 1].astype(f32)
        )

    def finish(self):
        for copy in self.sent:
            copy.wait_send()


def greet_heads():
    barrier = pltpu.get_barrier_semaphore()
    me = lax.axis_index("head")
    for by in range(1, HEADS):
        pl.semaphore_signal(
            barrier, inc=1, device_id={"head": lax.rem(me + by, HEADS)}, device_id_type=MESH
        )
    return barrier


def flat(row, count):
    turned = jnp.broadcast_to(row, (128, count)).T
    return jnp.concatenate([turned] * (STRETCH // 128), axis=1)


def column(table, start, count):
    rows = table.shape[0]
    entry = start + lax.broadcasted_iota(jnp.int32, (count, rows), 0)
    pick = (lax.shift_right_logical(entry, 7) == lax.broadcasted_iota(jnp.int32, (count, rows), 1))
    lines = jnp.dot(pick.astype(f32), table[...], precision=highest, preferred_element_type=f32)
    entry = start + lax.broadcasted_iota(jnp.int32, (count, 128), 0)
    keep = jnp.bitwise_and(entry, 127) == lax.broadcasted_iota(jnp.int32, (count, 128), 1)
    return jnp.sum(jnp.where(keep, lines, 0.0), axis=1, keepdims=True)


def send_sums(mine, peers, send_sems, recv_sems):
    me = lax.axis_index("head")
    out = []
    for by in range(1, HEADS):
        copy = remote(
            mine, peers.at[by - 1], send_sems.at[by - 1], recv_sems.at[by - 1],
            lax.rem(me + by, HEADS),
        )
        copy.start()
        out.append(copy)
    return out


def add_sums(mine, peers, out):
    total = mine[...]
    for by in range(1, HEADS):
        out[by - 1].wait_recv()
        total = total + peers[by - 1]
    return total


def silu(value):
    return value / (1.0 + jnp.exp(-value))


TN = (((0,), (0,)), ((), ()))
NT = (((1,), (1,)), ((), ()))
HL = 4


ROW = SIDE * SHARD


def row_of(by):
    return pl.ds(pl.multiple_of(around(place()[0], by) * ROW, 128), ROW)


def products(weight, rows, part, by):
    span = row_of(by)
    part[span, :] = lax.dot_general(
        weight[:, span], rows, TN, preferred_element_type=f32
    ).astype(bf16)


CHUNKS = 4
BLOCKS = 20


class Pool:
    def __init__(self, own, out, send_sems, recv_sems):
        self.own, self.out, self.ss, self.rs = own, out, send_sems, recv_sems
        seq = lax.axis_index("seq")
        self.x, self.core = lax.div(seq, 2), lax.rem(seq, 2)
        self.sent = []

    def slab(self, by, core, ch):
        per = BLOCKS // CHUNKS
        return self.out.at[pl.ds((around(self.x, by) * 2 + core) * BLOCKS + ch * per, per)]

    def copy(self, idx, src, dst, by, core):
        return pltpu.make_async_remote_copy(
            src_ref=src, dst_ref=dst, send_sem=self.ss.at[idx], recv_sem=self.rs.at[idx],
            device_id={"seq": around(self.x, by) * 2 + core}, device_id_type=MESH,
        )

    def go(self, idx, src, dst, by, core):
        copy = self.copy(idx, src, dst, by, core)
        copy.start()
        self.sent.append(copy)

    def arrive(self, idx, dst):
        self.copy(idx, dst, dst, 1, self.core).wait_recv()

    def spread(self, right, left):
        per = BLOCKS // CHUNKS
        for base, ch, by in ((0, right, 1), (4, left, -1)):
            self.go(base + ch, self.own.at[pl.ds(ch * per, per)], self.slab(0, self.core, ch), by, self.core)

    def start(self):
        per = BLOCKS // CHUNKS
        self.spread(0, 2)
        for ch in range(CHUNKS):
            self.go(12 + ch, self.own.at[pl.ds(ch * per, per)], self.slab(0, self.core, ch), 0, 1 - self.core)

    def share(self, j, by, ch):
        where = self.slab(by, self.core, ch)
        self.go(12 + 4 * j + ch, where, where, 0, 1 - self.core)

    def relay(self, ch):
        left = self.slab(-1, self.core, ch)
        right = self.slab(1, self.core, ch)
        if ch < 2:
            self.arrive(ch, left)
            self.go(8 + ch, left, left, 1, self.core)
            self.share(1, -1, ch)
        else:
            self.arrive(4 + ch, right)
            self.go(8 + ch, right, right, -1, self.core)
            self.share(2, 1, ch)

    def rest(self, ch):
        if ch < 2:
            self.arrive(4 + ch, self.slab(1, self.core, ch))
            self.share(2, 1, ch)
        else:
            self.arrive(ch, self.slab(-1, self.core, ch))
            self.share(1, -1, ch)

    def far(self, ch):
        self.arrive(8 + ch, self.slab(2, self.core, ch))
        self.share(3, 2, ch)

    def finish(self):
        for j, by in enumerate((0, -1, 1, 2)):
            for ch in range(CHUNKS):
                self.arrive(12 + 4 * j + ch, self.slab(by, 1 - self.core, ch))
        for copy in self.sent:
            copy.wait_send()


def front_kernel(hidden_in, embed_in, gain_in_in, gain_sh_in, states, tails_in, slots, w_in, w_gr, w_st, bias, decay,
                 skip, conv_in, mix_in, w_out_in, w_att, pool_in,
                 next_out, proj_out, final_out, pool_out,
                 hidden, embed, gain_in, gain_sh, conv_w, mix_g, weight,
                 wide, own_h, own_e, win, wgr, paired, grouped, sums, peers, stores, tail_all, lines, gained, watt,
                 emb, wide2, acc, squares, peers3, sums2, peers2, rounded,
                 part, near1, full1, mid, near2, full2, x_send, x_recv,
                 h_send, h_recv, e_send, e_recv, g_send, g_recv, q_send, q_recv, s_send, s_recv, t_send, t_recv,
                 u_send, u_recv, r_send, r_recv, p_send, p_recv, local, here, raws, tails_raw, tails):
    seq = lax.axis_index("seq")
    me = lax.axis_index("head")
    small = [
        pltpu.make_async_copy(src, dst, here.at[i])
        for i, (src, dst) in enumerate((
            (hidden_in, hidden), (gain_in_in, gain_in), (embed_in, embed), (gain_sh_in, gain_sh),
            (conv_in, conv_w), (mix_in, mix_g), (w_out_in, weight), (tails_in, tails_raw),
        ))
    ]
    for copy in small:
        copy.start()
    loads = [
        pltpu.make_async_copy(w_in, win, local.at[0]),
        pltpu.make_async_copy(w_gr, wgr, local.at[1]),
        pltpu.make_async_copy(states, stores.at[pl.ds(seq * 2, 2)], local.at[2]),
        pltpu.make_async_copy(w_att, watt, local.at[3]),
        pltpu.make_async_copy(pool_in, pool_out.at[pl.ds(seq * BLOCKS, BLOCKS)], local.at[4]),
    ]
    for copy in loads:
        copy.start()
    barrier = greet_heads()
    for by in range(1, SEQ):
        pl.semaphore_signal(
            barrier, inc=1, device_id={"seq": lax.rem(seq + by, SEQ)}, device_id_type=MESH
        )
    mine = pl.ds(pl.multiple_of(me * SHARD, 16), SHARD)
    small[0].wait()
    small[1].wait()
    value = hidden[...].astype(f32)
    sq_h = jnp.sum(value * value, axis=0, keepdims=True)
    ready = (value * column(gain_in, me * SHARD, SHARD)).astype(bf16)
    own_h[...] = ready
    wide[mine, :] = ready
    pl.semaphore_wait(barrier, HEADS - 1 + SEQ - 1)
    first = Gather(own_h, wide, h_send, h_recv)
    second = Gather(own_e, emb, e_send, e_recv)
    blocks = Pool(pool_in, pool_out, p_send, p_recv)
    first.start()
    for copy in small[2:]:
        copy.wait()
    tails[...] = tails_raw[...].astype(f32)
    tail_all[seq] = tails[...]
    value = embed[...].astype(f32)
    sq_e = jnp.sum(value * value, axis=0, keepdims=True)
    ready = (value * column(gain_sh, D + me * SHARD, SHARD)).astype(bf16)
    own_e[...] = ready
    emb[mine, :] = ready
    sums[0:1, :] = sq_h
    sums[1:2, :] = sq_e
    out = send_sums(sums, peers, q_send, q_recv)
    x, core = lax.div(seq, 2), lax.rem(seq, 2)
    held = (
        (states, stores, lambda at: stores.at[pl.ds(at * 2, 2)], s_send, s_recv),
        (tails, tail_all, lambda at: tail_all.at[at], t_send, t_recv),
    )
    moved = []

    def send_state(idx, src, dst, ss, rs, to):
        copy = pltpu.make_async_remote_copy(
            src_ref=src, dst_ref=dst, send_sem=ss.at[idx], recv_sem=rs.at[idx],
            device_id={"seq": to}, device_id_type=MESH,
        )
        copy.start()
        moved.append(copy)

    for src, _, at, ss, rs in held:
        for by in range(1, SIDE):
            send_state(by - 1, src, at(seq), ss, rs, around(x, by) * 2 + core)
        send_state(3, src, at(seq), ss, rs, x * 2 + 1 - core)

    def pass_states():
        for _, _, at, ss, rs in held:
            for by in range(1, SIDE):
                where = at(around(x, -by) * 2 + core)
                pltpu.make_async_remote_copy(
                    src_ref=where, dst_ref=where, send_sem=ss.at[by - 1], recv_sem=rs.at[by - 1],
                    device_id={"seq": x * 2 + 1 - core}, device_id_type=MESH,
                ).wait_recv()
                send_state(3 + by, where, where, ss, rs, x * 2 + 1 - core)

    def wait_states():
        for _, _, at, ss, rs in held:
            for by in range(SIDE):
                where = at(around(x, -by) * 2 + 1 - core)
                pltpu.make_async_remote_copy(
                    src_ref=where, dst_ref=where, send_sem=ss.at[3 + by], recv_sem=rs.at[3 + by],
                    device_id={"seq": x * 2 + 1 - core}, device_id_type=MESH,
                ).wait_recv()

    blocks.start()
    paired[...] = jnp.zeros_like(paired)
    grouped[...] = jnp.zeros_like(grouped)
    raws[...] = jnp.zeros_like(raws)
    for copy in loads[:2]:
        copy.wait()

    def project(by):
        span = row_of(by)
        rows = wide[span, :]
        paired[...] += lax.dot_general(win[span, :], rows, TN, preferred_element_type=f32)
        grouped[...] += lax.dot_general(wgr[span, :], rows, TN, preferred_element_type=f32)
        raws[...] += jnp.dot(w_st[:, span], rows, preferred_element_type=f32)

    def between():
        second.start()
        pass_states()
        blocks.spread(1, 3)
        blocks.relay(0)
        blocks.relay(2)
        blocks.spread(2, 0)

    first.run(project, between)
    total = add_sums(sums, peers, out)
    embed_sq = total[1:2, :]
    scale = lax.rsqrt(total[0:1, :] * (1.0 / D) + epsilon)
    raw = raws[...] * scale
    head = lax.broadcasted_iota(jnp.int32, (HL, STRETCH), 0)

    def by_head(ref):
        line = jnp.zeros((HL, STRETCH), f32)
        for i in range(HL):
            line = jnp.where(head == i, ref[i], line)
        return line

    raw = raw + by_head(bias)
    steps = jnp.maximum(raw, 0.0) + jnp.log1p(jnp.exp(-jnp.abs(raw)))
    cums = -by_head(decay) * steps
    lane = lax.broadcasted_iota(jnp.int32, (HL, STRETCH), 1)
    by = 1
    while by < STRETCH:
        cums = cums + jnp.where(lane >= by, pltpu.roll(cums, by, 1), 0.0)
        by *= 2
    turned = jnp.concatenate([cums, steps, jnp.zeros((128 - 2 * HL, STRETCH), f32)], axis=0).T
    group = lax.div(me, 8)
    b_proj = scale * grouped[pl.ds(pl.multiple_of(group * NS, NS), NS), :]
    c_proj = scale * grouped[pl.ds(pl.multiple_of(G * NS + group * NS, NS), NS), :]
    pairs = lax.dot_general(b_proj.astype(bf16), c_proj.astype(bf16), TN, preferred_element_type=f32)
    src = lax.broadcasted_iota(jnp.int32, pairs.shape, 0)
    dst = lax.broadcasted_iota(jnp.int32, pairs.shape, 1)
    pairs = jnp.where(src <= dst, pairs, 0.0)

    loads[2].wait()
    wait_states()
    slot = slots[seq]
    for h in range(HL):
        for i in range(32):
            lines[pl.ds(h * 32 + i, 1), :] = stores[slot, h : h + 1, i * 128 : (i + 1) * 128]
    p_row = lax.broadcasted_iota(jnp.int32, (P_SIZE, 32), 0)
    p_col = lax.broadcasted_iota(jnp.int32, (P_SIZE, 32), 1)
    even = (p_row == 2 * p_col).astype(f32)
    odd = (p_row == 2 * p_col + 1).astype(f32)
    lane = lax.broadcasted_iota(jnp.int32, (HL * P_SIZE, 128), 1)
    before = jnp.zeros((HL * P_SIZE, 128), f32)
    for k in range(CONV - 1):
        row = tail_all[lax.div(slot, 2), k, pl.ds(lax.rem(slot, 2), 1), :]
        turn_row = jnp.broadcast_to(row, (128, HL * P_SIZE)).T
        before = jnp.where(lane == 125 + k, turn_row, before)
    taps = [flat(conv_w[k : k + 1, :], HL * P_SIZE) for k in range(CONV)]
    mixing = flat(mix_g[...], HL * P_SIZE)
    second.first_near()
    square = jnp.zeros((1, STRETCH), f32)
    for h in range(HL):
        chan = slice(h * P_SIZE, (h + 1) * P_SIZE)
        gate = scale * paired[h * 128 : h * 128 + 64, :]
        signal = scale * paired[h * 128 + 64 : h * 128 + 128, :]
        padded = jnp.concatenate([before[chan], signal], axis=1)
        conv = taps[CONV - 1][chan] * signal
        for back in range(1, CONV):
            conv = conv + taps[CONV - 1 - back][chan] * pltpu.roll(padded, back, 1)[:, 128:]
        active = silu(conv)
        cum = cums[h : h + 1, :]
        step = steps[h : h + 1, :]
        mix = jnp.exp(jnp.minimum(cum - turned[:, h : h + 1], 0.0)) * pairs * turned[:, HL + h : HL + h + 1]
        within = jnp.dot(active.astype(bf16), mix.astype(bf16), preferred_element_type=f32)
        rows = lines[h * 32 : (h + 1) * 32, :]
        init = jnp.dot(even, rows[:, :NS], precision=highest, preferred_element_type=f32)
        init = init + jnp.dot(odd, rows[:, NS:], precision=highest, preferred_element_type=f32)
        carried = jnp.dot(init, c_proj, precision=highest, preferred_element_type=f32) * jnp.exp(cum)
        gated = (within + carried + skip[h] * active) * silu(gate)
        square = square + jnp.sum(gated * gated, axis=0, keepdims=True)
        gained[chan, :] = gated * mixing[chan]
        last = cum[:, STRETCH - 1 :]
        to_end = jnp.exp(last - cum) * step
        final_out[chan, :] = jnp.exp(last) * init + lax.dot_general(
            active * to_end, b_proj, NT, precision=highest, preferred_element_type=f32
        )
        if h == 1:
            second.second_near(0)
    squares[...] = square
    group = lax.div(me, 8)
    spot = lax.rem(me, 8)
    met = []
    for by in range(1, 8):
        copy = remote(
            squares, peers3.at[by - 1], u_send.at[by - 1], u_recv.at[by - 1],
            group * 8 + lax.rem(spot + by, 8),
        )
        copy.start()
        met.append(copy)
    second.first_far()
    total = square
    for by in range(1, 8):
        met[by - 1].wait_recv()
        total = total + peers3[by - 1, 0:1, :]
    scale = lax.rsqrt(total * (1.0 / (MH // G * P_SIZE)) + epsilon)
    scatter = Scatter(part, near1, full1, mid, near2, full2, x_send, x_recv)
    scatter.run(
        weight, (gained[...] * scale).astype(bf16),
        [lambda: second.second_near(1)],
        [lambda: second.second_near(2), lambda: blocks.relay(1), lambda: blocks.relay(3),
         lambda: blocks.spread(3, 1), lambda: second.second_near(3)],
    )
    gain = column(gain_sh, me * SHARD, SHARD)
    mine = pl.ds(pl.multiple_of(me * SHARD, 16), SHARD)
    sq = jnp.zeros((1, STRETCH), f32)
    for half in (0, 1):
        rows = pl.ds(half * HALF, HALF)
        value = hidden[rows, :].astype(f32) + scatter.result(half)
        next_out[rows, :] = value
        value = value.astype(bf16).astype(f32)
        sq = sq + jnp.sum(value * value, axis=0, keepdims=True)
        rounded[rows, :] = (value * gain[half * HALF : (half + 1) * HALF]).astype(bf16)
    sums2[...] = sq
    gather = Gather(rounded, wide2, g_send, g_recv)
    gather.start()
    sent = send_sums(sums2, peers2, r_send, r_recv)
    wide2[mine, :] = rounded[...]
    loads[3].wait()
    for k in range(SIDE):
        second.second_far(k)
    acc[...] = jnp.dot(watt[:, D:], emb[...], preferred_element_type=f32)

    def attend_rows(by):
        span = row_of(by)
        acc[...] += jnp.dot(watt[:, span], wide2[span, :], preferred_element_type=f32)

    def rest():
        for ch in range(CHUNKS):
            blocks.rest(ch)

    gather.run(attend_rows, rest)
    for ch in range(CHUNKS):
        blocks.far(ch)
    total = add_sums(sums2, peers2, sent) + embed_sq
    scale = lax.rsqrt(total * (0.5 / D) + epsilon)
    value = acc[...]
    proj_out[...] = (value * scale).astype(bf16)
    gather.finish()
    scatter.finish()
    loads[4].wait()
    blocks.finish()
    first.finish()
    second.finish()
    for copy in out + moved + met + sent:
        copy.wait_send()


def front_call(*args):
    anywhere = pl.BlockSpec(memory_space=pl.ANY)
    vmem = pl.BlockSpec(memory_space=pltpu.VMEM)
    smem = pl.BlockSpec(memory_space=pltpu.SMEM)
    dma = pltpu.SemaphoreType.DMA
    return pl.pallas_call(
        front_kernel,
        out_shape=(
            jax.ShapeDtypeStruct((SHARD, STRETCH), f32),
            jax.ShapeDtypeStruct((3 * HD, STRETCH), bf16),
            jax.ShapeDtypeStruct((HL * P_SIZE, NS), f32),
            jax.ShapeDtypeStruct((SEQ * BLOCKS, 2, HD, BLOCK), bf16),
        ),
        in_specs=[anywhere] * 6 + [smem] + [anywhere] * 2 + [vmem] + [smem] * 3 + [anywhere] * 5,
        out_specs=(vmem, vmem, vmem, anywhere),
        scratch_shapes=[
            pltpu.VMEM((SHARD, STRETCH), bf16),
            pltpu.VMEM((SHARD, STRETCH), bf16),
            pltpu.VMEM((D // 128, 128), f32),
            pltpu.VMEM((2 * D // 128, 128), f32),
            pltpu.VMEM((CONV, HL * P_SIZE), f32),
            pltpu.VMEM((1, HL * P_SIZE), f32),
            pltpu.VMEM((HL * P_SIZE, D), bf16),
            pltpu.VMEM((D, STRETCH), bf16),
            pltpu.VMEM((SHARD, STRETCH), bf16),
            pltpu.VMEM((SHARD, STRETCH), bf16),
            pltpu.VMEM((D, HL * 128), bf16),
            pltpu.VMEM((D, 2 * G * NS), bf16),
            pltpu.VMEM((HL * 128, STRETCH), f32),
            pltpu.VMEM((2 * G * NS, STRETCH), f32),
            pltpu.VMEM((2, STRETCH), f32),
            pltpu.VMEM((HEADS - 1, 2, STRETCH), f32),
            pltpu.VMEM((2 * SEQ, HL, P_SIZE * NS), f32),
            pltpu.VMEM((SEQ, CONV - 1, 2, HL * P_SIZE), f32),
            pltpu.VMEM((128, 128), f32),
            pltpu.VMEM((HL * P_SIZE, STRETCH), f32),
            pltpu.VMEM((3 * HD, 2 * D), bf16),
            pltpu.VMEM((D, STRETCH), bf16),
            pltpu.VMEM((D, STRETCH), bf16),
            pltpu.VMEM((3 * HD, STRETCH), f32),
            pltpu.VMEM((1, STRETCH), f32),
            pltpu.VMEM((7, 1, STRETCH), f32),
            pltpu.VMEM((1, STRETCH), f32),
            pltpu.VMEM((HEADS - 1, 1, STRETCH), f32),
            pltpu.VMEM((SHARD, STRETCH), bf16),
        ] + SCATTER_SCRATCH + GATHER_SEMS + GATHER_SEMS + GATHER_SEMS + [
            dma((HEADS - 1,)), dma((HEADS - 1,)),
            dma((SEQ - 1,)), dma((SEQ - 1,)),
            dma((SEQ - 1,)), dma((SEQ - 1,)),
            dma((7,)), dma((7,)),
            dma((HEADS - 1,)), dma((HEADS - 1,)),
            dma((28,)), dma((28,)),
            dma((5,)), dma((8,)),
            pltpu.VMEM((HL, STRETCH), f32),
            pltpu.VMEM((CONV - 1, 2, HL * P_SIZE), bf16),
            pltpu.VMEM((CONV - 1, 2, HL * P_SIZE), f32),
        ],
        compiler_params=pltpu.CompilerParams(
            collective_id=0, has_side_effects=True, vmem_limit_bytes=60 * 2**20
        ),
        name="front_rows",
    )(*args)


def merge_kernel(attended, weight, before, out,
                 part, near1, full1, mid, near2, full2, s_send, s_recv):
    barrier = greet_heads()
    pl.semaphore_wait(barrier, HEADS - 1)
    scatter = Scatter(part, near1, full1, mid, near2, full2, s_send, s_recv)
    scatter.run(weight, attended[...])
    for half in (0, 1):
        rows = pl.ds(half * HALF, HALF)
        out[rows, :] = before[rows, :] + scatter.result(half)
    scatter.finish()


def merge_call(attended, weight, before):
    vmem = pl.BlockSpec(memory_space=pltpu.VMEM)
    return pl.pallas_call(
        merge_kernel,
        out_shape=jax.ShapeDtypeStruct((SHARD, STRETCH), f32),
        in_specs=[vmem] * 3,
        out_specs=vmem,
        scratch_shapes=SCATTER_SCRATCH,
        compiler_params=pltpu.CompilerParams(
            collective_id=2, has_side_effects=True, vmem_limit_bytes=40 * 2**20
        ),
        name="merge_rows",
    )(attended, weight, before)


def turn(value):
    return jnp.concatenate([value, jnp.zeros((256 - HD, STRETCH), f32)], axis=0).T[:, :HD]


def attend_kernel(table, lengths, projected, pool, out, held, sems, acc, top, total):
    seq = lax.axis_index("seq")
    scale = HD ** -0.5 * 1.4426950408889634
    span = STEPB * BLOCK
    limit = lengths[seq]
    blocks = lax.div(limit + BLOCK - 1, BLOCK)
    steps = lax.div(blocks + STEPB - 1, STEPB)

    def fetch(step, slot):
        return [
            pltpu.make_async_copy(
                pool.at[table[seq, step * STEPB + i]],
                held.at[slot, :, :, pl.ds(i * BLOCK, BLOCK)],
                sems.at[slot, i],
            )
            for i in range(STEPB)
        ]

    for copy in fetch(0, 0):
        copy.start()
    q = turn(projected[:HD, :].astype(f32)).astype(bf16)
    scores = jnp.dot(q, projected[HD : 2 * HD, :], preferred_element_type=f32)
    row = lax.broadcasted_iota(jnp.int32, scores.shape, 0)
    col = lax.broadcasted_iota(jnp.int32, scores.shape, 1)
    scores = jnp.where(row >= col, scores, masked)
    high = jnp.max(scores, axis=1, keepdims=True)
    weights = jnp.exp2((scores - high) * scale)
    top[...] = high
    total[...] = jnp.sum(weights, axis=1, keepdims=True)
    acc[...] = lax.dot_general(
        weights.astype(bf16), projected[2 * HD :, :], NT, preferred_element_type=f32
    )

    def step_body(step, _):
        slot = lax.rem(step, 2)

        @pl.when(step + 1 < steps)
        def _():
            for copy in fetch(step + 1, 1 - slot):
                copy.start()

        for copy in fetch(step, slot):
            copy.wait()
        scores = jnp.dot(q, held[slot, 0], preferred_element_type=f32)

        def rest(scores):
            old = top[...]
            high = jnp.maximum(old, jnp.max(scores, axis=1, keepdims=True))
            weights = jnp.exp2((scores - high) * scale)
            factor = jnp.exp2((old - high) * scale)
            top[...] = high
            total[...] = total[...] * factor + jnp.sum(weights, axis=1, keepdims=True)
            acc[...] = acc[...] * factor + lax.dot_general(
                weights.astype(bf16), held[slot, 1], NT, preferred_element_type=f32
            )

        @pl.when((step + 1) * span <= limit)
        def _():
            rest(scores)

        @pl.when((step + 1) * span > limit)
        def _():
            where = step * span + lax.broadcasted_iota(jnp.int32, scores.shape, 1)
            rest(jnp.where(where < limit, scores, masked))

        return 0

    lax.fori_loop(0, steps, step_body, 0)
    value = acc[...] / total[...]
    value = jnp.concatenate([value, jnp.zeros((STRETCH, 256 - HD), f32)], axis=1).T
    out[...] = value[:HD].astype(bf16)


def attend_call(table, lengths, projected, pool):
    vmem = pl.BlockSpec(memory_space=pltpu.VMEM)
    smem = pl.BlockSpec(memory_space=pltpu.SMEM)
    return pl.pallas_call(
        attend_kernel,
        out_shape=jax.ShapeDtypeStruct((HD, STRETCH), bf16),
        in_specs=[smem, smem, vmem, pl.BlockSpec(memory_space=pl.ANY)],
        out_specs=vmem,
        scratch_shapes=[
            pltpu.VMEM((2, 2, HD, STEPB * BLOCK), bf16),
            pltpu.SemaphoreType.DMA((2, STEPB)),
            pltpu.VMEM((STRETCH, HD), f32),
            pltpu.VMEM((STRETCH, 1), f32),
            pltpu.VMEM((STRETCH, 1), f32),
        ],
        compiler_params=pltpu.CompilerParams(vmem_limit_bytes=48 * 2**20),
        name="attend_rows",
    )(table, lengths, projected, pool)


def body(hidden, embedding, input_gain, w_input, w_groups, w_step, step_bias, decay_rate, skip_gain,
         conv_weight, mix_gain, w_output, state_store, conv_store, state_slot, prefix_len, block_table,
         shared_gain, w_attend, cache_pool, w_merge):
    heads_local = w_step.shape[1]
    hidden_next, projected, final_state, pool = front_call(
        hidden.T, embedding.T, input_gain.reshape(D // 128, 128), shared_gain.reshape(2 * D // 128, 128),
        state_store, conv_store.transpose(1, 0, 2), state_slot, w_input, w_groups, w_step.T,
        step_bias, decay_rate, skip_gain, conv_weight, mix_gain[None, :], w_output, w_attend.T,
        cache_pool.transpose(0, 1, 3, 2),
    )
    attended = attend_call(block_table, prefix_len, projected, pool)
    layer_output = merge_call(attended, w_merge, hidden_next)
    return (layer_output.T, final_state.reshape(1, heads_local, P_SIZE * NS))


def solution(mesh):
    return jax.shard_map(
        body,
        mesh=mesh,
        in_specs=(
            P("seq", "head"),
            P("seq", "head"),
            P(),
            P(None, "head"),
            P(),
            P(None, "head"),
            P("head"),
            P("head"),
            P("head"),
            P(None, "head"),
            P("head"),
            P("head", None),
            P("seq", "head", None),
            P("seq", None, "head"),
            P(),
            P(),
            P(),
            P(),
            P(None, "head"),
            P("seq", None, None, "head"),
            P("head", None),
        ),
        out_specs=(P("seq", "head"), P("seq", "head", None)),
        check_vma=False,
    )
```

```python
import functools

import jax
import jax.numpy as jnp
from jax import lax
from jax.experimental import pallas as pl
from jax.experimental.pallas import tpu as pltpu
from jax.sharding import PartitionSpec as P

D = 3584
MH = 64
P_SIZE = 64
NS = 64
G = 2
CONV = 4
HD = 224
STRETCH = 512
BLOCK = 128
MAXB = 64
SEQ = 8
SIDE = 4
HEADS = SIDE * SIDE
SHARD = D // HEADS
HALF = SHARD // 2
LANES = STRETCH // 2
STEPB = 8

MESH = pl.DeviceIdType.MESH
epsilon = 1e-05
masked = -1e30
highest = lax.Precision.HIGHEST
f32 = jnp.float32
bf16 = jnp.bfloat16


def place():
    me = lax.axis_index("head")
    return lax.div(me, SIDE), lax.rem(me, SIDE)


def around(c, by):
    return lax.rem(c + by + SIDE, SIDE)


def coords(half):
    z, y = place()
    return (y, z) if half == 0 else (z, y)


def device(half, c1, c2):
    return c2 * SIDE + c1 if half == 0 else c1 * SIDE + c2


def piece(half, c1, c2):
    return pl.ds(pl.multiple_of(device(half, c1, c2) * SHARD + half * HALF, 16), HALF)


OFFSETS = (0, -1, 1, 2)
LEFT = pl.ds(0, LANES)
RIGHT = pl.ds(LANES, LANES)
FULL = pl.ds(0, STRETCH)


def remote(src, dst, send_sem, recv_sem, dev):
    return pltpu.make_async_remote_copy(
        src_ref=src, dst_ref=dst, send_sem=send_sem, recv_sem=recv_sem,
        device_id={"head": dev}, device_id_type=MESH,
    )


class Gather:
    def __init__(self, own, out, send_sems, recv_sems):
        self.own, self.out, self.ss, self.rs = own, out, send_sems, recv_sems
        self.sent = []

    def go(self, half, idx, src, c1, c2, lanes, to1, to2):
        dst = self.out.at[piece(half, c1, c2), lanes]
        copy = remote(src, dst, self.ss.at[half, idx], self.rs.at[half, idx], device(half, to1, to2))
        copy.start()
        self.sent.append(copy)

    def arrive(self, half, idx, c1, c2, lanes):
        where = self.out.at[piece(half, c1, c2), lanes]
        me1, me2 = coords(half)
        remote(where, where, self.ss.at[half, idx], self.rs.at[half, idx], device(half, around(me1, 1), me2)).wait_recv()

    def start(self):
        for axis in (1, 2):
            for half in (0, 1):
                c1, c2 = coords(half)
                src = self.own.at[pl.ds(half * HALF, HALF), FULL]
                if axis == 1:
                    self.go(half, 0, src, c1, c2, FULL, around(c1, 1), c2)
                    self.go(half, 1, src, c1, c2, FULL, around(c1, -1), c2)
                else:
                    self.go(half, 4, src, c1, c2, FULL, c1, around(c2, 1))
                    self.go(half, 5, src, c1, c2, FULL, c1, around(c2, -1))

    def second(self, half, k):
        c1, c2 = coords(half)
        o1 = around(c1, OFFSETS[k])
        src = self.out.at[piece(half, o1, c2), FULL]
        self.go(half, 4 + 4 * k, src, o1, c2, FULL, c1, around(c2, 1))
        self.go(half, 5 + 4 * k, src, o1, c2, FULL, c1, around(c2, -1))

    def first_near(self):
        for half in (0, 1):
            c1, c2 = coords(half)
            left = around(c1, -1)
            self.arrive(half, 0, left, c2, FULL)
            self.go(half, 2, self.out.at[piece(half, left, c2), LEFT], left, c2, LEFT, around(c1, 1), c2)
            self.second(half, 1)
        for half in (0, 1):
            c1, c2 = coords(half)
            right = around(c1, 1)
            self.arrive(half, 1, right, c2, FULL)
            self.go(half, 3, self.out.at[piece(half, right, c2), RIGHT], right, c2, RIGHT, around(c1, -1), c2)
            self.second(half, 2)

    def first_far(self):
        for half in (0, 1):
            c1, c2 = coords(half)
            far = around(c1, 2)
            self.arrive(half, 2, far, c2, LEFT)
            self.arrive(half, 3, far, c2, RIGHT)
            self.second(half, 3)

    def second_near(self, k, halves=(0, 1)):
        for half in halves:
            c1, c2 = coords(half)
            o1 = around(c1, OFFSETS[k])
            for way in (0, 1):
                nb = around(c2, -1 if way == 0 else 1)
                to = around(c2, 1 if way == 0 else -1)
                lanes = LEFT if way == 0 else RIGHT
                self.arrive(half, 4 + 4 * k + way, o1, nb, FULL)
                self.go(half, 6 + 4 * k + way, self.out.at[piece(half, o1, nb), lanes], o1, nb, lanes, c1, to)

    def second_far(self, k, halves=(0, 1)):
        for half in halves:
            c1, c2 = coords(half)
            o1 = around(c1, OFFSETS[k])
            far = around(c2, 2)
            self.arrive(half, 6 + 4 * k, o1, far, LEFT)
            self.arrive(half, 7 + 4 * k, o1, far, RIGHT)

    def run(self, use, between):
        self.first_near()
        self.second_near(0)
        self.first_far()
        self.second_near(1)
        self.second_far(0, (1,))
        use(0)
        self.second_near(2)
        self.second_near(3)
        between()
        self.second_far(1, (1,))
        use(-1)
        self.second_far(2, (1,))
        use(1)
        self.second_far(3, (1,))
        for k in range(SIDE):
            self.second_far(k, (0,))
        use(2)

    def finish(self):
        for copy in self.sent:
            copy.wait_send()


GATHER_SEMS = [pltpu.SemaphoreType.DMA((2, 20)), pltpu.SemaphoreType.DMA((2, 20))]

SCATTER_SCRATCH = [
    pltpu.VMEM((D, STRETCH), bf16),
    pltpu.VMEM((2, SIDE, 2, HALF, LANES), bf16),
    pltpu.VMEM((2, SIDE, 2, HALF, STRETCH), bf16),
    pltpu.VMEM((2, SIDE, HALF, STRETCH), bf16),
    pltpu.VMEM((2, 2, HALF, LANES), bf16),
    pltpu.VMEM((2, 2, HALF, STRETCH), bf16),
    pltpu.SemaphoreType.DMA((2, 20)),
    pltpu.SemaphoreType.DMA((2, 20)),
]


class Scatter:
    def __init__(self, part, near1, full1, mid, near2, full2, send_sems, recv_sems):
        self.part, self.near1, self.full1, self.mid = part, near1, full1, mid
        self.near2, self.full2, self.ss, self.rs = near2, full2, send_sems, recv_sems
        self.sent = []

    def go(self, half, idx, src, dst, to1, to2):
        copy = remote(src, dst, self.ss.at[half, idx], self.rs.at[half, idx], device(half, to1, to2))
        copy.start()
        self.sent.append(copy)

    def arrive(self, half, idx, where):
        me1, me2 = coords(half)
        remote(where, where, self.ss.at[half, idx], self.rs.at[half, idx], device(half, around(me1, 1), me2)).wait_recv()

    def one(self, k, halves):
        for half in halves:
            c1, c2 = coords(half)
            o1 = around(c1, OFFSETS[k])
            rows = piece(half, o1, around(c2, 2))
            self.go(half, 4 * k, self.part.at[rows, LEFT], self.near1.at[half, k, 0], c1, around(c2, 1))
            self.go(half, 4 * k + 1, self.part.at[rows, RIGHT], self.near1.at[half, k, 1], c1, around(c2, -1))

    def two(self, k):
        for half in (0, 1):
            c1, c2 = coords(half)
            o1 = around(c1, OFFSETS[k])
            for way in (0, 1):
                to = around(c2, 1 if way == 0 else -1)
                lanes = LEFT if way == 0 else RIGHT
                rows = piece(half, o1, to)
                self.arrive(half, 4 * k + way, self.near1.at[half, k, way])
                mine = self.part[rows, lanes].astype(f32)
                self.part[rows, lanes] = (mine + self.near1[half, k, way].astype(f32)).astype(bf16)
                self.go(half, 4 * k + 2 + way, self.part.at[rows, FULL], self.full1.at[half, k, way], c1, to)

    def three(self, k):
        for half in (0, 1):
            c1, c2 = coords(half)
            o1 = around(c1, OFFSETS[k])
            self.arrive(half, 4 * k + 2, self.full1.at[half, k, 0])
            self.arrive(half, 4 * k + 3, self.full1.at[half, k, 1])
            if k:
                self.mid[half, k] = self.total(half, k).astype(bf16)
                if k == 3:
                    self.go(half, 16, self.mid.at[half, 3, :, LEFT], self.near2.at[half, 0], around(c1, 1), c2)
                    self.go(half, 17, self.mid.at[half, 3, :, RIGHT], self.near2.at[half, 1], around(c1, -1), c2)

    def total(self, half, k):
        c1, c2 = coords(half)
        rows = piece(half, around(c1, OFFSETS[k]), c2)
        return (
            self.part[rows, :].astype(f32)
            + self.full1[half, k, 0].astype(f32)
            + self.full1[half, k, 1].astype(f32)
        )

    def four(self, k):
        way = 0 if k == 2 else 1
        lanes = LEFT if way == 0 else RIGHT
        for half in (0, 1):
            c1, c2 = coords(half)
            self.arrive(half, 16 + way, self.near2.at[half, way])
            mine = self.mid[half, k, :, lanes].astype(f32)
            self.mid[half, k, :, lanes] = (mine + self.near2[half, way].astype(f32)).astype(bf16)
            self.go(half, 18 + way, self.mid.at[half, k], self.full2.at[half, way], around(c1, OFFSETS[k]), c2)

    def run(self, weight, rows, early=(), late=()):
        products(weight, rows, self.part, 2)
        self.one(3, (0, 1))
        products(weight, rows, self.part, 1)
        self.one(2, (0, 1))
        products(weight, rows, self.part, -1)
        self.one(1, (0, 1))
        products(weight, rows, self.part, 0)
        self.one(0, (0, 1))
        for step in early:
            step()
        self.two(3)
        self.two(2)
        self.two(1)
        self.three(3)
        self.two(0)
        for step in late:
            step()
        self.three(2)
        self.four(2)
        self.three(1)
        self.four(1)
        self.three(0)

    def result(self, half):
        self.arrive(half, 18, self.full2.at[half, 0])
        self.arrive(half, 19, self.full2.at[half, 1])
        return (
            self.total(half, 0)
            + self.full2[half, 0].astype(f32)
            + self.full2[half, 1].astype(f32)
        )

    def finish(self):
        for copy in self.sent:
            copy.wait_send()


def greet_heads():
    barrier = pltpu.get_barrier_semaphore()
    me = lax.axis_index("head")
    for by in range(1, HEADS):
        pl.semaphore_signal(
            barrier, inc=1, device_id={"head": lax.rem(me + by, HEADS)}, device_id_type=MESH
        )
    return barrier


def flat(row, count):
    turned = jnp.broadcast_to(row, (128, count)).T
    return jnp.concatenate([turned] * (STRETCH // 128), axis=1)


def column(table, start, count):
    rows = table.shape[0]
    entry = start + lax.broadcasted_iota(jnp.int32, (count, rows), 0)
    pick = (lax.shift_right_logical(entry, 7) == lax.broadcasted_iota(jnp.int32, (count, rows), 1))
    lines = jnp.dot(pick.astype(f32), table[...], precision=highest, preferred_element_type=f32)
    entry = start + lax.broadcasted_iota(jnp.int32, (count, 128), 0)
    keep = jnp.bitwise_and(entry, 127) == lax.broadcasted_iota(jnp.int32, (count, 128), 1)
    return jnp.sum(jnp.where(keep, lines, 0.0), axis=1, keepdims=True)


def send_sums(mine, peers, send_sems, recv_sems):
    me = lax.axis_index("head")
    out = []
    for by in range(1, HEADS):
        copy = remote(
            mine, peers.at[by - 1], send_sems.at[by - 1], recv_sems.at[by - 1],
            lax.rem(me + by, HEADS),
        )
        copy.start()
        out.append(copy)
    return out


def add_sums(mine, peers, out):
    total = mine[...]
    for by in range(1, HEADS):
        out[by - 1].wait_recv()
        total = total + peers[by - 1]
    return total


def silu(value):
    return value / (1.0 + jnp.exp(-value))


TN = (((0,), (0,)), ((), ()))
NT = (((1,), (1,)), ((), ()))
HL = 4


ROW = SIDE * SHARD


def row_of(by):
    return pl.ds(pl.multiple_of(around(place()[0], by) * ROW, 128), ROW)


def products(weight, rows, part, by):
    span = row_of(by)
    part[span, :] = lax.dot_general(
        weight[:, span], rows, TN, preferred_element_type=f32
    ).astype(bf16)


CHUNKS = 4
BLOCKS = 20


class Pool:
    def __init__(self, own, out, send_sems, recv_sems):
        self.own, self.out, self.ss, self.rs = own, out, send_sems, recv_sems
        seq = lax.axis_index("seq")
        self.x, self.core = lax.div(seq, 2), lax.rem(seq, 2)
        self.sent = []

    def slab(self, by, core, ch):
        per = BLOCKS // CHUNKS
        return self.out.at[pl.ds((around(self.x, by) * 2 + core) * BLOCKS + ch * per, per)]

    def copy(self, idx, src, dst, by, core):
        return pltpu.make_async_remote_copy(
            src_ref=src, dst_ref=dst, send_sem=self.ss.at[idx], recv_sem=self.rs.at[idx],
            device_id={"seq": around(self.x, by) * 2 + core}, device_id_type=MESH,
        )

    def go(self, idx, src, dst, by, core):
        copy = self.copy(idx, src, dst, by, core)
        copy.start()
        self.sent.append(copy)

    def arrive(self, idx, dst):
        self.copy(idx, dst, dst, 1, self.core).wait_recv()

    def spread(self, right, left):
        per = BLOCKS // CHUNKS
        for base, ch, by in ((0, right, 1), (4, left, -1)):
            self.go(base + ch, self.own.at[pl.ds(ch * per, per)], self.slab(0, self.core, ch), by, self.core)

    def start(self):
        per = BLOCKS // CHUNKS
        self.spread(0, 2)
        for ch in range(CHUNKS):
            self.go(12 + ch, self.own.at[pl.ds(ch * per, per)], self.slab(0, self.core, ch), 0, 1 - self.core)

    def share(self, j, by, ch):
        where = self.slab(by, self.core, ch)
        self.go(12 + 4 * j + ch, where, where, 0, 1 - self.core)

    def relay(self, ch):
        left = self.slab(-1, self.core, ch)
        right = self.slab(1, self.core, ch)
        if ch < 2:
            self.arrive(ch, left)
            self.go(8 + ch, left, left, 1, self.core)
            self.share(1, -1, ch)
        else:
            self.arrive(4 + ch, right)
            self.go(8 + ch, right, right, -1, self.core)
            self.share(2, 1, ch)

    def rest(self, ch):
        if ch < 2:
            self.arrive(4 + ch, self.slab(1, self.core, ch))
            self.share(2, 1, ch)
        else:
            self.arrive(ch, self.slab(-1, self.core, ch))
            self.share(1, -1, ch)

    def far(self, ch):
        self.arrive(8 + ch, self.slab(2, self.core, ch))
        self.share(3, 2, ch)

    def finish(self):
        for j, by in enumerate((0, -1, 1, 2)):
            for ch in range(CHUNKS):
                self.arrive(12 + 4 * j + ch, self.slab(by, 1 - self.core, ch))
        for copy in self.sent:
            copy.wait_send()


def front_kernel(hidden_in, embed_in, gain_in_in, gain_sh_in, states, tails_in, slots, w_in, w_gr, w_st, bias, decay,
                 skip, conv_in, mix_in, w_out_in, w_att, pool_in,
                 next_out, proj_out, final_out, pool_out,
                 hidden, embed, gain_in, gain_sh, conv_w, mix_g, weight,
                 wide, own_h, own_e, win, wgr, paired, grouped, sums, peers, stores, tail_all, lines, gained, watt,
                 emb, wide2, acc, squares, peers3, sums2, peers2, rounded,
                 part, near1, full1, mid, near2, full2, x_send, x_recv,
                 h_send, h_recv, e_send, e_recv, g_send, g_recv, q_send, q_recv, s_send, s_recv, t_send, t_recv,
                 u_send, u_recv, r_send, r_recv, p_send, p_recv, local, here, raws, tails_raw, tails):
    seq = lax.axis_index("seq")
    me = lax.axis_index("head")
    small = [
        pltpu.make_async_copy(src, dst, here.at[i])
        for i, (src, dst) in enumerate((
            (hidden_in, hidden), (gain_in_in, gain_in), (embed_in, embed), (gain_sh_in, gain_sh),
            (conv_in, conv_w), (mix_in, mix_g), (w_out_in, weight), (tails_in, tails_raw),
        ))
    ]
    for copy in small:
        copy.start()
    loads = [
        pltpu.make_async_copy(w_in, win, local.at[0]),
        pltpu.make_async_copy(w_gr, wgr, local.at[1]),
        pltpu.make_async_copy(states, stores.at[pl.ds(seq * 2, 2)], local.at[2]),
        pltpu.make_async_copy(w_att, watt, local.at[3]),
        pltpu.make_async_copy(pool_in, pool_out.at[pl.ds(seq * BLOCKS, BLOCKS)], local.at[4]),
    ]
    for copy in loads:
        copy.start()
    barrier = greet_heads()
    for by in range(1, SEQ):
        pl.semaphore_signal(
            barrier, inc=1, device_id={"seq": lax.rem(seq + by, SEQ)}, device_id_type=MESH
        )
    mine = pl.ds(pl.multiple_of(me * SHARD, 16), SHARD)
    small[0].wait()
    small[1].wait()
    value = hidden[...].astype(f32)
    sq_h = jnp.sum(value * value, axis=0, keepdims=True)
    ready = (value * column(gain_in, me * SHARD, SHARD)).astype(bf16)
    own_h[...] = ready
    wide[mine, :] = ready
    pl.semaphore_wait(barrier, HEADS - 1 + SEQ - 1)
    first = Gather(own_h, wide, h_send, h_recv)
    second = Gather(own_e, emb, e_send, e_recv)
    blocks = Pool(pool_in, pool_out, p_send, p_recv)
    first.start()
    for copy in small[2:]:
        copy.wait()
    tails[...] = tails_raw[...].astype(f32)
    tail_all[seq] = tails[...]
    value = embed[...].astype(f32)
    sq_e = jnp.sum(value * value, axis=0, keepdims=True)
    ready = (value * column(gain_sh, D + me * SHARD, SHARD)).astype(bf16)
    own_e[...] = ready
    emb[mine, :] = ready
    sums[0:1, :] = sq_h
    sums[1:2, :] = sq_e
    out = send_sums(sums, peers, q_send, q_recv)
    x, core = lax.div(seq, 2), lax.rem(seq, 2)
    held = (
        (states, stores, lambda at: stores.at[pl.ds(at * 2, 2)], s_send, s_recv),
        (tails, tail_all, lambda at: tail_all.at[at], t_send, t_recv),
    )
    moved = []

    def send_state(idx, src, dst, ss, rs, to):
        copy = pltpu.make_async_remote_copy(
            src_ref=src, dst_ref=dst, send_sem=ss.at[idx], recv_sem=rs.at[idx],
            device_id={"seq": to}, device_id_type=MESH,
        )
        copy.start()
        moved.append(copy)

    for src, _, at, ss, rs in held:
        for by in range(1, SIDE):
            send_state(by - 1, src, at(seq), ss, rs, around(x, by) * 2 + core)
        send_state(3, src, at(seq), ss, rs, x * 2 + 1 - core)

    def pass_states():
        for _, _, at, ss, rs in held:
            for by in range(1, SIDE):
                where = at(around(x, -by) * 2 + core)
                pltpu.make_async_remote_copy(
                    src_ref=where, dst_ref=where, send_sem=ss.at[by - 1], recv_sem=rs.at[by - 1],
                    device_id={"seq": x * 2 + 1 - core}, device_id_type=MESH,
                ).wait_recv()
                send_state(3 + by, where, where, ss, rs, x * 2 + 1 - core)

    def wait_states():
        for _, _, at, ss, rs in held:
            for by in range(SIDE):
                where = at(around(x, -by) * 2 + 1 - core)
                pltpu.make_async_remote_copy(
                    src_ref=where, dst_ref=where, send_sem=ss.at[3 + by], recv_sem=rs.at[3 + by],
                    device_id={"seq": x * 2 + 1 - core}, device_id_type=MESH,
                ).wait_recv()

    blocks.start()
    paired[...] = jnp.zeros_like(paired)
    grouped[...] = jnp.zeros_like(grouped)
    raws[...] = jnp.zeros_like(raws)
    for copy in loads[:2]:
        copy.wait()

    def project(by):
        span = row_of(by)
        rows = wide[span, :]
        paired[...] += lax.dot_general(win[span, :], rows, TN, preferred_element_type=f32)
        grouped[...] += lax.dot_general(wgr[span, :], rows, TN, preferred_element_type=f32)
        raws[...] += jnp.dot(w_st[:, span], rows, preferred_element_type=f32)

    def between():
        second.start()
        pass_states()
        blocks.spread(1, 3)
        blocks.relay(0)
        blocks.relay(2)
        blocks.spread(2, 0)

    first.run(project, between)
    total = add_sums(sums, peers, out)
    embed_sq = total[1:2, :]
    scale = lax.rsqrt(total[0:1, :] * (1.0 / D) + epsilon)
    raw = raws[...] * scale
    head = lax.broadcasted_iota(jnp.int32, (HL, STRETCH), 0)

    def by_head(ref):
        line = jnp.zeros((HL, STRETCH), f32)
        for i in range(HL):
            line = jnp.where(head == i, ref[i], line)
        return line

    raw = raw + by_head(bias)
    steps = jnp.maximum(raw, 0.0) + jnp.log1p(jnp.exp(-jnp.abs(raw)))
    cums = -by_head(decay) * steps
    lane = lax.broadcasted_iota(jnp.int32, (HL, STRETCH), 1)
    by = 1
    while by < STRETCH:
        cums = cums + jnp.where(lane >= by, pltpu.roll(cums, by, 1), 0.0)
        by *= 2
    turned = jnp.concatenate([cums, steps, jnp.zeros((128 - 2 * HL, STRETCH), f32)], axis=0).T
    group = lax.div(me, 8)
    b_proj = scale * grouped[pl.ds(pl.multiple_of(group * NS, NS), NS), :]
    c_proj = scale * grouped[pl.ds(pl.multiple_of(G * NS + group * NS, NS), NS), :]
    pairs = lax.dot_general(b_proj.astype(bf16), c_proj.astype(bf16), TN, preferred_element_type=f32)
    src = lax.broadcasted_iota(jnp.int32, pairs.shape, 0)
    dst = lax.broadcasted_iota(jnp.int32, pairs.shape, 1)
    pairs = jnp.where(src <= dst, pairs, 0.0)

    loads[2].wait()
    wait_states()
    slot = slots[seq]
    for h in range(HL):
        for i in range(32):
            lines[pl.ds(h * 32 + i, 1), :] = stores[slot, h : h + 1, i * 128 : (i + 1) * 128]
    p_row = lax.broadcasted_iota(jnp.int32, (P_SIZE, 32), 0)
    p_col = lax.broadcasted_iota(jnp.int32, (P_SIZE, 32), 1)
    even = (p_row == 2 * p_col).astype(f32)
    odd = (p_row == 2 * p_col + 1).astype(f32)
    lane = lax.broadcasted_iota(jnp.int32, (HL * P_SIZE, 128), 1)
    before = jnp.zeros((HL * P_SIZE, 128), f32)
    for k in range(CONV - 1):
        row = tail_all[lax.div(slot, 2), k, pl.ds(lax.rem(slot, 2), 1), :]
        turn_row = jnp.broadcast_to(row, (128, HL * P_SIZE)).T
        before = jnp.where(lane == 125 + k, turn_row, before)
    taps = [flat(conv_w[k : k + 1, :], HL * P_SIZE) for k in range(CONV)]
    mixing = flat(mix_g[...], HL * P_SIZE)
    second.first_near()
    square = jnp.zeros((1, STRETCH), f32)
    for h in range(HL):
        chan = slice(h * P_SIZE, (h + 1) * P_SIZE)
        gate = scale * paired[h * 128 : h * 128 + 64, :]
        signal = scale * paired[h * 128 + 64 : h * 128 + 128, :]
        padded = jnp.concatenate([before[chan], signal], axis=1)
        conv = taps[CONV - 1][chan] * signal
        for back in range(1, CONV):
            conv = conv + taps[CONV - 1 - back][chan] * pltpu.roll(padded, back, 1)[:, 128:]
        active = silu(conv)
        cum = cums[h : h + 1, :]
        step = steps[h : h + 1, :]
        mix = jnp.exp(jnp.minimum(cum - turned[:, h : h + 1], 0.0)) * pairs * turned[:, HL + h : HL + h + 1]
        within = jnp.dot(active.astype(bf16), mix.astype(bf16), preferred_element_type=f32)
        rows = lines[h * 32 : (h + 1) * 32, :]
        init = jnp.dot(even, rows[:, :NS], precision=highest, preferred_element_type=f32)
        init = init + jnp.dot(odd, rows[:, NS:], precision=highest, preferred_element_type=f32)
        carried = jnp.dot(init, c_proj, precision=highest, preferred_element_type=f32) * jnp.exp(cum)
        gated = (within + carried + skip[h] * active) * silu(gate)
        square = square + jnp.sum(gated * gated, axis=0, keepdims=True)
        gained[chan, :] = gated * mixing[chan]
        last = cum[:, STRETCH - 1 :]
        to_end = jnp.exp(last - cum) * step
        final_out[chan, :] = jnp.exp(last) * init + lax.dot_general(
            active * to_end, b_proj, NT, precision=highest, preferred_element_type=f32
        )
        if h == 1:
            second.second_near(0)
    squares[...] = square
    group = lax.div(me, 8)
    spot = lax.rem(me, 8)
    met = []
    for by in range(1, 8):
        copy = remote(
            squares, peers3.at[by - 1], u_send.at[by - 1], u_recv.at[by - 1],
            group * 8 + lax.rem(spot + by, 8),
        )
        copy.start()
        met.append(copy)
    second.first_far()
    total = square
    for by in range(1, 8):
        met[by - 1].wait_recv()
        total = total + peers3[by - 1, 0:1, :]
    scale = lax.rsqrt(total * (1.0 / (MH // G * P_SIZE)) + epsilon)
    scatter = Scatter(part, near1, full1, mid, near2, full2, x_send, x_recv)
    scatter.run(
        weight, (gained[...] * scale).astype(bf16),
        [lambda: second.second_near(1)],
        [lambda: second.second_near(2), lambda: blocks.relay(1), lambda: blocks.relay(3),
         lambda: blocks.spread(3, 1), lambda: second.second_near(3)],
    )
    gain = column(gain_sh, me * SHARD, SHARD)
    mine = pl.ds(pl.multiple_of(me * SHARD, 16), SHARD)
    sq = jnp.zeros((1, STRETCH), f32)
    for half in (0, 1):
        rows = pl.ds(half * HALF, HALF)
        value = hidden[rows, :].astype(f32) + scatter.result(half)
        next_out[rows, :] = value
        value = value.astype(bf16).astype(f32)
        sq = sq + jnp.sum(value * value, axis=0, keepdims=True)
        rounded[rows, :] = (value * gain[half * HALF : (half + 1) * HALF]).astype(bf16)
    sums2[...] = sq
    gather = Gather(rounded, wide2, g_send, g_recv)
    gather.start()
    sent = send_sums(sums2, peers2, r_send, r_recv)
    wide2[mine, :] = rounded[...]
    loads[3].wait()
    for k in range(SIDE):
        second.second_far(k)
    acc[...] = jnp.dot(watt[:, D:], emb[...], preferred_element_type=f32)

    def attend_rows(by):
        span = row_of(by)
        acc[...] += jnp.dot(watt[:, span], wide2[span, :], preferred_element_type=f32)

    def rest():
        for ch in range(CHUNKS):
            blocks.rest(ch)

    gather.run(attend_rows, rest)
    for ch in range(CHUNKS):
        blocks.far(ch)
    total = add_sums(sums2, peers2, sent) + embed_sq
    scale = lax.rsqrt(total * (0.5 / D) + epsilon)
    value = acc[...]
    proj_out[...] = (value * scale).astype(bf16)
    gather.finish()
    scatter.finish()
    loads[4].wait()
    blocks.finish()
    first.finish()
    second.finish()
    for copy in out + moved + met + sent:
        copy.wait_send()


def front_call(*args):
    anywhere = pl.BlockSpec(memory_space=pl.ANY)
    vmem = pl.BlockSpec(memory_space=pltpu.VMEM)
    smem = pl.BlockSpec(memory_space=pltpu.SMEM)
    dma = pltpu.SemaphoreType.DMA
    return pl.pallas_call(
        front_kernel,
        out_shape=(
            jax.ShapeDtypeStruct((SHARD, STRETCH), f32),
            jax.ShapeDtypeStruct((3 * HD, STRETCH), bf16),
            jax.ShapeDtypeStruct((HL * P_SIZE, NS), f32),
            jax.ShapeDtypeStruct((SEQ * BLOCKS, 2, HD, BLOCK), bf16),
        ),
        in_specs=[anywhere] * 6 + [smem] + [anywhere] * 2 + [vmem] + [smem] * 3 + [anywhere] * 5,
        out_specs=(vmem, vmem, vmem, anywhere),
        scratch_shapes=[
            pltpu.VMEM((SHARD, STRETCH), bf16),
            pltpu.VMEM((SHARD, STRETCH), bf16),
            pltpu.VMEM((D // 128, 128), f32),
            pltpu.VMEM((2 * D // 128, 128), f32),
            pltpu.VMEM((CONV, HL * P_SIZE), f32),
            pltpu.VMEM((1, HL * P_SIZE), f32),
            pltpu.VMEM((HL * P_SIZE, D), bf16),
            pltpu.VMEM((D, STRETCH), bf16),
            pltpu.VMEM((SHARD, STRETCH), bf16),
            pltpu.VMEM((SHARD, STRETCH), bf16),
            pltpu.VMEM((D, HL * 128), bf16),
            pltpu.VMEM((D, 2 * G * NS), bf16),
            pltpu.VMEM((HL * 128, STRETCH), f32),
            pltpu.VMEM((2 * G * NS, STRETCH), f32),
            pltpu.VMEM((2, STRETCH), f32),
            pltpu.VMEM((HEADS - 1, 2, STRETCH), f32),
            pltpu.VMEM((2 * SEQ, HL, P_SIZE * NS), f32),
            pltpu.VMEM((SEQ, CONV - 1, 2, HL * P_SIZE), f32),
            pltpu.VMEM((128, 128), f32),
            pltpu.VMEM((HL * P_SIZE, STRETCH), f32),
            pltpu.VMEM((3 * HD, 2 * D), bf16),
            pltpu.VMEM((D, STRETCH), bf16),
            pltpu.VMEM((D, STRETCH), bf16),
            pltpu.VMEM((3 * HD, STRETCH), f32),
            pltpu.VMEM((1, STRETCH), f32),
            pltpu.VMEM((7, 1, STRETCH), f32),
            pltpu.VMEM((1, STRETCH), f32),
            pltpu.VMEM((HEADS - 1, 1, STRETCH), f32),
            pltpu.VMEM((SHARD, STRETCH), bf16),
        ] + SCATTER_SCRATCH + GATHER_SEMS + GATHER_SEMS + GATHER_SEMS + [
            dma((HEADS - 1,)), dma((HEADS - 1,)),
            dma((SEQ - 1,)), dma((SEQ - 1,)),
            dma((SEQ - 1,)), dma((SEQ - 1,)),
            dma((7,)), dma((7,)),
            dma((HEADS - 1,)), dma((HEADS - 1,)),
            dma((28,)), dma((28,)),
            dma((5,)), dma((8,)),
            pltpu.VMEM((HL, STRETCH), f32),
            pltpu.VMEM((CONV - 1, 2, HL * P_SIZE), bf16),
            pltpu.VMEM((CONV - 1, 2, HL * P_SIZE), f32),
        ],
        compiler_params=pltpu.CompilerParams(
            collective_id=0, has_side_effects=True, vmem_limit_bytes=60 * 2**20
        ),
        name="front_rows",
    )(*args)


def merge_kernel(attended, weight, before, out,
                 part, near1, full1, mid, near2, full2, s_send, s_recv):
    barrier = greet_heads()
    pl.semaphore_wait(barrier, HEADS - 1)
    scatter = Scatter(part, near1, full1, mid, near2, full2, s_send, s_recv)
    scatter.run(weight, attended[...])
    for half in (0, 1):
        rows = pl.ds(half * HALF, HALF)
        out[rows, :] = before[rows, :] + scatter.result(half)
    scatter.finish()


def merge_call(attended, weight, before):
    vmem = pl.BlockSpec(memory_space=pltpu.VMEM)
    return pl.pallas_call(
        merge_kernel,
        out_shape=jax.ShapeDtypeStruct((SHARD, STRETCH), f32),
        in_specs=[vmem] * 3,
        out_specs=vmem,
        scratch_shapes=SCATTER_SCRATCH,
        compiler_params=pltpu.CompilerParams(
            collective_id=2, has_side_effects=True, vmem_limit_bytes=40 * 2**20
        ),
        name="merge_rows",
    )(attended, weight, before)


def turn(value):
    return jnp.concatenate([value, jnp.zeros((256 - HD, STRETCH), f32)], axis=0).T[:, :HD]


def attend_kernel(table, lengths, projected, pool, out, held, sems, acc, top, total):
    seq = lax.axis_index("seq")
    scale = HD ** -0.5 * 1.4426950408889634
    span = STEPB * BLOCK
    limit = lengths[seq]
    blocks = lax.div(limit + BLOCK - 1, BLOCK)
    steps = lax.div(blocks + STEPB - 1, STEPB)

    def fetch(step, slot):
        return [
            pltpu.make_async_copy(
                pool.at[table[seq, step * STEPB + i]],
                held.at[slot, :, :, pl.ds(i * BLOCK, BLOCK)],
                sems.at[slot, i],
            )
            for i in range(STEPB)
        ]

    for copy in fetch(0, 0):
        copy.start()
    q = turn(projected[:HD, :].astype(f32)).astype(bf16)
    scores = jnp.dot(q, projected[HD : 2 * HD, :], preferred_element_type=f32)
    row = lax.broadcasted_iota(jnp.int32, scores.shape, 0)
    col = lax.broadcasted_iota(jnp.int32, scores.shape, 1)
    scores = jnp.where(row >= col, scores, masked)
    high = jnp.max(scores, axis=1, keepdims=True)
    weights = jnp.exp2((scores - high) * scale)
    top[...] = high
    total[...] = jnp.sum(weights, axis=1, keepdims=True)
    acc[...] = lax.dot_general(
        weights.astype(bf16), projected[2 * HD :, :], NT, preferred_element_type=f32
    )

    def step_body(step, _):
        slot = lax.rem(step, 2)

        @pl.when(step + 1 < steps)
        def _():
            for copy in fetch(step + 1, 1 - slot):
                copy.start()

        for copy in fetch(step, slot):
            copy.wait()
        scores = jnp.dot(q, held[slot, 0], preferred_element_type=f32)

        def rest(scores):
            old = top[...]
            high = jnp.maximum(old, jnp.max(scores, axis=1, keepdims=True))
            weights = jnp.exp2((scores - high) * scale)
            factor = jnp.exp2((old - high) * scale)
            top[...] = high
            total[...] = total[...] * factor + jnp.sum(weights, axis=1, keepdims=True)
            acc[...] = acc[...] * factor + lax.dot_general(
                weights.astype(bf16), held[slot, 1], NT, preferred_element_type=f32
            )

        @pl.when((step + 1) * span <= limit)
        def _():
            rest(scores)

        @pl.when((step + 1) * span > limit)
        def _():
            where = step * span + lax.broadcasted_iota(jnp.int32, scores.shape, 1)
            rest(jnp.where(where < limit, scores, masked))

        return 0

    lax.fori_loop(0, steps, step_body, 0)
    value = acc[...] / total[...]
    value = jnp.concatenate([value, jnp.zeros((STRETCH, 256 - HD), f32)], axis=1).T
    out[...] = value[:HD].astype(bf16)


def attend_call(table, lengths, projected, pool):
    vmem = pl.BlockSpec(memory_space=pltpu.VMEM)
    smem = pl.BlockSpec(memory_space=pltpu.SMEM)
    return pl.pallas_call(
        attend_kernel,
        out_shape=jax.ShapeDtypeStruct((HD, STRETCH), bf16),
        in_specs=[smem, smem, vmem, pl.BlockSpec(memory_space=pl.ANY)],
        out_specs=vmem,
        scratch_shapes=[
            pltpu.VMEM((2, 2, HD, STEPB * BLOCK), bf16),
            pltpu.SemaphoreType.DMA((2, STEPB)),
            pltpu.VMEM((STRETCH, HD), f32),
            pltpu.VMEM((STRETCH, 1), f32),
            pltpu.VMEM((STRETCH, 1), f32),
        ],
        compiler_params=pltpu.CompilerParams(vmem_limit_bytes=48 * 2**20),
        name="attend_rows",
    )(table, lengths, projected, pool)


def body(hidden, embedding, input_gain, w_input, w_groups, w_step, step_bias, decay_rate, skip_gain,
         conv_weight, mix_gain, w_output, state_store, conv_store, state_slot, prefix_len, block_table,
         shared_gain, w_attend, cache_pool, w_merge):
    heads_local = w_step.shape[1]
    hidden_next, projected, final_state, pool = front_call(
        hidden.T, embedding.T, input_gain.reshape(D // 128, 128), shared_gain.reshape(2 * D // 128, 128),
        state_store, conv_store.transpose(1, 0, 2), state_slot, w_input, w_groups, w_step.T,
        step_bias, decay_rate, skip_gain, conv_weight, mix_gain[None, :], w_output, w_attend.T,
        cache_pool.transpose(0, 1, 3, 2),
    )
    attended = attend_call(block_table, prefix_len, projected, pool)
    layer_output = merge_call(attended, w_merge, hidden_next)
    return (layer_output.T, final_state.reshape(1, heads_local, P_SIZE * NS))


def solution(mesh):
    return jax.shard_map(
        body,
        mesh=mesh,
        in_specs=(
            P("seq", "head"),
            P("seq", "head"),
            P(),
            P(None, "head"),
            P(),
            P(None, "head"),
            P("head"),
            P("head"),
            P("head"),
            P(None, "head"),
            P("head"),
            P("head", None),
            P("seq", "head", None),
            P("seq", None, "head"),
            P(),
            P(),
            P(),
            P(),
            P(None, "head"),
            P("seq", None, None, "head"),
            P("head", None),
        ),
        out_specs=(P("seq", "head"), P("seq", "head", None)),
        check_vma=False,
    )
```
